32 devices in a mesh: mesh: 8 (over y, x, core), four: 4 (over z).
Axes of the slice: x: 2, y: 2, z: 4, core: 2. Of those that a mesh axis runs over, the one named last changes fastest.
Arguments:
- adj_modes: float32 [3, 256, 64, 2048], P(None, 'four', None, 'mesh'), may hold values from -1 to 1
- base_flow: bfloat16 [12, 256, 64, 2048], P(None, None, 'four', 'mesh'), may hold values from -6 to 6
- geometry: float32 [4, 64, 2048], P(None, None, 'mesh'), may hold values from -1 to 1
- mass: float32 [64, 2048], P(None, 'mesh'), may hold values from 0.2 to 2
- connect: int32 [64, 2048], P(None, 'mesh'), may hold values from 0 to 12824, as said below
- edge_nodes: int32 [8, 2, 225], P('mesh'), may hold values from 0 to 12824, as said below
Outputs:
- adj_next: float32 [3, 256, 64, 2048], P(None, 'four', None, 'mesh')
The draws below stay inside these ranges and needn't reach their ends.
Inputs may be any that keep to these rules, and one draw needn't show every extreme that they name: `connect`: columns p * 256 to (p + 1) * 256 - 1 form partition p. Each partition numbers its 12825 nodes from 0; element nodes at the same place share an id, and every id is used. edge_nodes[p, 1] lists the ids of partition p's nodes that coincide with nodes of partition p + 1 (mod 8), in the same order in which edge_nodes[p + 1, 0] lists them; the two lists of a partition are disjoint, and no other node is shared between partitions.
All inputs are finite; a program needn't handle non-finite values.
Results may differ from the reference program's by a relative error of at most 0.0003.
Values sent between devices are 32-bit elements; how exact they have to be, the bound alone decides.
No kernel may reach another device: no remote copies, remote signals or barrier semaphores. Data moves between devices by JAX's collectives and lax.ppermute only.
A program may use at most 256 MiB of HBM per device.

```python
import math
import jax
import jax.numpy as jnp
from jax import lax

NP = 8
NODES = 64
PLANES = 256
ER = 32
EA = 8
E_DEV = 256
ELEMS = 2048
UNIQUE = 12825
N_MESH = 8


def mesh_tables(key):
    radial_n = (NP - 1) * ER + 1
    azimuth_n = (NP - 1) * EA + 1

    def one_part(part_index):
        part_key = jax.random.fold_in(key, part_index)
        node_perm = jax.random.permutation(jax.random.fold_in(part_key, 1), radial_n * azimuth_n).astype(jnp.int32)
        elem_perm = jax.random.permutation(jax.random.fold_in(part_key, 2), ER * EA).astype(jnp.int32)
        elem_radial = elem_perm // EA
        elem_azimuth = elem_perm % EA
        node_index = jnp.arange(NP * NP, dtype=jnp.int32)
        first_dir = node_index // NP
        second_dir = node_index % NP
        radial_pos = (NP - 1) * elem_radial[None, :] + first_dir[:, None]
        azimuth_pos = (NP - 1) * elem_azimuth[None, :] + second_dir[:, None]
        conn_part = node_perm[radial_pos * azimuth_n + azimuth_pos]
        radial_all = jnp.arange(radial_n, dtype=jnp.int32)
        lower = node_perm[radial_all * azimuth_n]
        upper = node_perm[radial_all * azimuth_n + azimuth_n - 1]
        return (conn_part, jnp.stack([lower, upper]))
    conn_all, edge_all = jax.vmap(one_part)(jnp.arange(N_MESH, dtype=jnp.int32))
    conn_all = conn_all.transpose(1, 0, 2).reshape(NP * NP, N_MESH * ER * EA)
    return (conn_all, edge_all)


def draw_connect(key, part):
    return mesh_tables(key)[0]


def draw_edge_nodes(key, part):
    return mesh_tables(key)[1]


def shard_levels(rng, shape, cuts, least, high):
    gain, own = 1.0, jax.random.fold_in(rng, 6)
    for dim, shards_of in cuts:
        draws = jnp.exp(jax.random.uniform(jax.random.fold_in(own, dim), (shards_of,), jnp.float32, least / len(cuts), high / len(cuts)))
        gain = gain * jnp.repeat(draws, shape[dim] // shards_of).reshape([-1 if axis == dim else 1 for axis in range(len(shape))])
    return gain


def gaussian(rng, extent, scale, bound, cuts=(), kind=jnp.bfloat16):
    array = scale * jax.random.normal(rng, extent, jnp.float32)
    if cuts:
        array = array * shard_levels(rng, extent, cuts, -0.22, 0.18)
    return jnp.clip(array, -bound, bound).astype(kind)


def setup_inputs(seed: int = 0) -> dict:
    streams_of = jax.random.split(jax.random.key(seed), 7)
    return {
        "adj_modes": gaussian(streams_of[0], (3, PLANES, NODES, ELEMS), (PLANES ** -0.5), 1.0, ((1, 4), (3, 8)), jnp.float32),
        "base_flow": gaussian(streams_of[1], (12, PLANES, NODES, ELEMS), 1.0, 6.0, ((2, 4), (3, 8))),
        "geometry": gaussian(streams_of[2], (4, NODES, ELEMS), 0.2, 1.0, ((2, 8),), jnp.float32),
        "mass": jnp.clip(jnp.exp(math.log(2.0) - 2.3025851 * jax.random.uniform(streams_of[3], (NODES, ELEMS), jnp.float32) ** shard_levels(streams_of[3], (NODES, ELEMS), ((1, 8),), -0.2, 0.2)), 0.2, 2.0),
        "connect": draw_connect(jax.random.fold_in(streams_of[6], 71), 0),
        "edge_nodes": draw_edge_nodes(jax.random.fold_in(streams_of[6], 71), 0),
    }


STEP_SIZE = 0.1
HIGH = lax.Precision.HIGHEST


def legendre_values(degree, point):
    before = 1.0
    current = point
    for order in range(1, degree):
        after = ((2 * order + 1) * point * current - order * before) / (order + 1)
        before = current
        current = after
    return current, before


def gll_derivative(points_n):
    degree = points_n - 1
    points = []
    for index in range(points_n):
        point = -math.cos(math.pi * index / degree)
        for sweep in range(100):
            top_val, below_val = legendre_values(degree, point)
            point = point - (point * top_val - below_val) / (points_n * top_val)
        points.append(point)
    values = [legendre_values(degree, point)[0] for point in points]
    deriv_rows = []
    for row_index in range(points_n):
        row_vals = []
        for col_index in range(points_n):
            if row_index != col_index:
                row_vals.append(values[row_index] / (values[col_index] * (points[row_index] - points[col_index])))
            else:
                row_vals.append(0.0)
        deriv_rows.append(row_vals)
    deriv_rows[0][0] = -degree * (degree + 1) / 4.0
    deriv_rows[degree][degree] = degree * (degree + 1) / 4.0
    deriv_table = jnp.asarray(deriv_rows, jnp.float32)
    identity = jnp.eye(points_n, dtype=jnp.float32)
    return jnp.kron(deriv_table, identity), jnp.kron(identity, deriv_table)


def plane_tables(planes):
    plane_idx = jnp.arange(planes, dtype=jnp.int32)
    wave_idx = plane_idx // 2
    phase = ((plane_idx[:, None] * wave_idx[None, :]) % planes).astype(jnp.float32) * (2.0 * math.pi / planes)
    is_sine = (plane_idx % 2) == 1
    synth = jnp.where(is_sine[None, :], jnp.sin(phase), jnp.cos(phase))
    alternate = (1 - 2 * (plane_idx % 2)).astype(jnp.float32)
    synth = synth.at[:, 1].set(alternate)
    scales = jnp.where(wave_idx == 0, 1.0 / planes, 2.0 / planes).astype(jnp.float32)
    analysis = synth.T * scales[:, None]
    return synth, analysis


def axial(coef, wave):
    pairs = coef.reshape(coef.shape[0], coef.shape[1] // 2, 2, coef.shape[2], coef.shape[3])
    factor = wave[None, :, None, None]
    return jnp.stack([factor * pairs[:, :, 1], -factor * pairs[:, :, 0]], axis=2).reshape(coef.shape)


def gradients(coef, geometry, deriv_r, deriv_s):
    along_r = jnp.einsum('mn,fpne->fpme', deriv_r, coef, precision=HIGH)
    along_s = jnp.einsum('mn,fpne->fpme', deriv_s, coef, precision=HIGH)
    grad_x = geometry[0] * along_r + geometry[1] * along_s
    grad_y = geometry[2] * along_r + geometry[3] * along_s
    return grad_x, grad_y


def advect(physical, base):
    pieces = []
    for component in range(3):
        total = jnp.zeros(physical.shape[1:], jnp.float32)
        for direction in range(3):
            total = total - base[direction].astype(jnp.float32) * physical[3 + 3 * direction + component] + physical[direction] * base[3 + 3 * component + direction].astype(jnp.float32)
        pieces.append(total)
    return jnp.stack(pieces)


def take_cols(table_rows, node_ids):
    return table_rows[:, node_ids]


def put_cols(table_rows, node_ids, new_vals):
    return table_rows.at[:, node_ids].set(new_vals)


def reference(adj_modes, base_flow, geometry, mass, connect, edge_nodes):
    deriv_r, deriv_s = gll_derivative(NP)
    synth, analysis = plane_tables(PLANES)
    wave = jnp.arange(PLANES // 2, dtype=jnp.int32).astype(jnp.float32) * (2.0 / PLANES)

    def one_part(part_index):
        start = (part_index * E_DEV).astype(jnp.int32)
        coef = lax.dynamic_slice_in_dim(adj_modes, start, E_DEV, 3)
        base = lax.dynamic_slice_in_dim(base_flow, start, E_DEV, 3)
        geo_part = lax.dynamic_slice_in_dim(geometry, start, E_DEV, 2)
        weights = lax.dynamic_slice_in_dim(mass, start, E_DEV, 1)
        node_ids = lax.dynamic_slice_in_dim(connect, start, E_DEV, 1).reshape(-1)
        grad_x, grad_y = gradients(coef, geo_part, deriv_r, deriv_s)
        grad_z = axial(coef, wave)
        fields = jnp.concatenate([coef, grad_x, grad_y, grad_z])
        physical = jnp.einsum('jm,fmne->fjne', synth, fields, precision=HIGH)
        forcing = advect(physical, base)
        forcing_modes = jnp.einsum('mj,fjne->fmne', analysis, forcing, precision=HIGH)
        weighted = weights * (coef + STEP_SIZE * forcing_modes)
        rows = jnp.concatenate([weighted.reshape(3 * PLANES, -1), weights.reshape(1, -1)])
        return jnp.zeros((rows.shape[0], UNIQUE), jnp.float32).at[:, node_ids].add(rows)

    summed = lax.map(one_part, jnp.arange(N_MESH, dtype=jnp.int32))
    lower = edge_nodes[:, 0]
    upper = edge_nodes[:, 1]
    low_vals = jax.vmap(take_cols)(summed, lower)
    high_vals = jax.vmap(take_cols)(summed, upper)
    new_low = low_vals + jnp.roll(high_vals, 1, axis=0)
    new_high = high_vals + jnp.roll(low_vals, -1, axis=0)
    summed = jax.vmap(put_cols)(summed, lower, new_low)
    summed = jax.vmap(put_cols)(summed, upper, new_high)
    conn_parts = connect.reshape(NODES, N_MESH, E_DEV).transpose(1, 0, 2).reshape(N_MESH, -1)
    spread = jax.vmap(take_cols)(summed, conn_parts)
    result = spread[:, :-1] / spread[:, -1:]
    result = result.reshape(N_MESH, 3, PLANES, NODES, E_DEV).transpose(1, 2, 3, 0, 4)
    return result.reshape(3, PLANES, NODES, ELEMS)
```

```python
import functools
import math

import jax
import jax.numpy as jnp
import numpy as np
from jax import lax
from jax.experimental import pallas as pl
from jax.experimental.pallas import tpu as pltpu
from jax.sharding import PartitionSpec as P

NP = 8
PLANES = 256
UNIQUE = 12825
STEP_SIZE = 0.1
HIGH = lax.Precision.HIGHEST
LANES = 128
BATCH = 8
VMEM_LIMIT = 56 * 1024 * 1024


def legendre_values(degree, point):
    before = 1.0
    current = point
    for order in range(1, degree):
        after = ((2 * order + 1) * point * current - order * before) / (order + 1)
        before = current
        current = after
    return (current, before)


def gll_derivative(points_n):
    degree = points_n - 1
    points = []
    for index in range(points_n):
        point = -math.cos(math.pi * index / degree)
        for sweep in range(100):
            top_val, below_val = legendre_values(degree, point)
            point = point - (point * top_val - below_val) / (points_n * top_val)
        points.append(point)
    values = [legendre_values(degree, point)[0] for point in points]
    deriv_rows = []
    for row_index in range(points_n):
        row_vals = []
        for col_index in range(points_n):
            if row_index != col_index:
                row_vals.append(
                    values[row_index]
                    / (values[col_index] * (points[row_index] - points[col_index]))
                )
            else:
                row_vals.append(0.0)
        deriv_rows.append(row_vals)
    deriv_rows[0][0] = -degree * (degree + 1) / 4.0
    deriv_rows[degree][degree] = degree * (degree + 1) / 4.0
    return deriv_rows


def plane_tables(planes):
    plane = np.arange(planes)
    wave = plane // 2
    phase = ((plane[:, None] * wave[None, :]) % planes) * (2.0 * math.pi / planes)
    synth = np.where((plane % 2 == 1)[None, :], np.sin(phase), np.cos(phase))
    synth[:, 1] = 1 - 2 * (plane % 2)
    scales = np.where(wave == 0, 1.0 / planes, 2.0 / planes)
    analysis = synth.T * scales[:, None]
    number = wave * (2.0 / planes)
    along = np.zeros_like(synth)
    along[:, 1::2] = number[1::2] * synth[:, 0::2]
    along[:, 0::2] = -number[0::2] * synth[:, 1::2]
    along[:, :2] = 0.0
    return tuple(jnp.asarray(t, jnp.float32) for t in (synth, along, analysis))


def params(**kw):
    return pltpu.CompilerParams(vmem_limit_bytes=VMEM_LIMIT, **kw)


def derivative(x, groups):
    a_n, c_n, l_n, m_n, e_n = x.shape
    deriv = gll_derivative(NP)
    rows = 8

    def kernel(x_ref, o_ref):
        for line in groups:
            vals = [x_ref[a, 0, l] for a, l in line]
            for i, (a, l) in enumerate(line):
                total = deriv[i][0] * vals[0]
                for k in range(1, NP):
                    if deriv[i][k] != 0.0:
                        total = total + deriv[i][k] * vals[k]
                o_ref[a, 0, l] = total

    spec = pl.BlockSpec((a_n, 1, l_n, rows, e_n), lambda c, m: (0, c, 0, m, 0))
    return pl.pallas_call(
        kernel,
        grid=(c_n, m_n // rows),
        in_specs=[spec],
        out_specs=spec,
        out_shape=jax.ShapeDtypeStruct(x.shape, jnp.float32),
        compiler_params=params(),
        cost_estimate=pl.CostEstimate(flops=16 * x.size, bytes_accessed=8 * x.size, transcendentals=0),
        name="line_derivative",
    )(x)


def base_products(synth, along, u, us, base, geo):
    s_n, c_n, l_n, m_n, e_n = u.shape
    p_n = base.shape[2]

    def kernel(synth_ref, along_ref, u_ref, us_ref, b_ref, g_ref, vr_ref, part_ref):
        l = pl.program_id(0)
        s_mat = synth_ref[...]
        z_mat = along_ref[...]
        field = lambda i: b_ref[i, 0].astype(jnp.float32)
        dot = functools.partial(jnp.dot, precision=HIGH, preferred_element_type=jnp.float32)
        g = [g_ref[i, pl.ds(l, 1), :] for i in range(4)]
        ux, uy = field(0), field(1)
        vr_ref[0] = ux * g[0] + uy * g[2]
        vs = ux * g[1] + uy * g[3]
        uz = field(2)
        phys = []
        for c in range(3):
            coef = u_ref[:, c, 0].reshape(s_n * m_n, e_n)
            phys.append(dot(s_mat, coef))
            dz = dot(z_mat, coef)
            ds = dot(s_mat, us_ref[:, c, 0].reshape(s_n * m_n, e_n))
            part_ref[c, 0] = -(vs * ds) - uz * dz
        for c in range(3):
            part_ref[c, 0] += phys[0] * field(3 + 3 * c) + phys[1] * field(4 + 3 * c) + phys[2] * field(5 + 3 * c)

    whole = pl.BlockSpec((p_n, p_n), lambda l: (0, 0))
    coefs = pl.BlockSpec((s_n, 3, 1, m_n, e_n), lambda l: (0, 0, l, 0, 0))
    return pl.pallas_call(
        kernel,
        grid=(l_n,),
        in_specs=[
            whole,
            whole,
            coefs,
            coefs,
            pl.BlockSpec((12, 1, p_n, e_n), lambda l: (0, l, 0, 0)),
            pl.BlockSpec((4, l_n, e_n), lambda l: (0, 0, 0)),
        ],
        out_specs=[
            pl.BlockSpec((1, p_n, e_n), lambda l: (l, 0, 0)),
            pl.BlockSpec((3, 1, p_n, e_n), lambda l: (0, l, 0, 0)),
        ],
        out_shape=[
            jax.ShapeDtypeStruct((l_n, p_n, e_n), jnp.float32),
            jax.ShapeDtypeStruct((3, l_n, p_n, e_n), jnp.float32),
        ],
        compiler_params=params(),
        cost_estimate=pl.CostEstimate(
            flops=9 * 2 * 6 * l_n * p_n * p_n * e_n, bytes_accessed=l_n * p_n * e_n * 64, transcendentals=0
        ),
        name="base_products",
    )(synth, along, u, us, base, geo)


def forcing_modes(synth, analysis, ur, vr, part, mass, first):
    s_n, c_n, l_n, m_n, e_n = ur.shape
    p_n = vr.shape[1]

    def kernel(synth_ref, analysis_ref, ur_ref, vr_ref, part_ref, mass_ref, o_ref):
        l = pl.program_id(1)
        dot = functools.partial(jnp.dot, precision=HIGH, preferred_element_type=jnp.float32)
        dr = dot(synth_ref[...], ur_ref[:, 0, 0].reshape(s_n * m_n, e_n))
        forcing = part_ref[0, 0] - vr_ref[0] * dr
        modes = dot(analysis_ref[...], forcing) * (STEP_SIZE * mass_ref[pl.ds(l, 1), :])
        o_ref[:, 0, 0] = modes.reshape(s_n, m_n, e_n)

    whole = pl.BlockSpec((p_n, p_n), lambda c, l: (0, 0))
    coefs = pl.BlockSpec((s_n, 1, 1, m_n, e_n), lambda c, l: (0, c, l, 0, 0))
    return pl.pallas_call(
        kernel,
        grid=(c_n, l_n),
        in_specs=[
            whole,
            whole,
            coefs,
            pl.BlockSpec((1, p_n, e_n), lambda c, l: (l, 0, 0)),
            pl.BlockSpec((1, 1, p_n, e_n), lambda c, l: (first + c, l, 0, 0)),
            pl.BlockSpec((l_n, e_n), lambda c, l: (0, 0)),
        ],
        out_specs=coefs,
        out_shape=jax.ShapeDtypeStruct(ur.shape, jnp.float32),
        compiler_params=params(),
        cost_estimate=pl.CostEstimate(
            flops=2 * 2 * 6 * c_n * l_n * p_n * p_n * e_n,
            bytes_accessed=c_n * l_n * p_n * e_n * 16,
            transcendentals=0,
        ),
        name="forcing_modes",
    )(synth, analysis, ur, vr, part, mass)


def local_sums(modes, u, mass, pairs, edge_reps, first):
    s_n, c_n, l_n, m_n, e_n = modes.shape
    nodes_n = s_n * l_n
    rows_n = nodes_n * e_n
    step = min(8, l_n)
    per = l_n // step
    close_k, close_r, close_n, far_k, far_r, far_n = pairs
    edges_n = edge_reps.shape[1]
    feats = c_n * m_n

    def kernel(ck, cr, cn, fk, fr, fn, er, f_ref, u_ref, mass_ref, o_ref, e_ref):
        b = pl.program_id(0)

        def fill(t, _):
            node = b * step + t
            weight = mass_ref[pl.ds(node, 1), :]
            rows = [f_ref[0, c, t] + weight * u_ref[0, c, t] for c in range(c_n)]
            if feats < LANES:
                rows.append(jnp.zeros((LANES - feats, e_n), jnp.float32))
            table = jnp.concatenate(rows, axis=0)
            o_ref[pl.ds(pl.multiple_of(node * e_n, e_n), e_n), :] = table.T
            return 0

        lax.fori_loop(0, step, fill, 0)

        @pl.when(b == pl.num_programs(0) - 1)
        def _():
            o_ref[pl.ds(rows_n, 8), :] = jnp.zeros((8, LANES), jnp.float32)

            def close(i, _):
                heads = [cr[i * BATCH + t] for t in range(BATCH)]
                others = [ck[i * BATCH + t] for t in range(BATCH)]
                sums = [o_ref[pl.ds(r, 1), :] + o_ref[pl.ds(k, 1), :] for r, k in zip(heads, others)]
                for r, total in zip(heads, sums):
                    o_ref[pl.ds(r, 1), :] = total
                return 0

            lax.fori_loop(0, pl.cdiv(cn[0], BATCH), close, 0)

            def far(i, _):
                r = fr[i]
                o_ref[pl.ds(r, 1), :] = o_ref[pl.ds(r, 1), :] + o_ref[pl.ds(fk[i], 1), :]
                return 0

            lax.fori_loop(0, fn[0], far, 0)

            def edge(i, _):
                for side in range(2):
                    for t in range(BATCH):
                        e_ref[side, pl.ds(i * BATCH + t, 1), :] = o_ref[pl.ds(er[side, i * BATCH + t], 1), :]
                return 0

            lax.fori_loop(0, edges_n // BATCH, edge, 0)

    smem = pl.BlockSpec(memory_space=pltpu.SMEM)
    where = lambda b: (b // per, 0, b % per, 0, 0)
    where_u = lambda b: (b // per, first // c_n, b % per, 0, 0)
    return pl.pallas_call(
        kernel,
        grid=(nodes_n // step,),
        in_specs=[smem] * 7
        + [
            pl.BlockSpec((1, c_n, step, m_n, e_n), where),
            pl.BlockSpec((1, c_n, step, m_n, e_n), where_u),
            pl.BlockSpec((nodes_n, e_n), lambda b: (0, 0)),
        ],
        out_specs=[
            pl.BlockSpec((rows_n + 8, LANES), lambda b: (0, 0)),
            pl.BlockSpec((2, edges_n, LANES), lambda b: (0, 0, 0)),
        ],
        out_shape=[
            jax.ShapeDtypeStruct((rows_n + 8, LANES), jnp.float32),
            jax.ShapeDtypeStruct((2, edges_n, LANES), jnp.float32),
        ],
        compiler_params=params(),
        cost_estimate=pl.CostEstimate(
            flops=rows_n * LANES * 400, bytes_accessed=rows_n * LANES * 12, transcendentals=0
        ),
        name="local_sums",
    )(close_k, close_r, close_n, far_k, far_r, far_n, edge_reps, modes, u, mass)


def spread(table, came, edge_reps, back_k, back_r, inverse, held, shape, first, c_n):
    _, m_n, nodes_n, e_n = shape
    rows_n = nodes_n * e_n
    step = 8
    edges_n = edge_reps.shape[1]
    pairs_n = back_k.shape[0]

    def kernel(er, bk, br, t_ref, came_ref, inv_ref, *rest):
        o_ref, work = rest[-2], t_ref
        b = pl.program_id(0)

        @pl.when(b == 0)
        def _():
            def edge(i, _):
                for side in range(2):
                    spots = [er[side, i * BATCH + t] for t in range(BATCH)]
                    sums = [
                        work[pl.ds(r, 1), :] + came_ref[side, pl.ds(i * BATCH + t, 1), :]
                        for t, r in enumerate(spots)
                    ]
                    for r, total in zip(spots, sums):
                        work[pl.ds(r, 1), :] = total
                return 0

            lax.fori_loop(0, edges_n // BATCH, edge, 0)

            def back(i, _):
                got = [work[pl.ds(br[i * BATCH + t], 1), :] for t in range(BATCH)]
                for t, row in enumerate(got):
                    work[pl.ds(bk[i * BATCH + t], 1), :] = row
                return 0

            lax.fori_loop(0, pairs_n // BATCH, back, 0)

        stage = rest[-1]

        def node(t, _):
            n = b * step + t
            rows = work[pl.ds(pl.multiple_of(n * e_n, e_n), e_n), :].T
            scaled = rows * inv_ref[pl.ds(n, 1), :]
            for c in range(c_n):
                stage[c, t] = scaled[c * m_n : (c + 1) * m_n]
            return 0

        lax.fori_loop(0, step, node, 0)
        for c in range(c_n):
            o_ref[c] = jnp.swapaxes(stage[c], 0, 1)

    smem = pl.BlockSpec(memory_space=pltpu.SMEM)
    in_specs = [smem] * 3 + [
        pl.BlockSpec((rows_n + 8, LANES), lambda b: (0, 0)),
        pl.BlockSpec((2, edges_n, LANES), lambda b: (0, 0, 0)),
        pl.BlockSpec((nodes_n, e_n), lambda b: (0, 0)),
    ]
    args = [edge_reps, back_k, back_r, table, came, inverse]
    aliases = {}
    if held is not None:
        in_specs.append(pl.BlockSpec(memory_space=pl.ANY))
        args.append(held)
        aliases = {len(args) - 1: 0}
    return pl.pallas_call(
        kernel,
        grid=(nodes_n // step,),
        in_specs=in_specs,
        out_specs=pl.BlockSpec((c_n, m_n, step, e_n), lambda b: (first // c_n, 0, b, 0)),
        out_shape=jax.ShapeDtypeStruct(shape, jnp.float32),
        scratch_shapes=[pltpu.VMEM((c_n, step, m_n, e_n), jnp.float32)],
        input_output_aliases=aliases,
        compiler_params=params(),
        cost_estimate=pl.CostEstimate(
            flops=rows_n * LANES * 400, bytes_accessed=rows_n * LANES * 12, transcendentals=0
        ),
        name="spread",
    )(*args)


def fill_up(values, multiple, filler):
    short = -values.shape[-1] % multiple
    pad = [(0, 0)] * (values.ndim - 1) + [(0, short)]
    return jnp.pad(values, pad, constant_values=filler)


def pair_lists(ids, edges):
    rows_n = ids.shape[0]
    place = jnp.arange(rows_n, dtype=jnp.int32)
    ids_sorted, member = lax.sort((ids, place), num_keys=1)
    head = jnp.concatenate([jnp.ones((1,), bool), ids_sorted[1:] != ids_sorted[:-1]])
    code = lax.cummax(jnp.where(head, place * rows_n + member, 0))
    rep = code % rows_n
    rank = place - code // rows_n
    group = jnp.where(rank == 0, 2, jnp.where(rank == 1, 0, 1)).astype(jnp.int32)
    _, member_l, rep_l = lax.sort((group, member, rep), num_keys=1)
    pairs_n = rows_n - UNIQUE
    member_l = member_l[:pairs_n]
    rep_l = rep_l[:pairs_n]
    close_n = jnp.sum(group == 0, dtype=jnp.int32)
    far_n = pairs_n - close_n
    spot = jnp.arange(pairs_n, dtype=jnp.int32)
    close_k = fill_up(jnp.where(spot < close_n, member_l, rows_n), BATCH, rows_n)
    close_r = fill_up(jnp.where(spot < close_n, rep_l, rows_n), BATCH, rows_n)
    far_k = jnp.roll(member_l, -close_n)
    far_r = jnp.roll(rep_l, -close_n)
    back_k = fill_up(member_l, BATCH, rows_n)
    back_r = fill_up(rep_l, BATCH, rows_n)
    flat = edges.reshape(-1)
    start = jnp.sum(ids_sorted[None, :] < flat[:, None], axis=1, dtype=jnp.int32)
    edge_reps = fill_up(member[start].reshape(edges.shape), BATCH, rows_n)
    pairs = (close_k, close_r, close_n.reshape(1), far_k, far_r, far_n.reshape(1))
    return pairs, (back_k, back_r), edge_reps


def swap_edges(sums):
    count = lax.axis_size("mesh")
    up = [(i, (i + 1) % count) for i in range(count)]
    down = [(j, i) for i, j in up]
    return jnp.stack([lax.ppermute(sums[1], "mesh", up), lax.ppermute(sums[0], "mesh", down)])


def inverse_mass(mass, ids, edges):
    summed = jnp.zeros((UNIQUE,), jnp.float32).at[ids].add(mass.reshape(-1))
    came = swap_edges(summed[edges])
    summed = summed.at[edges.reshape(-1)].add(came.reshape(-1))
    return (1.0 / summed[ids]).reshape(mass.shape)


def exchange(x):
    return lax.all_to_all(x, "four", split_axis=0, concat_axis=0, tiled=True)


def body(adj_modes, base_flow, geometry, mass, connect, edge_nodes):
    comps, m_n, nodes_n, e_n = adj_modes.shape
    parts = lax.axis_size("four")
    l_n = nodes_n // parts
    mine = lax.axis_index("four") * l_n
    synth, along, analysis = plane_tables(PLANES)
    ids = connect.reshape(-1)
    edges = edge_nodes[0]

    u = adj_modes.reshape(comps, m_n, parts, l_n, e_n).transpose(2, 0, 3, 1, 4)
    u_here = exchange(u)
    spot = lambda n: (n // l_n, n % l_n)
    ur = derivative(u, [[spot(NP * i + j) for i in range(NP)] for j in range(NP)])
    if l_n % NP == 0:
        lines = [[(a, l + j) for j in range(NP)] for a in range(parts) for l in range(0, l_n, NP)]
        us_here = derivative(u_here, lines)
    else:
        us_here = exchange(derivative(u, [[spot(NP * i + j) for j in range(NP)] for i in range(NP)]))
    ur_here_a = exchange(ur[:, :2])
    ur_here_b = exchange(ur[:, 2:])

    base = base_flow.transpose(0, 2, 1, 3)
    geo = lax.dynamic_slice_in_dim(geometry, mine, l_n, 1)
    mass_here = lax.dynamic_slice_in_dim(mass, mine, l_n, 0)
    pairs, backs, edge_reps = pair_lists(ids, edges)
    inverse = inverse_mass(mass, ids, edges)

    vr, part = base_products(synth, along, u_here, us_here, base, geo)
    modes_a = exchange(forcing_modes(synth, analysis, ur_here_a, vr, part, mass_here, 0))
    modes_b = exchange(forcing_modes(synth, analysis, ur_here_b, vr, part, mass_here, 2))

    table_a, rims_a = local_sums(modes_a, u, mass, pairs, edge_reps, 0)
    out = spread(table_a, swap_edges(rims_a), edge_reps, *backs, inverse, None, adj_modes.shape, 0, 2)
    table_b, rims_b = local_sums(modes_b, u, mass, pairs, edge_reps, 2)
    return spread(table_b, swap_edges(rims_b), edge_reps, *backs, inverse, out, adj_modes.shape, 2, 1)


def solution(mesh):
    return jax.shard_map(
        body,
        mesh=mesh,
        in_specs=(
            P(None, "four", None, "mesh"),
            P(None, None, "four", "mesh"),
            P(None, None, "mesh"),
            P(None, "mesh"),
            P(None, "mesh"),
            P("mesh", None, None),
        ),
        out_specs=P(None, "four", None, "mesh"),
        check_vma=False,
    )
```

```python
import functools
import math

import jax
import jax.numpy as jnp
import numpy as np
from jax import lax
from jax.experimental import pallas as pl
from jax.experimental.pallas import tpu as pltpu
from jax.sharding import PartitionSpec as P

NP = 8
PLANES = 256
UNIQUE = 12825
STEP_SIZE = 0.1
HIGH = lax.Precision.HIGHEST
LANES = 128
BATCH = 8
VMEM_LIMIT = 56 * 1024 * 1024


def legendre_values(degree, point):
    before = 1.0
    current = point
    for order in range(1, degree):
        after = ((2 * order + 1) * point * current - order * before) / (order + 1)
        before = current
        current = after
    return (current, before)


def gll_derivative(points_n):
    degree = points_n - 1
    points = []
    for index in range(points_n):
        point = -math.cos(math.pi * index / degree)
        for sweep in range(100):
            top_val, below_val = legendre_values(degree, point)
            point = point - (point * top_val - below_val) / (points_n * top_val)
        points.append(point)
    values = [legendre_values(degree, point)[0] for point in points]
    deriv_rows = []
    for row_index in range(points_n):
        row_vals = []
        for col_index in range(points_n):
            if row_index != col_index:
                row_vals.append(
                    values[row_index]
                    / (values[col_index] * (points[row_index] - points[col_index]))
                )
            else:
                row_vals.append(0.0)
        deriv_rows.append(row_vals)
    deriv_rows[0][0] = -degree * (degree + 1) / 4.0
    deriv_rows[degree][degree] = degree * (degree + 1) / 4.0
    return deriv_rows


def plane_tables(planes):
    plane = np.arange(planes)
    wave = plane // 2
    phase = ((plane[:, None] * wave[None, :]) % planes) * (2.0 * math.pi / planes)
    synth = np.where((plane % 2 == 1)[None, :], np.sin(phase), np.cos(phase))
    synth[:, 1] = 1 - 2 * (plane % 2)
    scales = np.where(wave == 0, 1.0 / planes, 2.0 / planes)
    analysis = synth.T * scales[:, None]
    number = wave * (2.0 / planes)
    along = np.zeros_like(synth)
    along[:, 1::2] = number[1::2] * synth[:, 0::2]
    along[:, 0::2] = -number[0::2] * synth[:, 1::2]
    along[:, :2] = 0.0
    return tuple(jnp.asarray(t, jnp.float32) for t in (synth, along, analysis))


def params(**kw):
    return pltpu.CompilerParams(vmem_limit_bytes=VMEM_LIMIT, **kw)


def node_major(x, parts):
    c_n, m_n, n_n, e_n = x.shape
    l_n = n_n // parts
    rows = 16
    wide = min(LANES, e_n)

    def kernel(x_ref, o_ref):
        for n in range(n_n):
            o_ref[n // l_n, 0, n % l_n] = x_ref[0, pl.ds(n, rows, stride=n_n), :]

    return pl.pallas_call(
        kernel,
        grid=(c_n, m_n // rows, e_n // wide),
        in_specs=[pl.BlockSpec((1, rows * n_n, wide), lambda c, m, e: (c, m, e))],
        out_specs=pl.BlockSpec((parts, 1, l_n, rows, wide), lambda c, m, e: (0, c, 0, m, e)),
        out_shape=jax.ShapeDtypeStruct((parts, c_n, l_n, m_n, e_n), jnp.float32),
        compiler_params=params(),
        cost_estimate=pl.CostEstimate(flops=x.size, bytes_accessed=8 * x.size, transcendentals=0),
        name="node_major",
    )(x.reshape(c_n, m_n * n_n, e_n))


def derivative(x, groups, first=0, c_n=3):
    a_n, _, l_n, m_n, e_n = x.shape
    deriv = gll_derivative(NP)
    rows = 8

    def kernel(x_ref, o_ref):
        for line in groups:
            vals = [x_ref[a, 0, l] for a, l in line]
            for i, (a, l) in enumerate(line):
                total = deriv[i][0] * vals[0]
                for k in range(1, NP):
                    if deriv[i][k] != 0.0:
                        total = total + deriv[i][k] * vals[k]
                o_ref[a, 0, l] = total

    block = (a_n, 1, l_n, rows, e_n)
    size = a_n * c_n * l_n * m_n * e_n
    return pl.pallas_call(
        kernel,
        grid=(c_n, m_n // rows),
        in_specs=[pl.BlockSpec(block, lambda c, m: (0, first + c, 0, m, 0))],
        out_specs=pl.BlockSpec(block, lambda c, m: (0, c, 0, m, 0)),
        out_shape=jax.ShapeDtypeStruct((a_n, c_n, l_n, m_n, e_n), jnp.float32),
        compiler_params=params(),
        cost_estimate=pl.CostEstimate(flops=16 * size, bytes_accessed=8 * size, transcendentals=0),
        name="line_derivative",
    )(x)


def base_products(synth, along, u, us, base, geo):
    s_n, c_n, l_n, m_n, e_n = u.shape
    p_n = base.shape[2]

    def kernel(synth_ref, along_ref, u_ref, us_ref, b_ref, g_ref, vr_ref, part_ref):
        l = pl.program_id(0)
        s_mat = synth_ref[...]
        z_mat = along_ref[...]
        field = lambda i: b_ref[i, 0].astype(jnp.float32)
        dot = functools.partial(jnp.dot, precision=HIGH, preferred_element_type=jnp.float32)
        g = [g_ref[i, pl.ds(l, 1), :] for i in range(4)]
        ux, uy = field(0), field(1)
        vr_ref[0] = ux * g[0] + uy * g[2]
        vs = ux * g[1] + uy * g[3]
        uz = field(2)
        phys = []
        for c in range(3):
            coef = u_ref[:, c, 0].reshape(s_n * m_n, e_n)
            phys.append(dot(s_mat, coef))
            dz = dot(z_mat, coef)
            ds = dot(s_mat, us_ref[:, c, 0].reshape(s_n * m_n, e_n))
            part_ref[c, 0] = -(vs * ds) - uz * dz
        for c in range(3):
            part_ref[c, 0] += phys[0] * field(3 + 3 * c) + phys[1] * field(4 + 3 * c) + phys[2] * field(5 + 3 * c)

    whole = pl.BlockSpec((p_n, p_n), lambda l: (0, 0))
    coefs = pl.BlockSpec((s_n, 3, 1, m_n, e_n), lambda l: (0, 0, l, 0, 0))
    return pl.pallas_call(
        kernel,
        grid=(l_n,),
        in_specs=[
            whole,
            whole,
            coefs,
            coefs,
            pl.BlockSpec((12, 1, p_n, e_n), lambda l: (0, l, 0, 0)),
            pl.BlockSpec((4, l_n, e_n), lambda l: (0, 0, 0)),
        ],
        out_specs=[
            pl.BlockSpec((1, p_n, e_n), lambda l: (l, 0, 0)),
            pl.BlockSpec((3, 1, p_n, e_n), lambda l: (0, l, 0, 0)),
        ],
        out_shape=[
            jax.ShapeDtypeStruct((l_n, p_n, e_n), jnp.float32),
            jax.ShapeDtypeStruct((3, l_n, p_n, e_n), jnp.float32),
        ],
        compiler_params=params(),
        cost_estimate=pl.CostEstimate(
            flops=9 * 2 * 6 * l_n * p_n * p_n * e_n, bytes_accessed=l_n * p_n * e_n * 64, transcendentals=0
        ),
        name="base_products",
    )(synth, along, u, us, base, geo)


def forcing_modes(synth, analysis, ur, vr, part, mass, first):
    s_n, c_n, l_n, m_n, e_n = ur.shape
    p_n = vr.shape[1]

    def kernel(synth_ref, analysis_ref, ur_ref, vr_ref, part_ref, mass_ref, o_ref):
        l = pl.program_id(1)
        dot = functools.partial(jnp.dot, precision=HIGH, preferred_element_type=jnp.float32)
        dr = dot(synth_ref[...], ur_ref[:, 0, 0].reshape(s_n * m_n, e_n))
        forcing = part_ref[0, 0] - vr_ref[0] * dr
        modes = dot(analysis_ref[...], forcing) * (STEP_SIZE * mass_ref[pl.ds(l, 1), :])
        o_ref[:, 0, 0] = modes.reshape(s_n, m_n, e_n)

    whole = pl.BlockSpec((p_n, p_n), lambda c, l: (0, 0))
    coefs = pl.BlockSpec((s_n, 1, 1, m_n, e_n), lambda c, l: (0, c, l, 0, 0))
    return pl.pallas_call(
        kernel,
        grid=(c_n, l_n),
        in_specs=[
            whole,
            whole,
            coefs,
            pl.BlockSpec((1, p_n, e_n), lambda c, l: (l, 0, 0)),
            pl.BlockSpec((1, 1, p_n, e_n), lambda c, l: (first + c, l, 0, 0)),
            pl.BlockSpec((l_n, e_n), lambda c, l: (0, 0)),
        ],
        out_specs=coefs,
        out_shape=jax.ShapeDtypeStruct(ur.shape, jnp.float32),
        compiler_params=params(),
        cost_estimate=pl.CostEstimate(
            flops=2 * 2 * 6 * c_n * l_n * p_n * p_n * e_n,
            bytes_accessed=c_n * l_n * p_n * e_n * 16,
            transcendentals=0,
        ),
        name="forcing_modes",
    )(synth, analysis, ur, vr, part, mass)


def local_sums(modes, u, mass, pairs, edge_reps, first):
    s_n, c_n, l_n, m_n, e_n = modes.shape
    nodes_n = s_n * l_n
    rows_n = nodes_n * e_n
    step = min(8, l_n)
    per = l_n // step
    close_k, close_r, close_n, far_k, far_r, far_n = pairs
    edges_n = edge_reps.shape[1]
    feats = c_n * m_n

    def kernel(ck, cr, cn, fk, fr, fn, er, f_ref, u_ref, mass_ref, o_ref, e_ref):
        b = pl.program_id(0)

        def fill(t, _):
            node = b * step + t
            weight = mass_ref[pl.ds(node, 1), :]
            rows = [f_ref[0, c, t] + weight * u_ref[0, c, t] for c in range(c_n)]
            if feats < LANES:
                rows.append(jnp.zeros((LANES - feats, e_n), jnp.float32))
            table = jnp.concatenate(rows, axis=0)
            o_ref[pl.ds(pl.multiple_of(node * e_n, e_n), e_n), :] = table.T
            return 0

        lax.fori_loop(0, step, fill, 0)

        @pl.when(b == pl.num_programs(0) - 1)
        def _():
            o_ref[pl.ds(rows_n, 8), :] = jnp.zeros((8, LANES), jnp.float32)

            def close(i, _):
                heads = [cr[i * BATCH + t] for t in range(BATCH)]
                others = [ck[i * BATCH + t] for t in range(BATCH)]
                sums = [o_ref[pl.ds(r, 1), :] + o_ref[pl.ds(k, 1), :] for r, k in zip(heads, others)]
                for r, total in zip(heads, sums):
                    o_ref[pl.ds(r, 1), :] = total
                return 0

            lax.fori_loop(0, pl.cdiv(cn[0], BATCH), close, 0)

            def far(i, _):
                r = fr[i]
                o_ref[pl.ds(r, 1), :] = o_ref[pl.ds(r, 1), :] + o_ref[pl.ds(fk[i], 1), :]
                return 0

            lax.fori_loop(0, fn[0], far, 0)

            def edge(i, _):
                for side in range(2):
                    for t in range(BATCH):
                        e_ref[side, pl.ds(i * BATCH + t, 1), :] = o_ref[pl.ds(er[side, i * BATCH + t], 1), :]
                return 0

            lax.fori_loop(0, edges_n // BATCH, edge, 0)

    smem = pl.BlockSpec(memory_space=pltpu.SMEM)
    where = lambda b: (b // per, 0, b % per, 0, 0)
    where_u = lambda b: (b // per, first // c_n, b % per, 0, 0)
    return pl.pallas_call(
        kernel,
        grid=(nodes_n // step,),
        in_specs=[smem] * 7
        + [
            pl.BlockSpec((1, c_n, step, m_n, e_n), where),
            pl.BlockSpec((1, c_n, step, m_n, e_n), where_u),
            pl.BlockSpec((nodes_n, e_n), lambda b: (0, 0)),
        ],
        out_specs=[
            pl.BlockSpec((rows_n + 8, LANES), lambda b: (0, 0)),
            pl.BlockSpec((2, edges_n, LANES), lambda b: (0, 0, 0)),
        ],
        out_shape=[
            jax.ShapeDtypeStruct((rows_n + 8, LANES), jnp.float32),
            jax.ShapeDtypeStruct((2, edges_n, LANES), jnp.float32),
        ],
        compiler_params=params(),
        cost_estimate=pl.CostEstimate(
            flops=rows_n * LANES * 400, bytes_accessed=rows_n * LANES * 12, transcendentals=0
        ),
        name="local_sums",
    )(close_k, close_r, close_n, far_k, far_r, far_n, edge_reps, modes, u, mass)


def spread(table, came, edge_reps, back_k, back_r, inverse, held, shape, first, c_n):
    _, m_n, nodes_n, e_n = shape
    rows_n = nodes_n * e_n
    step = 8
    edges_n = edge_reps.shape[1]
    pairs_n = back_k.shape[0]

    def kernel(er, bk, br, t_ref, came_ref, inv_ref, *rest):
        o_ref, work = rest[-2], t_ref
        b = pl.program_id(0)

        @pl.when(b == 0)
        def _():
            def edge(i, _):
                for side in range(2):
                    spots = [er[side, i * BATCH + t] for t in range(BATCH)]
                    sums = [
                        work[pl.ds(r, 1), :] + came_ref[side, pl.ds(i * BATCH + t, 1), :]
                        for t, r in enumerate(spots)
                    ]
                    for r, total in zip(spots, sums):
                        work[pl.ds(r, 1), :] = total
                return 0

            lax.fori_loop(0, edges_n // BATCH, edge, 0)

            def back(i, _):
                got = [work[pl.ds(br[i * BATCH + t], 1), :] for t in range(BATCH)]
                for t, row in enumerate(got):
                    work[pl.ds(bk[i * BATCH + t], 1), :] = row
                return 0

            lax.fori_loop(0, pairs_n // BATCH, back, 0)

        stage = rest[-1]

        def node(t, _):
            n = b * step + t
            rows = work[pl.ds(pl.multiple_of(n * e_n, e_n), e_n), :].T
            scaled = rows * inv_ref[pl.ds(n, 1), :]
            for c in range(c_n):
                stage[c, t] = scaled[c * m_n : (c + 1) * m_n]
            return 0

        lax.fori_loop(0, step, node, 0)
        for c in range(c_n):
            o_ref[c] = jnp.swapaxes(stage[c], 0, 1)

    smem = pl.BlockSpec(memory_space=pltpu.SMEM)
    in_specs = [smem] * 3 + [
        pl.BlockSpec((rows_n + 8, LANES), lambda b: (0, 0)),
        pl.BlockSpec((2, edges_n, LANES), lambda b: (0, 0, 0)),
        pl.BlockSpec((nodes_n, e_n), lambda b: (0, 0)),
    ]
    args = [edge_reps, back_k, back_r, table, came, inverse]
    aliases = {}
    if held is not None:
        in_specs.append(pl.BlockSpec(memory_space=pl.ANY))
        args.append(held)
        aliases = {len(args) - 1: 0}
    return pl.pallas_call(
        kernel,
        grid=(nodes_n // step,),
        in_specs=in_specs,
        out_specs=pl.BlockSpec((c_n, m_n, step, e_n), lambda b: (first // c_n, 0, b, 0)),
        out_shape=jax.ShapeDtypeStruct(shape, jnp.float32),
        scratch_shapes=[pltpu.VMEM((c_n, step, m_n, e_n), jnp.float32)],
        input_output_aliases=aliases,
        compiler_params=params(),
        cost_estimate=pl.CostEstimate(
            flops=rows_n * LANES * 400, bytes_accessed=rows_n * LANES * 12, transcendentals=0
        ),
        name="spread",
    )(*args)


def fill_up(values, multiple, filler):
    short = -values.shape[-1] % multiple
    pad = [(0, 0)] * (values.ndim - 1) + [(0, short)]
    return jnp.pad(values, pad, constant_values=filler)


def pair_lists(ids, edges):
    rows_n = ids.shape[0]
    place = jnp.arange(rows_n, dtype=jnp.int32)
    ids_sorted, member = lax.sort((ids, place), num_keys=1)
    head = jnp.concatenate([jnp.ones((1,), bool), ids_sorted[1:] != ids_sorted[:-1]])
    code = lax.cummax(jnp.where(head, place * rows_n + member, 0))
    rep = code % rows_n
    rank = place - code // rows_n
    group = jnp.where(rank == 0, 2, jnp.where(rank == 1, 0, 1)).astype(jnp.int32)
    _, member_l, rep_l = lax.sort((group, member, rep), num_keys=1)
    pairs_n = rows_n - UNIQUE
    member_l = member_l[:pairs_n]
    rep_l = rep_l[:pairs_n]
    close_n = jnp.sum(group == 0, dtype=jnp.int32)
    far_n = pairs_n - close_n
    spot = jnp.arange(pairs_n, dtype=jnp.int32)
    close_k = fill_up(jnp.where(spot < close_n, member_l, rows_n), BATCH, rows_n)
    close_r = fill_up(jnp.where(spot < close_n, rep_l, rows_n), BATCH, rows_n)
    far_k = jnp.roll(member_l, -close_n)
    far_r = jnp.roll(rep_l, -close_n)
    back_k = fill_up(member_l, BATCH, rows_n)
    back_r = fill_up(rep_l, BATCH, rows_n)
    flat = edges.reshape(-1)
    start = jnp.sum(ids_sorted[None, :] < flat[:, None], axis=1, dtype=jnp.int32)
    edge_reps = fill_up(member[start].reshape(edges.shape), BATCH, rows_n)
    pairs = (close_k, close_r, close_n.reshape(1), far_k, far_r, far_n.reshape(1))
    return pairs, (back_k, back_r), edge_reps


def swap_edges(sums):
    count = lax.axis_size("mesh")
    up = [(i, (i + 1) % count) for i in range(count)]
    down = [(j, i) for i, j in up]
    return jnp.stack([lax.ppermute(sums[1], "mesh", up), lax.ppermute(sums[0], "mesh", down)])


def inverse_mass(mass, ids, edges):
    summed = jnp.zeros((UNIQUE,), jnp.float32).at[ids].add(mass.reshape(-1))
    came = swap_edges(summed[edges])
    summed = summed.at[edges.reshape(-1)].add(came.reshape(-1))
    return (1.0 / summed[ids]).reshape(mass.shape)


def exchange(x):
    return lax.all_to_all(x, "four", split_axis=0, concat_axis=0, tiled=True)


def body(adj_modes, base_flow, geometry, mass, connect, edge_nodes):
    comps, m_n, nodes_n, e_n = adj_modes.shape
    parts = lax.axis_size("four")
    l_n = nodes_n // parts
    mine = lax.axis_index("four") * l_n
    synth, along, analysis = plane_tables(PLANES)
    together = lax.optimization_barrier
    u = node_major(adj_modes, parts)
    u, connect, edge_nodes, mass, base_flow = together((u, connect, edge_nodes, mass, base_flow))
    u_here = exchange(u)

    ids = connect.reshape(-1)
    edges = edge_nodes[0]
    spot = lambda n: (n // l_n, n % l_n)
    along_r = [[spot(NP * i + j) for i in range(NP)] for j in range(NP)]
    ur_a, ur_b = derivative(u, along_r, 0, 2), derivative(u, along_r, 2, 1)
    pairs, backs, edge_reps = pair_lists(ids, edges)
    inverse = inverse_mass(mass, ids, edges)
    base = base_flow.transpose(0, 2, 1, 3)
    ur_a, ur_b, u_here, pairs, backs, edge_reps, inverse, base = together(
        (ur_a, ur_b, u_here, pairs, backs, edge_reps, inverse, base)
    )

    ur_here_a = exchange(ur_a)
    if l_n % NP == 0:
        lines = [[(a, l + j) for j in range(NP)] for a in range(parts) for l in range(0, l_n, NP)]
        us_here = derivative(u_here, lines)
    else:
        us_here = exchange(derivative(u, [[spot(NP * i + j) for j in range(NP)] for i in range(NP)]))
    geo = lax.dynamic_slice_in_dim(geometry, mine, l_n, 1)
    mass_here = lax.dynamic_slice_in_dim(mass, mine, l_n, 0)
    vr, part = base_products(synth, along, u_here, us_here, base, geo)
    ur_b, ur_here_a, vr, part = together((ur_b, ur_here_a, vr, part))

    ur_here_b = exchange(ur_b)
    f_a = forcing_modes(synth, analysis, ur_here_a, vr, part, mass_here, 0)
    f_a, ur_here_b = together((f_a, ur_here_b))

    modes_a = exchange(f_a)
    f_b = forcing_modes(synth, analysis, ur_here_b, vr, part, mass_here, 2)
    f_b, modes_a = together((f_b, modes_a))

    modes_b = exchange(f_b)
    table_a, rims_a = local_sums(modes_a, u, mass, pairs, edge_reps, 0)
    out = spread(table_a, swap_edges(rims_a), edge_reps, *backs, inverse, None, adj_modes.shape, 0, 2)
    modes_b, out = together((modes_b, out))

    table_b, rims_b = local_sums(modes_b, u, mass, pairs, edge_reps, 2)
    return spread(table_b, swap_edges(rims_b), edge_reps, *backs, inverse, out, adj_modes.shape, 2, 1)


def solution(mesh):
    return jax.shard_map(
        body,
        mesh=mesh,
        in_specs=(
            P(None, "four", None, "mesh"),
            P(None, None, "four", "mesh"),
            P(None, None, "mesh"),
            P(None, "mesh"),
            P(None, "mesh"),
            P("mesh", None, None),
        ),
        out_specs=P(None, "four", None, "mesh"),
        check_vma=False,
    )
```

```python
import functools
import math

import jax
import jax.numpy as jnp
import numpy as np
from jax import lax
from jax.experimental import pallas as pl
from jax.experimental.pallas import tpu as pltpu
from jax.sharding import PartitionSpec as P

NP = 8
PLANES = 256
UNIQUE = 12825
STEP_SIZE = 0.1
HIGH = lax.Precision.HIGHEST
LANES = 128
BATCH = 8
VMEM_LIMIT = 56 * 1024 * 1024


def legendre_values(degree, point):
    before = 1.0
    current = point
    for order in range(1, degree):
        after = ((2 * order + 1) * point * current - order * before) / (order + 1)
        before = current
        current = after
    return (current, before)


def gll_derivative(points_n):
    degree = points_n - 1
    points = []
    for index in range(points_n):
        point = -math.cos(math.pi * index / degree)
        for sweep in range(100):
            top_val, below_val = legendre_values(degree, point)
            point = point - (point * top_val - below_val) / (points_n * top_val)
        points.append(point)
    values = [legendre_values(degree, point)[0] for point in points]
    deriv_rows = []
    for row_index in range(points_n):
        row_vals = []
        for col_index in range(points_n):
            if row_index != col_index:
                row_vals.append(
                    values[row_index]
                    / (values[col_index] * (points[row_index] - points[col_index]))
                )
            else:
                row_vals.append(0.0)
        deriv_rows.append(row_vals)
    deriv_rows[0][0] = -degree * (degree + 1) / 4.0
    deriv_rows[degree][degree] = degree * (degree + 1) / 4.0
    return deriv_rows


def plane_tables(planes):
    plane = np.arange(planes)
    wave = plane // 2
    phase = ((plane[:, None] * wave[None, :]) % planes) * (2.0 * math.pi / planes)
    synth = np.where((plane % 2 == 1)[None, :], np.sin(phase), np.cos(phase))
    synth[:, 1] = 1 - 2 * (plane % 2)
    scales = np.where(wave == 0, 1.0 / planes, 2.0 / planes)
    analysis = synth.T * scales[:, None]
    number = wave * (2.0 / planes)
    along = np.zeros_like(synth)
    along[:, 1::2] = number[1::2] * synth[:, 0::2]
    along[:, 0::2] = -number[0::2] * synth[:, 1::2]
    along[:, :2] = 0.0
    return tuple(jnp.asarray(t, jnp.float32) for t in (synth, along, analysis))


def params(**kw):
    return pltpu.CompilerParams(vmem_limit_bytes=VMEM_LIMIT, **kw)


def node_major(x, parts):
    c_n, m_n, n_n, e_n = x.shape
    l_n = n_n // parts
    rows = 16
    wide = min(LANES, e_n)

    def kernel(x_ref, o_ref):
        for n in range(n_n):
            o_ref[n // l_n, 0, n % l_n] = x_ref[0, pl.ds(n, rows, stride=n_n), :]

    return pl.pallas_call(
        kernel,
        grid=(c_n, m_n // rows, e_n // wide),
        in_specs=[pl.BlockSpec((1, rows * n_n, wide), lambda c, m, e: (c, m, e))],
        out_specs=pl.BlockSpec((parts, 1, l_n, rows, wide), lambda c, m, e: (0, c, 0, m, e)),
        out_shape=jax.ShapeDtypeStruct((parts, c_n, l_n, m_n, e_n), jnp.float32),
        compiler_params=params(),
        cost_estimate=pl.CostEstimate(flops=x.size, bytes_accessed=8 * x.size, transcendentals=0),
        name="node_major",
    )(x.reshape(c_n, m_n * n_n, e_n))


def derivative(x, groups, first=0, c_n=3):
    a_n, _, l_n, m_n, e_n = x.shape
    deriv = gll_derivative(NP)
    rows = 8

    def kernel(x_ref, o_ref):
        for line in groups:
            vals = [x_ref[a, 0, l] for a, l in line]
            for i, (a, l) in enumerate(line):
                total = deriv[i][0] * vals[0]
                for k in range(1, NP):
                    if deriv[i][k] != 0.0:
                        total = total + deriv[i][k] * vals[k]
                o_ref[a, 0, l] = total

    block = (a_n, 1, l_n, rows, e_n)
    size = a_n * c_n * l_n * m_n * e_n
    return pl.pallas_call(
        kernel,
        grid=(c_n, m_n // rows),
        in_specs=[pl.BlockSpec(block, lambda c, m: (0, first + c, 0, m, 0))],
        out_specs=pl.BlockSpec(block, lambda c, m: (0, c, 0, m, 0)),
        out_shape=jax.ShapeDtypeStruct((a_n, c_n, l_n, m_n, e_n), jnp.float32),
        compiler_params=params(),
        cost_estimate=pl.CostEstimate(flops=16 * size, bytes_accessed=8 * size, transcendentals=0),
        name="line_derivative",
    )(x)


def base_products(synth, along, u, us, base, geo):
    s_n, c_n, l_n, m_n, e_n = u.shape
    p_n = base.shape[2]

    def kernel(synth_ref, along_ref, u_ref, us_ref, b_ref, g_ref, vr_ref, part_ref):
        l = pl.program_id(0)
        s_mat = synth_ref[...]
        z_mat = along_ref[...]
        field = lambda i: b_ref[i, 0].astype(jnp.float32)
        dot = functools.partial(jnp.dot, precision=HIGH, preferred_element_type=jnp.float32)
        g = [g_ref[i, pl.ds(l, 1), :] for i in range(4)]
        ux, uy = field(0), field(1)
        vr_ref[0] = ux * g[0] + uy * g[2]
        vs = ux * g[1] + uy * g[3]
        uz = field(2)
        phys = []
        for c in range(3):
            coef = u_ref[:, c, 0].reshape(s_n * m_n, e_n)
            phys.append(dot(s_mat, coef))
            dz = dot(z_mat, coef)
            ds = dot(s_mat, us_ref[:, c, 0].reshape(s_n * m_n, e_n))
            part_ref[c, 0] = -(vs * ds) - uz * dz
        for c in range(3):
            part_ref[c, 0] += phys[0] * field(3 + 3 * c) + phys[1] * field(4 + 3 * c) + phys[2] * field(5 + 3 * c)

    whole = pl.BlockSpec((p_n, p_n), lambda l: (0, 0))
    coefs = pl.BlockSpec((s_n, 3, 1, m_n, e_n), lambda l: (0, 0, l, 0, 0))
    return pl.pallas_call(
        kernel,
        grid=(l_n,),
        in_specs=[
            whole,
            whole,
            coefs,
            coefs,
            pl.BlockSpec((12, 1, p_n, e_n), lambda l: (0, l, 0, 0)),
            pl.BlockSpec((4, l_n, e_n), lambda l: (0, 0, 0)),
        ],
        out_specs=[
            pl.BlockSpec((1, p_n, e_n), lambda l: (l, 0, 0)),
            pl.BlockSpec((3, 1, p_n, e_n), lambda l: (0, l, 0, 0)),
        ],
        out_shape=[
            jax.ShapeDtypeStruct((l_n, p_n, e_n), jnp.float32),
            jax.ShapeDtypeStruct((3, l_n, p_n, e_n), jnp.float32),
        ],
        compiler_params=params(),
        cost_estimate=pl.CostEstimate(
            flops=9 * 2 * 6 * l_n * p_n * p_n * e_n, bytes_accessed=l_n * p_n * e_n * 64, transcendentals=0
        ),
        name="base_products",
    )(synth, along, u, us, base, geo)


def forcing_modes(synth, analysis, ur, vr, part, mass, first):
    s_n, c_n, l_n, m_n, e_n = ur.shape
    p_n = vr.shape[1]

    def kernel(synth_ref, analysis_ref, ur_ref, vr_ref, part_ref, mass_ref, o_ref):
        l = pl.program_id(1)
        dot = functools.partial(jnp.dot, precision=HIGH, preferred_element_type=jnp.float32)
        dr = dot(synth_ref[...], ur_ref[:, 0, 0].reshape(s_n * m_n, e_n))
        forcing = part_ref[0, 0] - vr_ref[0] * dr
        modes = dot(analysis_ref[...], forcing) * (STEP_SIZE * mass_ref[pl.ds(l, 1), :])
        o_ref[:, 0, 0] = modes.reshape(s_n, m_n, e_n)

    whole = pl.BlockSpec((p_n, p_n), lambda c, l: (0, 0))
    coefs = pl.BlockSpec((s_n, 1, 1, m_n, e_n), lambda c, l: (0, c, l, 0, 0))
    return pl.pallas_call(
        kernel,
        grid=(c_n, l_n),
        in_specs=[
            whole,
            whole,
            coefs,
            pl.BlockSpec((1, p_n, e_n), lambda c, l: (l, 0, 0)),
            pl.BlockSpec((1, 1, p_n, e_n), lambda c, l: (first + c, l, 0, 0)),
            pl.BlockSpec((l_n, e_n), lambda c, l: (0, 0)),
        ],
        out_specs=coefs,
        out_shape=jax.ShapeDtypeStruct(ur.shape, jnp.float32),
        compiler_params=params(),
        cost_estimate=pl.CostEstimate(
            flops=2 * 2 * 6 * c_n * l_n * p_n * p_n * e_n,
            bytes_accessed=c_n * l_n * p_n * e_n * 16,
            transcendentals=0,
        ),
        name="forcing_modes",
    )(synth, analysis, ur, vr, part, mass)


def local_sums(modes, u, mass, pairs, edge_reps, first):
    s_n, c_n, l_n, m_n, e_n = modes.shape
    nodes_n = s_n * l_n
    rows_n = nodes_n * e_n
    step = min(8, l_n)
    per = l_n // step
    close_k, close_r, close_n, far_k, far_r, far_n = pairs
    edges_n = edge_reps.shape[1]
    feats = c_n * m_n

    def kernel(ck, cr, cn, fk, fr, fn, er, f_ref, u_ref, mass_ref, o_ref, e_ref):
        b = pl.program_id(0)

        def fill(t, _):
            node = b * step + t
            weight = mass_ref[pl.ds(node, 1), :]
            rows = [f_ref[0, c, t] + weight * u_ref[0, c, t] for c in range(c_n)]
            if feats < LANES:
                rows.append(jnp.zeros((LANES - feats, e_n), jnp.float32))
            table = jnp.concatenate(rows, axis=0)
            o_ref[pl.ds(pl.multiple_of(node * e_n, e_n), e_n), :] = table.T
            return 0

        lax.fori_loop(0, step, fill, 0)

        @pl.when(b == pl.num_programs(0) - 1)
        def _():
            o_ref[pl.ds(rows_n, 8), :] = jnp.zeros((8, LANES), jnp.float32)

            def close(i, _):
                heads = [cr[i * BATCH + t] for t in range(BATCH)]
                others = [ck[i * BATCH + t] for t in range(BATCH)]
                sums = [o_ref[pl.ds(r, 1), :] + o_ref[pl.ds(k, 1), :] for r, k in zip(heads, others)]
                for r, total in zip(heads, sums):
                    o_ref[pl.ds(r, 1), :] = total
                return 0

            lax.fori_loop(0, pl.cdiv(cn[0], BATCH), close, 0)

            def far(i, _):
                r = fr[i]
                o_ref[pl.ds(r, 1), :] = o_ref[pl.ds(r, 1), :] + o_ref[pl.ds(fk[i], 1), :]
                return 0

            lax.fori_loop(0, fn[0], far, 0)

            def edge(i, _):
                for side in range(2):
                    for t in range(BATCH):
                        e_ref[side, pl.ds(i * BATCH + t, 1), :] = o_ref[pl.ds(er[side, i * BATCH + t], 1), :]
                return 0

            lax.fori_loop(0, edges_n // BATCH, edge, 0)

    smem = pl.BlockSpec(memory_space=pltpu.SMEM)
    where = lambda b: (b // per, 0, b % per, 0, 0)
    where_u = lambda b: (b // per, first // c_n, b % per, 0, 0)
    return pl.pallas_call(
        kernel,
        grid=(nodes_n // step,),
        in_specs=[smem] * 7
        + [
            pl.BlockSpec((1, c_n, step, m_n, e_n), where),
            pl.BlockSpec((1, c_n, step, m_n, e_n), where_u),
            pl.BlockSpec((nodes_n, e_n), lambda b: (0, 0)),
        ],
        out_specs=[
            pl.BlockSpec((rows_n + 8, LANES), lambda b: (0, 0)),
            pl.BlockSpec((2, edges_n, LANES), lambda b: (0, 0, 0)),
        ],
        out_shape=[
            jax.ShapeDtypeStruct((rows_n + 8, LANES), jnp.float32),
            jax.ShapeDtypeStruct((2, edges_n, LANES), jnp.float32),
        ],
        compiler_params=params(),
        cost_estimate=pl.CostEstimate(
            flops=rows_n * LANES * 400, bytes_accessed=rows_n * LANES * 12, transcendentals=0
        ),
        name="local_sums",
    )(close_k, close_r, close_n, far_k, far_r, far_n, edge_reps, modes, u, mass)


def spread(table, came, edge_reps, back_k, back_r, inverse, held, shape, first, c_n):
    _, m_n, nodes_n, e_n = shape
    rows_n = nodes_n * e_n
    step = 8
    edges_n = edge_reps.shape[1]
    pairs_n = back_k.shape[0]

    def kernel(er, bk, br, t_ref, came_ref, inv_ref, *rest):
        o_ref, work = rest[-2], t_ref
        b = pl.program_id(0)

        @pl.when(b == 0)
        def _():
            def edge(i, _):
                for side in range(2):
                    spots = [er[side, i * BATCH + t] for t in range(BATCH)]
                    sums = [
                        work[pl.ds(r, 1), :] + came_ref[side, pl.ds(i * BATCH + t, 1), :]
                        for t, r in enumerate(spots)
                    ]
                    for r, total in zip(spots, sums):
                        work[pl.ds(r, 1), :] = total
                return 0

            lax.fori_loop(0, edges_n // BATCH, edge, 0)

            def back(i, _):
                got = [work[pl.ds(br[i * BATCH + t], 1), :] for t in range(BATCH)]
                for t, row in enumerate(got):
                    work[pl.ds(bk[i * BATCH + t], 1), :] = row
                return 0

            lax.fori_loop(0, pairs_n // BATCH, back, 0)

        stage = rest[-1]

        def node(t, _):
            n = b * step + t
            rows = work[pl.ds(pl.multiple_of(n * e_n, e_n), e_n), :].T
            scaled = rows * inv_ref[pl.ds(n, 1), :]
            for c in range(c_n):
                stage[c, t] = scaled[c * m_n : (c + 1) * m_n]
            return 0

        lax.fori_loop(0, step, node, 0)
        for c in range(c_n):
            o_ref[c] = jnp.swapaxes(stage[c], 0, 1)

    smem = pl.BlockSpec(memory_space=pltpu.SMEM)
    in_specs = [smem] * 3 + [
        pl.BlockSpec((rows_n + 8, LANES), lambda b: (0, 0)),
        pl.BlockSpec((2, edges_n, LANES), lambda b: (0, 0, 0)),
        pl.BlockSpec((nodes_n, e_n), lambda b: (0, 0)),
    ]
    args = [edge_reps, back_k, back_r, table, came, inverse]
    aliases = {}
    if held is not None:
        in_specs.append(pl.BlockSpec(memory_space=pl.ANY))
        args.append(held)
        aliases = {len(args) - 1: 0}
    return pl.pallas_call(
        kernel,
        grid=(nodes_n // step,),
        in_specs=in_specs,
        out_specs=pl.BlockSpec((c_n, m_n, step, e_n), lambda b: (first // c_n, 0, b, 0)),
        out_shape=jax.ShapeDtypeStruct(shape, jnp.float32),
        scratch_shapes=[pltpu.VMEM((c_n, step, m_n, e_n), jnp.float32)],
        input_output_aliases=aliases,
        compiler_params=params(),
        cost_estimate=pl.CostEstimate(
            flops=rows_n * LANES * 400, bytes_accessed=rows_n * LANES * 12, transcendentals=0
        ),
        name="spread",
    )(*args)


def fill_up(values, multiple, filler):
    short = -values.shape[-1] % multiple
    pad = [(0, 0)] * (values.ndim - 1) + [(0, short)]
    return jnp.pad(values, pad, constant_values=filler)


def pair_lists(ids, edges):
    rows_n = ids.shape[0]
    place = jnp.arange(rows_n, dtype=jnp.int32)
    ids_sorted, member = lax.sort((ids, place), num_keys=1)
    head = jnp.concatenate([jnp.ones((1,), bool), ids_sorted[1:] != ids_sorted[:-1]])
    code = lax.cummax(jnp.where(head, place * rows_n + member, 0))
    rep = code % rows_n
    rank = place - code // rows_n
    group = jnp.where(rank == 0, 2, jnp.where(rank == 1, 0, 1)).astype(jnp.int32)
    _, member_l, rep_l = lax.sort((group, member, rep), num_keys=1)
    pairs_n = rows_n - UNIQUE
    member_l = member_l[:pairs_n]
    rep_l = rep_l[:pairs_n]
    close_n = jnp.sum(group == 0, dtype=jnp.int32)
    far_n = pairs_n - close_n
    spot = jnp.arange(pairs_n, dtype=jnp.int32)
    close_k = fill_up(jnp.where(spot < close_n, member_l, rows_n), BATCH, rows_n)
    close_r = fill_up(jnp.where(spot < close_n, rep_l, rows_n), BATCH, rows_n)
    far_k = jnp.roll(member_l, -close_n)
    far_r = jnp.roll(rep_l, -close_n)
    back_k = fill_up(member_l, BATCH, rows_n)
    back_r = fill_up(rep_l, BATCH, rows_n)
    flat = edges.reshape(-1)
    start = jnp.sum(ids_sorted[None, :] < flat[:, None], axis=1, dtype=jnp.int32)
    edge_reps = fill_up(member[start].reshape(edges.shape), BATCH, rows_n)
    pairs = (close_k, close_r, close_n.reshape(1), far_k, far_r, far_n.reshape(1))
    return pairs, (back_k, back_r), edge_reps


def swap_edges(sums):
    count = lax.axis_size("mesh")
    up = [(i, (i + 1) % count) for i in range(count)]
    down = [(j, i) for i, j in up]
    return jnp.stack([lax.ppermute(sums[1], "mesh", up), lax.ppermute(sums[0], "mesh", down)])


def inverse_mass(mass, ids, edges):
    summed = jnp.zeros((UNIQUE,), jnp.float32).at[ids].add(mass.reshape(-1))
    came = swap_edges(summed[edges])
    summed = summed.at[edges.reshape(-1)].add(came.reshape(-1))
    return (1.0 / summed[ids]).reshape(mass.shape)


def exchange(x):
    count = lax.axis_size("four")
    me = lax.axis_index("four")
    came = []
    for step in range(1, count):
        piece = lax.dynamic_index_in_dim(x, (me + step) % count, 0, keepdims=False)
        came.append(lax.ppermute(piece, "four", [(i, (i + step) % count) for i in range(count)]))
    for step, piece in enumerate(came, 1):
        x = lax.dynamic_update_index_in_dim(x, piece, (me - step) % count, 0)
    return x


def body(adj_modes, base_flow, geometry, mass, connect, edge_nodes):
    comps, m_n, nodes_n, e_n = adj_modes.shape
    parts = lax.axis_size("four")
    l_n = nodes_n // parts
    mine = lax.axis_index("four") * l_n
    synth, along, analysis = plane_tables(PLANES)
    together = lax.optimization_barrier
    u = node_major(adj_modes, parts)
    u, connect, edge_nodes, mass, base_flow = together((u, connect, edge_nodes, mass, base_flow))
    u_here = exchange(u)

    ids = connect.reshape(-1)
    edges = edge_nodes[0]
    spot = lambda n: (n // l_n, n % l_n)
    along_r = [[spot(NP * i + j) for i in range(NP)] for j in range(NP)]
    ur_a, ur_b = derivative(u, along_r, 0, 2), derivative(u, along_r, 2, 1)
    pairs, backs, edge_reps = pair_lists(ids, edges)
    inverse = inverse_mass(mass, ids, edges)
    base = base_flow.transpose(0, 2, 1, 3)
    ur_a, ur_b, u_here, pairs, backs, edge_reps, inverse, base = together(
        (ur_a, ur_b, u_here, pairs, backs, edge_reps, inverse, base)
    )

    ur_here_a = exchange(ur_a)
    if l_n % NP == 0:
        lines = [[(a, l + j) for j in range(NP)] for a in range(parts) for l in range(0, l_n, NP)]
        us_here = derivative(u_here, lines)
    else:
        us_here = exchange(derivative(u, [[spot(NP * i + j) for j in range(NP)] for i in range(NP)]))
    geo = lax.dynamic_slice_in_dim(geometry, mine, l_n, 1)
    mass_here = lax.dynamic_slice_in_dim(mass, mine, l_n, 0)
    vr, part = base_products(synth, along, u_here, us_here, base, geo)
    ur_b, ur_here_a, vr, part = together((ur_b, ur_here_a, vr, part))

    ur_here_b = exchange(ur_b)
    f_a = forcing_modes(synth, analysis, ur_here_a, vr, part, mass_here, 0)
    f_a, ur_here_b = together((f_a, ur_here_b))

    modes_a = exchange(f_a)
    f_b = forcing_modes(synth, analysis, ur_here_b, vr, part, mass_here, 2)
    f_b, modes_a = together((f_b, modes_a))

    modes_b = exchange(f_b)
    table_a, rims_a = local_sums(modes_a, u, mass, pairs, edge_reps, 0)
    out = spread(table_a, swap_edges(rims_a), edge_reps, *backs, inverse, None, adj_modes.shape, 0, 2)
    modes_b, out = together((modes_b, out))

    table_b, rims_b = local_sums(modes_b, u, mass, pairs, edge_reps, 2)
    return spread(table_b, swap_edges(rims_b), edge_reps, *backs, inverse, out, adj_modes.shape, 2, 1)


def solution(mesh):
    return jax.shard_map(
        body,
        mesh=mesh,
        in_specs=(
            P(None, "four", None, "mesh"),
            P(None, None, "four", "mesh"),
            P(None, None, "mesh"),
            P(None, "mesh"),
            P(None, "mesh"),
            P("mesh", None, None),
        ),
        out_specs=P(None, "four", None, "mesh"),
        check_vma=False,
    )
```

```python
import math

import jax
import jax.numpy as jnp
import ml_dtypes
import numpy as np
from jax import lax
from jax.experimental import pallas as pl
from jax.experimental.pallas import tpu as pltpu
from jax.sharding import PartitionSpec as P

NP = 8
PLANES = 256
UNIQUE = 12825
STEP_SIZE = 0.1
LANES = 128
BATCH = 8
RANKS = 3
VMEM_LIMIT = 56 * 1024 * 1024


def legendre_values(degree, point):
    before = 1.0
    current = point
    for order in range(1, degree):
        after = ((2 * order + 1) * point * current - order * before) / (order + 1)
        before = current
        current = after
    return (current, before)


def gll_derivative(points_n):
    degree = points_n - 1
    points = []
    for index in range(points_n):
        point = -math.cos(math.pi * index / degree)
        for sweep in range(100):
            top_val, below_val = legendre_values(degree, point)
            point = point - (point * top_val - below_val) / (points_n * top_val)
        points.append(point)
    values = [legendre_values(degree, point)[0] for point in points]
    deriv_rows = []
    for row_index in range(points_n):
        row_vals = []
        for col_index in range(points_n):
            if row_index != col_index:
                row_vals.append(
                    values[row_index]
                    / (values[col_index] * (points[row_index] - points[col_index]))
                )
            else:
                row_vals.append(0.0)
        deriv_rows.append(row_vals)
    deriv_rows[0][0] = -degree * (degree + 1) / 4.0
    deriv_rows[degree][degree] = degree * (degree + 1) / 4.0
    return deriv_rows


def plane_tables(planes):
    plane = np.arange(planes)
    wave = plane // 2
    phase = ((plane[:, None] * wave[None, :]) % planes) * (2.0 * math.pi / planes)
    synth = np.where((plane % 2 == 1)[None, :], np.sin(phase), np.cos(phase))
    synth[:, 1] = 1 - 2 * (plane % 2)
    scales = np.where(wave == 0, 1.0 / planes, 2.0 / planes)
    analysis = synth.T * scales[:, None]
    number = wave * (2.0 / planes)
    along = np.zeros_like(synth)
    along[:, 1::2] = number[1::2] * synth[:, 0::2]
    along[:, 0::2] = -number[0::2] * synth[:, 1::2]
    along[:, :2] = 0.0
    return tuple(t.astype(np.float32) for t in (synth, along, analysis))


def params(**kw):
    return pltpu.CompilerParams(vmem_limit_bytes=VMEM_LIMIT, **kw)


def node_major(x, parts):
    c_n, m_n, n_n, e_n = x.shape
    l_n = n_n // parts
    rows = 16

    def kernel(x_ref, o_ref):
        for n in range(0, n_n, 8):
            turned = jnp.swapaxes(x_ref[0, :, n : n + 8, :], 0, 1)
            for t in range(8):
                o_ref[(n + t) // l_n, 0, (n + t) % l_n] = turned[t]

    return pl.pallas_call(
        kernel,
        grid=(c_n, m_n // rows),
        in_specs=[pl.BlockSpec((1, rows, n_n, e_n), lambda c, m: (c, m, 0, 0))],
        out_specs=pl.BlockSpec((parts, 1, l_n, rows, e_n), lambda c, m: (0, c, 0, m, 0)),
        out_shape=jax.ShapeDtypeStruct((parts, c_n, l_n, m_n, e_n), jnp.float32),
        compiler_params=params(),
        cost_estimate=pl.CostEstimate(flops=x.size, bytes_accessed=8 * x.size, transcendentals=0),
        name="node_major",
    )(x)


def derivative(x, groups, first=0, c_n=3):
    a_n, _, l_n, m_n, e_n = x.shape
    deriv = gll_derivative(NP)
    rows = 8

    def kernel(x_ref, o_ref):
        for line in groups:
            vals = [x_ref[a, 0, l] for a, l in line]
            for i, (a, l) in enumerate(line):
                total = deriv[i][0] * vals[0]
                for k in range(1, NP):
                    if deriv[i][k] != 0.0:
                        total = total + deriv[i][k] * vals[k]
                o_ref[a, 0, l] = total

    block = (a_n, 1, l_n, rows, e_n)
    size = a_n * c_n * l_n * m_n * e_n
    return pl.pallas_call(
        kernel,
        grid=(c_n, m_n // rows),
        in_specs=[pl.BlockSpec(block, lambda c, m: (0, first + c, 0, m, 0))],
        out_specs=pl.BlockSpec(block, lambda c, m: (0, c, 0, m, 0)),
        out_shape=jax.ShapeDtypeStruct((a_n, c_n, l_n, m_n, e_n), jnp.float32),
        compiler_params=params(),
        cost_estimate=pl.CostEstimate(flops=16 * size, bytes_accessed=8 * size, transcendentals=0),
        name="line_derivative",
    )(x)


def split(x):
    high = x.astype(jnp.bfloat16)
    return high, (x - high.astype(jnp.float32)).astype(jnp.bfloat16)


def left_form(table):
    high = table.astype(ml_dtypes.bfloat16)
    low = (table - high.astype(np.float32)).astype(ml_dtypes.bfloat16)
    return jnp.asarray(np.concatenate([high, high, low], axis=1))


def right_form(x):
    high, low = split(x)
    return jnp.concatenate([high, low, high], axis=0)


def product(left, right):
    return jnp.dot(left, right, preferred_element_type=jnp.float32)


def base_products(synth_along, synth, u_a, u_b, us_a, us_b, base, geo):
    s_n, _, l_n, m_n, e_n = u_a.shape
    p_n = base.shape[2]

    def kernel(both_ref, synth_ref, ua_ref, ub_ref, usa_ref, usb_ref, b_ref, g_ref, vr_ref, part_ref):
        l = pl.program_id(0)
        field = lambda i: b_ref[i, 0].astype(jnp.float32)
        g = [g_ref[i, pl.ds(l, 1), :] for i in range(4)]
        ux, uy = field(0), field(1)
        vr_ref[0] = ux * g[0] + uy * g[2]
        vs = ux * g[1] + uy * g[3]
        uz = field(2)
        phys = []
        for c in range(3):
            u_c = ua_ref[:, 0, 0] if c == 0 else ub_ref[:, c - 1, 0]
            us_c = usa_ref[:, 0, 0] if c == 0 else usb_ref[:, c - 1, 0]
            both = product(both_ref[...], right_form(u_c.reshape(s_n * m_n, e_n)))
            phys.append(both[:p_n])
            ds = product(synth_ref[...], right_form(us_c.reshape(s_n * m_n, e_n)))
            part_ref[c, 0] = -(vs * ds) - uz * both[p_n:]
        for c in range(3):
            part_ref[c, 0] += phys[0] * field(3 + 3 * c) + phys[1] * field(4 + 3 * c) + phys[2] * field(5 + 3 * c)

    one = pl.BlockSpec((s_n, 1, 1, m_n, e_n), lambda l: (0, 0, l, 0, 0))
    two = pl.BlockSpec((s_n, 2, 1, m_n, e_n), lambda l: (0, 0, l, 0, 0))
    return pl.pallas_call(
        kernel,
        grid=(l_n,),
        in_specs=[
            pl.BlockSpec((2 * p_n, 3 * p_n), lambda l: (0, 0)),
            pl.BlockSpec((p_n, 3 * p_n), lambda l: (0, 0)),
            one,
            two,
            one,
            two,
            pl.BlockSpec((12, 1, p_n, e_n), lambda l: (0, l, 0, 0)),
            pl.BlockSpec((4, l_n, e_n), lambda l: (0, 0, 0)),
        ],
        out_specs=[
            pl.BlockSpec((1, p_n, e_n), lambda l: (l, 0, 0)),
            pl.BlockSpec((3, 1, p_n, e_n), lambda l: (0, l, 0, 0)),
        ],
        out_shape=[
            jax.ShapeDtypeStruct((l_n, p_n, e_n), jnp.float32),
            jax.ShapeDtypeStruct((3, l_n, p_n, e_n), jnp.float32),
        ],
        compiler_params=params(),
        cost_estimate=pl.CostEstimate(
            flops=9 * 2 * 3 * l_n * p_n * p_n * e_n, bytes_accessed=l_n * p_n * e_n * 64, transcendentals=0
        ),
        name="base_products",
    )(synth_along, synth, u_a, u_b, us_a, us_b, base, geo)


def forcing_modes(synth, analysis, ur, vr, part, mass, held_at, first, c_n):
    s_n, _, l_n, m_n, e_n = ur.shape
    p_n = vr.shape[1]

    def kernel(synth_ref, analysis_ref, ur_ref, vr_ref, part_ref, mass_ref, o_ref):
        l = pl.program_id(1)
        dr = product(synth_ref[...], right_form(ur_ref[:, 0, 0].reshape(s_n * m_n, e_n)))
        forcing = part_ref[0, 0] - vr_ref[0] * dr
        modes = product(analysis_ref[...], right_form(forcing)) * (STEP_SIZE * mass_ref[pl.ds(l, 1), :])
        o_ref[:, 0, 0] = modes.reshape(s_n, m_n, e_n)

    whole = pl.BlockSpec((p_n, 3 * p_n), lambda c, l: (0, 0))
    block = (s_n, 1, 1, m_n, e_n)
    return pl.pallas_call(
        kernel,
        grid=(c_n, l_n),
        in_specs=[
            whole,
            whole,
            pl.BlockSpec(block, lambda c, l: (0, held_at + c, l, 0, 0)),
            pl.BlockSpec((1, p_n, e_n), lambda c, l: (l, 0, 0)),
            pl.BlockSpec((1, 1, p_n, e_n), lambda c, l: (first + c, l, 0, 0)),
            pl.BlockSpec((l_n, e_n), lambda c, l: (0, 0)),
        ],
        out_specs=pl.BlockSpec(block, lambda c, l: (0, c, l, 0, 0)),
        out_shape=jax.ShapeDtypeStruct((s_n, c_n, l_n, m_n, e_n), jnp.float32),
        compiler_params=params(),
        cost_estimate=pl.CostEstimate(
            flops=2 * 2 * 3 * c_n * l_n * p_n * p_n * e_n,
            bytes_accessed=c_n * l_n * p_n * e_n * 16,
            transcendentals=0,
        ),
        name="forcing_modes",
    )(synth, analysis, ur, vr, part, mass)


def local_sums(modes, u, mass, pairs, edge_reps, first):
    s_n, c_n, l_n, m_n, e_n = modes.shape
    nodes_n = s_n * l_n
    rows_n = nodes_n * e_n
    step = min(8, l_n)
    per = l_n // step
    members, reps, bounds = pairs
    edges_n = edge_reps.shape[1]
    feats = c_n * m_n

    def kernel(mem, rep, bnd, er, f_ref, u_ref, mass_ref, o_ref, low_ref, up_ref):
        b = pl.program_id(0)
        for t in range(step):
            node = b * step + t
            weight = mass_ref[pl.ds(node, 1), :]
            rows = [f_ref[0, c, t] + weight * u_ref[0, c, t] for c in range(c_n)]
            table = jnp.concatenate(rows, axis=0) if c_n > 1 else rows[0]
            o_ref[pl.ds(pl.multiple_of(node * e_n, e_n), e_n), :] = table.T

        @pl.when(b == pl.num_programs(0) - 1)
        def _():
            o_ref[pl.ds(rows_n, 8), :] = jnp.zeros((8, feats), jnp.float32)

            for rank in range(RANKS):

                def close(i, _):
                    at = bnd[2 * rank] + i * BATCH
                    heads = [rep[at + t] for t in range(BATCH)]
                    others = [mem[at + t] for t in range(BATCH)]
                    sums = [o_ref[pl.ds(r, 1), :] + o_ref[pl.ds(k, 1), :] for r, k in zip(heads, others)]
                    for r, total in zip(heads, sums):
                        o_ref[pl.ds(r, 1), :] = total
                    return 0

                lax.fori_loop(0, pl.cdiv(bnd[2 * rank + 1], BATCH), close, 0)

            def far(i, _):
                at = bnd[2 * RANKS] + i
                r = rep[at]
                o_ref[pl.ds(r, 1), :] = o_ref[pl.ds(r, 1), :] + o_ref[pl.ds(mem[at], 1), :]
                return 0

            lax.fori_loop(0, bnd[2 * RANKS + 1], far, 0)

            def edge(i, _):
                for side, to in enumerate((low_ref, up_ref)):
                    got = [o_ref[pl.ds(er[side, i * BATCH + t], 1), :] for t in range(BATCH)]
                    for t, row in enumerate(got):
                        to[pl.ds(i * BATCH + t, 1), :] = row
                return 0

            lax.fori_loop(0, edges_n // BATCH, edge, 0)

    smem = pl.BlockSpec(memory_space=pltpu.SMEM)
    where = lambda b: (b // per, 0, b % per, 0, 0)
    where_u = lambda b: (b // per, first // c_n, b % per, 0, 0)
    rim = pl.BlockSpec((edges_n, feats), lambda b: (0, 0))
    rim_shape = jax.ShapeDtypeStruct((edges_n, feats), jnp.float32)
    return pl.pallas_call(
        kernel,
        grid=(nodes_n // step,),
        in_specs=[smem] * 4
        + [
            pl.BlockSpec((1, c_n, step, m_n, e_n), where),
            pl.BlockSpec((1, c_n, step, m_n, e_n), where_u),
            pl.BlockSpec((nodes_n, e_n), lambda b: (0, 0)),
        ],
        out_specs=[pl.BlockSpec((rows_n + 8, feats), lambda b: (0, 0)), rim, rim],
        out_shape=[jax.ShapeDtypeStruct((rows_n + 8, feats), jnp.float32), rim_shape, rim_shape],
        compiler_params=params(),
        cost_estimate=pl.CostEstimate(
            flops=rows_n * LANES * 400, bytes_accessed=rows_n * LANES * 12, transcendentals=0
        ),
        name="local_sums",
    )(members, reps, bounds, edge_reps, modes, u, mass)


def spread(table, rims, pairs, edge_reps, inverse, held, shape, first, c_n):
    _, m_n, nodes_n, e_n = shape
    rows_n = nodes_n * e_n
    step = 8
    edges_n = edge_reps.shape[1]
    members, reps, _ = pairs
    pairs_n = members.shape[0]
    feats = c_n * m_n

    def kernel(mem, rep, er, t_ref, low_ref, up_ref, inv_ref, *rest):
        o_ref, stage = rest[-2:]
        b = pl.program_id(0)

        @pl.when(b == 0)
        def _():
            def edge(i, _):
                for side, came in enumerate((low_ref, up_ref)):
                    spots = [er[side, i * BATCH + t] for t in range(BATCH)]
                    sums = [
                        t_ref[pl.ds(r, 1), :] + came[pl.ds(i * BATCH + t, 1), :] for t, r in enumerate(spots)
                    ]
                    for r, total in zip(spots, sums):
                        t_ref[pl.ds(r, 1), :] = total
                return 0

            lax.fori_loop(0, edges_n // BATCH, edge, 0)

            def back(i, _):
                got = [t_ref[pl.ds(rep[i * BATCH + t], 1), :] for t in range(BATCH)]
                for t, row in enumerate(got):
                    t_ref[pl.ds(mem[i * BATCH + t], 1), :] = row
                return 0

            lax.fori_loop(0, pairs_n // BATCH, back, 0)

        for t in range(step):
            n = b * step + t
            rows = t_ref[pl.ds(pl.multiple_of(n * e_n, e_n), e_n), :].T
            scaled = rows * inv_ref[pl.ds(n, 1), :]
            for c in range(c_n):
                stage[c, t] = scaled[c * m_n : (c + 1) * m_n]
        for c in range(c_n):
            o_ref[c] = jnp.swapaxes(stage[c], 0, 1)

    smem = pl.BlockSpec(memory_space=pltpu.SMEM)
    rim = pl.BlockSpec((edges_n, feats), lambda b: (0, 0))
    in_specs = [smem] * 3 + [
        pl.BlockSpec((rows_n + 8, feats), lambda b: (0, 0)),
        rim,
        rim,
        pl.BlockSpec((nodes_n, e_n), lambda b: (0, 0)),
    ]
    args = [members, reps, edge_reps, table, *rims, inverse]
    aliases = {}
    if held is not None:
        in_specs.append(pl.BlockSpec(memory_space=pl.ANY))
        args.append(held)
        aliases = {len(args) - 1: 0}
    return pl.pallas_call(
        kernel,
        grid=(nodes_n // step,),
        in_specs=in_specs,
        out_specs=pl.BlockSpec((c_n, m_n, step, e_n), lambda b: (first // c_n, 0, b, 0)),
        out_shape=jax.ShapeDtypeStruct(shape, jnp.float32),
        scratch_shapes=[pltpu.VMEM((c_n, step, m_n, e_n), jnp.float32)],
        input_output_aliases=aliases,
        compiler_params=params(),
        cost_estimate=pl.CostEstimate(
            flops=rows_n * LANES * 400, bytes_accessed=rows_n * LANES * 12, transcendentals=0
        ),
        name="spread",
    )(*args)


def fill_up(values, multiple, filler):
    short = -values.shape[-1] % multiple
    pad = [(0, 0)] * (values.ndim - 1) + [(0, short)]
    return jnp.pad(values, pad, constant_values=filler)


def pair_lists(ids, edges):
    rows_n = ids.shape[0]
    place = jnp.arange(rows_n, dtype=jnp.int32)
    ids_sorted, member = lax.sort((ids, place), num_keys=1)
    head = jnp.concatenate([jnp.ones((1,), bool), ids_sorted[1:] != ids_sorted[:-1]])
    code = lax.cummax(jnp.where(head, place * rows_n + member, 0))
    rep = code % rows_n
    rank = place - code // rows_n
    group = jnp.where(rank == 0, RANKS + 2, jnp.minimum(rank, RANKS + 1)).astype(jnp.int32)
    spare = jnp.full((RANKS * BATCH,), rows_n, jnp.int32)
    spare_group = jnp.arange(RANKS * BATCH, dtype=jnp.int32) // BATCH + 1
    _, members, reps = lax.sort(
        (
            jnp.concatenate([group, spare_group]),
            jnp.concatenate([member, spare]),
            jnp.concatenate([rep, spare]),
        ),
        num_keys=1,
        is_stable=True,
    )
    pairs_n = rows_n - UNIQUE + RANKS * BATCH
    numbers = jnp.stack([jnp.sum(group == r, dtype=jnp.int32) for r in range(1, RANKS + 2)])
    starts = jnp.cumsum(numbers) - numbers + BATCH * jnp.arange(RANKS + 1, dtype=jnp.int32)
    bounds = jnp.stack([starts, numbers], axis=1).reshape(-1).astype(jnp.int32)
    members = fill_up(members[:pairs_n], BATCH, rows_n)
    reps = fill_up(reps[:pairs_n], BATCH, rows_n)
    flat = edges.reshape(-1)
    start = jnp.sum(ids_sorted[None, :] < flat[:, None], axis=1, dtype=jnp.int32)
    edge_reps = fill_up(member[start].reshape(edges.shape), BATCH, rows_n)
    return (members, reps, bounds), edge_reps


def swap_edges(low, up):
    count = lax.axis_size("mesh")
    upward = [(i, (i + 1) % count) for i in range(count)]
    downward = [(j, i) for i, j in upward]
    return lax.ppermute(up, "mesh", upward), lax.ppermute(low, "mesh", downward)


def inverse_mass(mass, ids, edges):
    summed = jnp.zeros((UNIQUE,), jnp.float32).at[ids].add(mass.reshape(-1))
    came = jnp.concatenate(swap_edges(summed[edges[0]], summed[edges[1]]))
    summed = summed.at[edges.reshape(-1)].add(came)
    return (1.0 / summed[ids]).reshape(mass.shape)


def exchange(x):
    return lax.all_to_all(x, "four", split_axis=0, concat_axis=0, tiled=True)


def body(adj_modes, base_flow, geometry, mass, connect, edge_nodes):
    comps, m_n, nodes_n, e_n = adj_modes.shape
    parts = lax.axis_size("four")
    l_n = nodes_n // parts
    mine = lax.axis_index("four") * l_n
    synth, along, analysis = plane_tables(PLANES)
    both_3 = left_form(np.concatenate([synth, along]))
    synth_3, analysis_3 = left_form(synth), left_form(analysis)
    together = lax.optimization_barrier
    spot = lambda n: (n // l_n, n % l_n)
    along_r = [[spot(NP * i + j) for i in range(NP)] for j in range(NP)]
    along_s = [[spot(NP * i + j) for j in range(NP)] for i in range(NP)]
    inside = [[(a, l + j) for j in range(NP)] for a in range(parts) for l in range(0, l_n, NP)]
    whole_rows = l_n % NP == 0

    u_first = adj_modes[0].reshape(m_n, parts, l_n, e_n).transpose(1, 0, 2, 3)
    u_first, adj_modes = together((u_first, adj_modes))
    first_here = exchange(u_first)

    u = node_major(adj_modes, parts)
    ur_a, ur_b = derivative(u, along_r, 0, 2), derivative(u, along_r, 2, 1)
    sent = [u[:, 1:], ur_a] + ([] if whole_rows else [derivative(u, along_s)])
    sent = jnp.concatenate(sent, axis=1)
    sent, u, ur_b, first_here, connect, edge_nodes, mass, base_flow = together(
        (sent, u, ur_b, first_here, connect, edge_nodes, mass, base_flow)
    )

    here = exchange(sent)
    edges = edge_nodes[0]
    ids = connect.reshape(-1)
    pairs, edge_reps = pair_lists(ids, edges)
    inverse = inverse_mass(mass, ids, edges)
    base = base_flow.transpose(0, 2, 1, 3)
    if l_n % 8 == 0:
        u0_here = node_major(first_here, 1).reshape(parts, 1, l_n, m_n, e_n)
    else:
        u0_here = first_here.transpose(0, 2, 1, 3)[:, None]
    us0_here = derivative(u0_here, inside, 0, 1) if whole_rows else None
    held = (here, ur_b, pairs, edge_reps, inverse, base, u0_here, us0_here)
    here, ur_b, pairs, edge_reps, inverse, base, u0_here, us0_here = together(held)

    ur_b_here = exchange(ur_b)
    us_here = derivative(here, inside, 0, 2) if whole_rows else here[:, 5:7]
    if not whole_rows:
        us0_here = here[:, 4:5]
    geo = lax.dynamic_slice_in_dim(geometry, mine, l_n, 1)
    mass_here = lax.dynamic_slice_in_dim(mass, mine, l_n, 0)
    vr, part = base_products(both_3, synth_3, u0_here, here, us0_here, us_here, base, geo)
    f_a = forcing_modes(synth_3, analysis_3, here, vr, part, mass_here, 2, 0, 2)
    f_a, ur_b_here = together((f_a, ur_b_here))

    modes_a = exchange(f_a)
    f_b = forcing_modes(synth_3, analysis_3, ur_b_here, vr, part, mass_here, 0, 2, 1)
    f_b, modes_a = together((f_b, modes_a))

    modes_b = exchange(f_b)
    table, *rims = local_sums(modes_a, u, mass, pairs, edge_reps, 0)
    out = spread(table, swap_edges(*rims), pairs, edge_reps, inverse, None, adj_modes.shape, 0, 2)
    modes_b, out = together((modes_b, out))

    table, *rims = local_sums(modes_b, u, mass, pairs, edge_reps, 2)
    return spread(table, swap_edges(*rims), pairs, edge_reps, inverse, out, adj_modes.shape, 2, 1)


def solution(mesh):
    return jax.shard_map(
        body,
        mesh=mesh,
        in_specs=(
            P(None, "four", None, "mesh"),
            P(None, None, "four", "mesh"),
            P(None, None, "mesh"),
            P(None, "mesh"),
            P(None, "mesh"),
            P("mesh", None, None),
        ),
        out_specs=P(None, "four", None, "mesh"),
        check_vma=False,
    )
```

```python
import math

import jax
import jax.numpy as jnp
import ml_dtypes
import numpy as np
from jax import lax
from jax.experimental import pallas as pl
from jax.experimental.pallas import tpu as pltpu
from jax.sharding import PartitionSpec as P

NP = 8
PLANES = 256
UNIQUE = 12825
STEP_SIZE = 0.1
LANES = 128
BATCH = 16
CLASSES = 4
VMEM_LIMIT = 56 * 1024 * 1024


def legendre_values(degree, point):
    before = 1.0
    current = point
    for order in range(1, degree):
        after = ((2 * order + 1) * point * current - order * before) / (order + 1)
        before = current
        current = after
    return (current, before)


def gll_derivative(points_n):
    degree = points_n - 1
    points = []
    for index in range(points_n):
        point = -math.cos(math.pi * index / degree)
        for sweep in range(100):
            top_val, below_val = legendre_values(degree, point)
            point = point - (point * top_val - below_val) / (points_n * top_val)
        points.append(point)
    values = [legendre_values(degree, point)[0] for point in points]
    deriv_rows = []
    for row_index in range(points_n):
        row_vals = []
        for col_index in range(points_n):
            if row_index != col_index:
                row_vals.append(
                    values[row_index]
                    / (values[col_index] * (points[row_index] - points[col_index]))
                )
            else:
                row_vals.append(0.0)
        deriv_rows.append(row_vals)
    deriv_rows[0][0] = -degree * (degree + 1) / 4.0
    deriv_rows[degree][degree] = degree * (degree + 1) / 4.0
    return deriv_rows


def plane_tables(planes):
    plane = np.arange(planes)
    wave = plane // 2
    phase = ((plane[:, None] * wave[None, :]) % planes) * (2.0 * math.pi / planes)
    synth = np.where((plane % 2 == 1)[None, :], np.sin(phase), np.cos(phase))
    synth[:, 1] = 1 - 2 * (plane % 2)
    scales = np.where(wave == 0, 1.0 / planes, 2.0 / planes)
    analysis = synth.T * scales[:, None]
    number = wave * (2.0 / planes)
    along = np.zeros_like(synth)
    along[:, 1::2] = number[1::2] * synth[:, 0::2]
    along[:, 0::2] = -number[0::2] * synth[:, 1::2]
    along[:, :2] = 0.0
    return tuple(t.astype(np.float32) for t in (synth, along, analysis))


def params(**kw):
    return pltpu.CompilerParams(vmem_limit_bytes=VMEM_LIMIT, **kw)


def node_major(x, parts):
    c_n, m_n, n_n, e_n = x.shape
    l_n = n_n // parts
    rows = 16

    def kernel(x_ref, o_ref):
        for n in range(0, n_n, 8):
            turned = jnp.swapaxes(x_ref[0, :, n : n + 8, :], 0, 1)
            for t in range(8):
                o_ref[(n + t) // l_n, 0, (n + t) % l_n] = turned[t]

    return pl.pallas_call(
        kernel,
        grid=(c_n, m_n // rows),
        in_specs=[pl.BlockSpec((1, rows, n_n, e_n), lambda c, m: (c, m, 0, 0))],
        out_specs=pl.BlockSpec((parts, 1, l_n, rows, e_n), lambda c, m: (0, c, 0, m, 0)),
        out_shape=jax.ShapeDtypeStruct((parts, c_n, l_n, m_n, e_n), jnp.float32),
        compiler_params=params(),
        cost_estimate=pl.CostEstimate(flops=x.size, bytes_accessed=8 * x.size, transcendentals=0),
        name="node_major",
    )(x)


def derivative(x, groups, first=0, c_n=3):
    a_n, _, l_n, m_n, e_n = x.shape
    deriv = gll_derivative(NP)
    rows = 8

    def kernel(x_ref, o_ref):
        for line in groups:
            vals = [x_ref[a, 0, l] for a, l in line]
            for i, (a, l) in enumerate(line):
                total = deriv[i][0] * vals[0]
                for k in range(1, NP):
                    if deriv[i][k] != 0.0:
                        total = total + deriv[i][k] * vals[k]
                o_ref[a, 0, l] = total

    block = (a_n, 1, l_n, rows, e_n)
    size = a_n * c_n * l_n * m_n * e_n
    return pl.pallas_call(
        kernel,
        grid=(c_n, m_n // rows),
        in_specs=[pl.BlockSpec(block, lambda c, m: (0, first + c, 0, m, 0))],
        out_specs=pl.BlockSpec(block, lambda c, m: (0, c, 0, m, 0)),
        out_shape=jax.ShapeDtypeStruct((a_n, c_n, l_n, m_n, e_n), jnp.float32),
        compiler_params=params(),
        cost_estimate=pl.CostEstimate(flops=16 * size, bytes_accessed=8 * size, transcendentals=0),
        name="line_derivative",
    )(x)


def split(x):
    high = x.astype(jnp.bfloat16)
    return high, (x - high.astype(jnp.float32)).astype(jnp.bfloat16)


def left_form(table):
    high = table.astype(ml_dtypes.bfloat16)
    low = (table - high.astype(np.float32)).astype(ml_dtypes.bfloat16)
    return jnp.asarray(np.concatenate([high, high, low], axis=1))


def right_form(x):
    high, low = split(x)
    return jnp.concatenate([high, low, high], axis=0)


def product(left, right):
    return jnp.dot(left, right, preferred_element_type=jnp.float32)


def base_products(synth_along, synth, u_a, u_b, us_a, us_b, base, geo):
    s_n, _, l_n, m_n, e_n = u_a.shape
    p_n = base.shape[2]

    def kernel(both_ref, synth_ref, ua_ref, ub_ref, usa_ref, usb_ref, b_ref, g_ref, vr_ref, part_ref):
        l = pl.program_id(0)
        field = lambda i: b_ref[i, 0].astype(jnp.float32)
        g = [g_ref[i, pl.ds(l, 1), :] for i in range(4)]
        ux, uy = field(0), field(1)
        vr_ref[0] = ux * g[0] + uy * g[2]
        vs = ux * g[1] + uy * g[3]
        uz = field(2)
        phys = []
        for c in range(3):
            u_c = ua_ref[:, 0, 0] if c == 0 else ub_ref[:, c - 1, 0]
            us_c = usa_ref[:, 0, 0] if c == 0 else usb_ref[:, c - 1, 0]
            both = product(both_ref[...], right_form(u_c.reshape(s_n * m_n, e_n)))
            phys.append(both[:p_n])
            ds = product(synth_ref[...], right_form(us_c.reshape(s_n * m_n, e_n)))
            part_ref[c, 0] = -(vs * ds) - uz * both[p_n:]
        for c in range(3):
            part_ref[c, 0] += phys[0] * field(3 + 3 * c) + phys[1] * field(4 + 3 * c) + phys[2] * field(5 + 3 * c)

    one = pl.BlockSpec((s_n, 1, 1, m_n, e_n), lambda l: (0, 0, l, 0, 0))
    two = pl.BlockSpec((s_n, 2, 1, m_n, e_n), lambda l: (0, 0, l, 0, 0))
    return pl.pallas_call(
        kernel,
        grid=(l_n,),
        in_specs=[
            pl.BlockSpec((2 * p_n, 3 * p_n), lambda l: (0, 0)),
            pl.BlockSpec((p_n, 3 * p_n), lambda l: (0, 0)),
            one,
            two,
            one,
            two,
            pl.BlockSpec((12, 1, p_n, e_n), lambda l: (0, l, 0, 0)),
            pl.BlockSpec((4, l_n, e_n), lambda l: (0, 0, 0)),
        ],
        out_specs=[
            pl.BlockSpec((1, p_n, e_n), lambda l: (l, 0, 0)),
            pl.BlockSpec((3, 1, p_n, e_n), lambda l: (0, l, 0, 0)),
        ],
        out_shape=[
            jax.ShapeDtypeStruct((l_n, p_n, e_n), jnp.float32),
            jax.ShapeDtypeStruct((3, l_n, p_n, e_n), jnp.float32),
        ],
        compiler_params=params(),
        cost_estimate=pl.CostEstimate(
            flops=9 * 2 * 3 * l_n * p_n * p_n * e_n, bytes_accessed=l_n * p_n * e_n * 64, transcendentals=0
        ),
        name="base_products",
    )(synth_along, synth, u_a, u_b, us_a, us_b, base, geo)


def forcing_modes(synth, analysis, ur, vr, part, mass, held_at, first, c_n):
    s_n, _, l_n, m_n, e_n = ur.shape
    p_n = vr.shape[1]

    def kernel(synth_ref, analysis_ref, ur_ref, vr_ref, part_ref, mass_ref, o_ref):
        l = pl.program_id(1)
        dr = product(synth_ref[...], right_form(ur_ref[:, 0, 0].reshape(s_n * m_n, e_n)))
        forcing = part_ref[0, 0] - vr_ref[0] * dr
        modes = product(analysis_ref[...], right_form(forcing)) * (STEP_SIZE * mass_ref[pl.ds(l, 1), :])
        o_ref[:, 0, 0] = modes.reshape(s_n, m_n, e_n)

    whole = pl.BlockSpec((p_n, 3 * p_n), lambda c, l: (0, 0))
    block = (s_n, 1, 1, m_n, e_n)
    return pl.pallas_call(
        kernel,
        grid=(c_n, l_n),
        in_specs=[
            whole,
            whole,
            pl.BlockSpec(block, lambda c, l: (0, held_at + c, l, 0, 0)),
            pl.BlockSpec((1, p_n, e_n), lambda c, l: (l, 0, 0)),
            pl.BlockSpec((1, 1, p_n, e_n), lambda c, l: (first + c, l, 0, 0)),
            pl.BlockSpec((l_n, e_n), lambda c, l: (0, 0)),
        ],
        out_specs=pl.BlockSpec(block, lambda c, l: (0, c, l, 0, 0)),
        out_shape=jax.ShapeDtypeStruct((s_n, c_n, l_n, m_n, e_n), jnp.float32),
        compiler_params=params(),
        cost_estimate=pl.CostEstimate(
            flops=2 * 2 * 3 * c_n * l_n * p_n * p_n * e_n,
            bytes_accessed=c_n * l_n * p_n * e_n * 16,
            transcendentals=0,
        ),
        name="forcing_modes",
    )(synth, analysis, ur, vr, part, mass)


def forcing_and_rims(synth, analysis, ur, u, vr, part, mass, connect, edge_ids, c, u_at):
    s_n, _, l_n, m_n, e_n = ur.shape
    p_n = vr.shape[1]
    k_n = edge_ids.shape[0]

    def kernel(synth_ref, analysis_ref, ur_ref, u_ref, vr_ref, part_ref, mass_ref, conn_ref, id_ref, o_ref, rim_ref):
        l = pl.program_id(0)
        dr = product(synth_ref[...], right_form(ur_ref[:, 0, 0].reshape(s_n * m_n, e_n)))
        forcing = part_ref[0, 0] - vr_ref[0] * dr
        weight = mass_ref[pl.ds(l, 1), :]
        modes = product(analysis_ref[...], right_form(forcing)) * (STEP_SIZE * weight)
        o_ref[:, 0, 0] = modes.reshape(s_n, m_n, e_n)
        high, low = split(modes + weight * u_ref[:, 0, 0].reshape(s_n * m_n, e_n))
        here = jnp.where(id_ref[...] == conn_ref[pl.ds(l, 1), :], 1.0, 0.0).astype(jnp.bfloat16)
        sums = lax.dot_general(
            jnp.concatenate([here, here], axis=1),
            jnp.concatenate([high, low], axis=1),
            (((1,), (1,)), ((), ())),
            preferred_element_type=jnp.float32,
        )

        @pl.when(l == 0)
        def _():
            rim_ref[...] = sums

        @pl.when(l > 0)
        def _():
            rim_ref[...] += sums

    whole = pl.BlockSpec((p_n, 3 * p_n), lambda l: (0, 0))
    block = (s_n, 1, 1, m_n, e_n)
    nodes = pl.BlockSpec((l_n, e_n), lambda l: (0, 0))
    return pl.pallas_call(
        kernel,
        grid=(l_n,),
        in_specs=[
            whole,
            whole,
            pl.BlockSpec(block, lambda l: (0, 0, l, 0, 0)),
            pl.BlockSpec(block, lambda l: (0, u_at, l, 0, 0)),
            pl.BlockSpec((1, p_n, e_n), lambda l: (l, 0, 0)),
            pl.BlockSpec((1, 1, p_n, e_n), lambda l: (c, l, 0, 0)),
            nodes,
            nodes,
            pl.BlockSpec((k_n, 1), lambda l: (0, 0)),
        ],
        out_specs=[
            pl.BlockSpec(block, lambda l: (0, 0, l, 0, 0)),
            pl.BlockSpec((k_n, s_n * m_n), lambda l: (0, 0)),
        ],
        out_shape=[
            jax.ShapeDtypeStruct((s_n, 1, l_n, m_n, e_n), jnp.float32),
            jax.ShapeDtypeStruct((k_n, s_n * m_n), jnp.float32),
        ],
        compiler_params=params(),
        cost_estimate=pl.CostEstimate(
            flops=4 * 2 * 3 * l_n * p_n * p_n * e_n, bytes_accessed=l_n * p_n * e_n * 20, transcendentals=0
        ),
        name="forcing_and_rims",
    )(synth, analysis, ur, u, vr, part, mass, connect, edge_ids)


def take_rims(modes, rims, takers):
    s_n, _, l_n, m_n, e_n = modes.shape
    k_n = takers.shape[0]

    def kernel(f_ref, rim_ref, to_ref, o_ref):
        l = pl.program_id(0)
        column = l * e_n + lax.broadcasted_iota(jnp.int32, (1, e_n), 1)
        there = jnp.where(to_ref[...] == column, 1.0, 0.0).astype(jnp.bfloat16)
        high, low = split(rim_ref[...])
        add = product(jnp.concatenate([high, low], axis=1), jnp.concatenate([there, there], axis=0))
        o_ref[:, 0, 0] = f_ref[:, 0, 0] + add.reshape(s_n, m_n, e_n)

    block = pl.BlockSpec((s_n, 1, 1, m_n, e_n), lambda l: (0, 0, l, 0, 0))
    return pl.pallas_call(
        kernel,
        grid=(l_n,),
        in_specs=[
            block,
            pl.BlockSpec((s_n * m_n, k_n), lambda l: (0, 0)),
            pl.BlockSpec((k_n, 1), lambda l: (0, 0)),
        ],
        out_specs=block,
        out_shape=jax.ShapeDtypeStruct(modes.shape, jnp.float32),
        input_output_aliases={0: 0},
        compiler_params=params(),
        cost_estimate=pl.CostEstimate(
            flops=4 * l_n * s_n * m_n * k_n * e_n, bytes_accessed=8 * modes.size, transcendentals=0
        ),
        name="take_rims",
    )(modes, rims, takers)


def rows_of(ref, places):
    return [ref[pl.ds(r, 1), :] for r in places]


def put_rows(ref, places, rows):
    for r, row in zip(places, rows):
        ref[pl.ds(r, 1), :] = row


def sum_class(ref, mem, rep, start, number, both):
    def batch(i, _):
        at = start + i * BATCH
        heads = [rep[at + t] for t in range(BATCH)]
        others = [mem[at + t] for t in range(BATCH)]
        sums = [a + b for a, b in zip(rows_of(ref, heads), rows_of(ref, others))]
        put_rows(ref, heads, sums)
        if both:
            put_rows(ref, others, sums)
        return 0

    lax.fori_loop(0, pl.cdiv(number, BATCH), batch, 0)


def sum_rest(ref, mem, rep, start, number):
    def one(i, _):
        r = rep[start + i]
        ref[pl.ds(r, 1), :] = ref[pl.ds(r, 1), :] + ref[pl.ds(mem[start + i], 1), :]
        return 0

    lax.fori_loop(0, number, one, 0)


def hand_back(ref, mem, rep, start, end):
    def batch(i, _):
        at = start + i * BATCH
        put_rows(ref, [mem[at + t] for t in range(BATCH)], rows_of(ref, [rep[at + t] for t in range(BATCH)]))
        return 0

    lax.fori_loop(0, pl.cdiv(end - start, BATCH), batch, 0)


def finish(modes, u, mass, pairs, inverse, held, shape, c):
    s_n, _, l_n, m_n, e_n = modes.shape
    _, _, nodes_n, _ = shape
    rows_n = nodes_n * e_n
    members, reps, bounds = pairs
    step = min(8, l_n)
    per = l_n // step
    fills = nodes_n // step
    outs = nodes_n // 8

    def kernel(mem, rep, bnd, f_ref, u_ref, mass_ref, inv_ref, _, o_ref, table, stage):
        b = pl.program_id(0)

        @pl.when(b < fills)
        def _():
            for t in range(step):
                node = b * step + t
                rows = f_ref[0, 0, t] + mass_ref[pl.ds(node, 1), :] * u_ref[0, 0, t]
                table[pl.ds(pl.multiple_of(node * e_n, e_n), e_n), :] = rows.T

        @pl.when(b == fills - 1)
        def _():
            table[pl.ds(rows_n, 8), :] = jnp.zeros((8, m_n), jnp.float32)
            for k in range(CLASSES):
                sum_class(table, mem, rep, bnd[2 * k], bnd[2 * k + 1], k == 0)
            sum_rest(table, mem, rep, bnd[2 * CLASSES], bnd[2 * CLASSES + 1])
            hand_back(table, mem, rep, bnd[2], bnd[2 * CLASSES] + bnd[2 * CLASSES + 1])

        @pl.when(b >= fills)
        def _():
            for t in range(8):
                n = (b - fills) * 8 + t
                rows = table[pl.ds(pl.multiple_of(n * e_n, e_n), e_n), :].T
                stage[t] = rows * inv_ref[pl.ds(n, 1), :]
            o_ref[0] = jnp.swapaxes(stage[...], 0, 1)

    smem = pl.BlockSpec(memory_space=pltpu.SMEM)

    def where(channel):
        def index(b):
            b = jnp.minimum(b, fills - 1)
            return (b // per, channel, b % per, 0, 0)

        return index

    nodes = pl.BlockSpec((nodes_n, e_n), lambda b: (0, 0))
    return pl.pallas_call(
        kernel,
        grid=(fills + outs,),
        in_specs=[smem] * 3
        + [
            pl.BlockSpec((1, 1, step, m_n, e_n), where(0)),
            pl.BlockSpec((1, 1, step, m_n, e_n), where(c)),
            nodes,
            nodes,
            pl.BlockSpec(memory_space=pl.ANY),
        ],
        out_specs=pl.BlockSpec((1, m_n, 8, e_n), lambda b: (c, 0, jnp.maximum(b - fills, 0), 0)),
        out_shape=jax.ShapeDtypeStruct(shape, jnp.float32),
        scratch_shapes=[pltpu.VMEM((rows_n + 8, m_n), jnp.float32), pltpu.VMEM((8, m_n, e_n), jnp.float32)],
        input_output_aliases={7: 0},
        compiler_params=params(),
        cost_estimate=pl.CostEstimate(
            flops=rows_n * LANES * 400, bytes_accessed=rows_n * m_n * 12, transcendentals=0
        ),
        name="finish",
    )(members, reps, bounds, modes, u, mass, inverse, held)


def local_sums(modes, u, mass, pairs, edge_reps, first):
    s_n, c_n, l_n, m_n, e_n = modes.shape
    nodes_n = s_n * l_n
    rows_n = nodes_n * e_n
    step = min(8, l_n)
    per = l_n // step
    members, reps, bounds = pairs
    edges_n = edge_reps.shape[1]
    feats = c_n * m_n

    def kernel(mem, rep, bnd, er, f_ref, u_ref, mass_ref, o_ref, low_ref, up_ref):
        b = pl.program_id(0)
        for t in range(step):
            node = b * step + t
            weight = mass_ref[pl.ds(node, 1), :]
            rows = [f_ref[0, c, t] + weight * u_ref[0, c, t] for c in range(c_n)]
            table = jnp.concatenate(rows, axis=0) if c_n > 1 else rows[0]
            o_ref[pl.ds(pl.multiple_of(node * e_n, e_n), e_n), :] = table.T

        @pl.when(b == pl.num_programs(0) - 1)
        def _():
            o_ref[pl.ds(rows_n, 8), :] = jnp.zeros((8, feats), jnp.float32)

            for k in range(CLASSES):
                sum_class(o_ref, mem, rep, bnd[2 * k], bnd[2 * k + 1], False)
            sum_rest(o_ref, mem, rep, bnd[2 * CLASSES], bnd[2 * CLASSES + 1])

            def edge(i, _):
                for side, to in enumerate((low_ref, up_ref)):
                    got = rows_of(o_ref, [er[side, i * BATCH + t] for t in range(BATCH)])
                    put_rows(to, [i * BATCH + t for t in range(BATCH)], got)
                return 0

            lax.fori_loop(0, edges_n // BATCH, edge, 0)

    smem = pl.BlockSpec(memory_space=pltpu.SMEM)
    where = lambda b: (b // per, 0, b % per, 0, 0)
    where_u = lambda b: (b // per, first // c_n, b % per, 0, 0)
    rim = pl.BlockSpec((edges_n, feats), lambda b: (0, 0))
    rim_shape = jax.ShapeDtypeStruct((edges_n, feats), jnp.float32)
    return pl.pallas_call(
        kernel,
        grid=(nodes_n // step,),
        in_specs=[smem] * 4
        + [
            pl.BlockSpec((1, c_n, step, m_n, e_n), where),
            pl.BlockSpec((1, c_n, step, m_n, e_n), where_u),
            pl.BlockSpec((nodes_n, e_n), lambda b: (0, 0)),
        ],
        out_specs=[pl.BlockSpec((rows_n + 8, feats), lambda b: (0, 0)), rim, rim],
        out_shape=[jax.ShapeDtypeStruct((rows_n + 8, feats), jnp.float32), rim_shape, rim_shape],
        compiler_params=params(),
        cost_estimate=pl.CostEstimate(
            flops=rows_n * LANES * 400, bytes_accessed=rows_n * LANES * 12, transcendentals=0
        ),
        name="local_sums",
    )(members, reps, bounds, edge_reps, modes, u, mass)


def spread(table, rims, pairs, edge_reps, inverse, held, shape, first, c_n):
    _, m_n, nodes_n, e_n = shape
    rows_n = nodes_n * e_n
    step = 8
    edges_n = edge_reps.shape[1]
    members, reps, bounds = pairs
    feats = c_n * m_n

    def kernel(mem, rep, bnd, er, t_ref, low_ref, up_ref, inv_ref, *rest):
        o_ref, stage = rest[-2:]
        b = pl.program_id(0)

        @pl.when(b == 0)
        def _():
            def edge(i, _):
                for side, came in enumerate((low_ref, up_ref)):
                    spots = [er[side, i * BATCH + t] for t in range(BATCH)]
                    more = rows_of(came, [i * BATCH + t for t in range(BATCH)])
                    put_rows(t_ref, spots, [a + b for a, b in zip(rows_of(t_ref, spots), more)])
                return 0

            lax.fori_loop(0, edges_n // BATCH, edge, 0)
            hand_back(t_ref, mem, rep, 0, bnd[2 * CLASSES] + bnd[2 * CLASSES + 1])

        for t in range(step):
            n = b * step + t
            rows = t_ref[pl.ds(pl.multiple_of(n * e_n, e_n), e_n), :].T
            scaled = rows * inv_ref[pl.ds(n, 1), :]
            for c in range(c_n):
                stage[c, t] = scaled[c * m_n : (c + 1) * m_n]
        for c in range(c_n):
            o_ref[c] = jnp.swapaxes(stage[c], 0, 1)

    smem = pl.BlockSpec(memory_space=pltpu.SMEM)
    rim = pl.BlockSpec((edges_n, feats), lambda b: (0, 0))
    in_specs = [smem] * 4 + [
        pl.BlockSpec((rows_n + 8, feats), lambda b: (0, 0)),
        rim,
        rim,
        pl.BlockSpec((nodes_n, e_n), lambda b: (0, 0)),
    ]
    args = [members, reps, bounds, edge_reps, table, *rims, inverse]
    aliases = {}
    if held is not None:
        in_specs.append(pl.BlockSpec(memory_space=pl.ANY))
        args.append(held)
        aliases = {len(args) - 1: 0}
    return pl.pallas_call(
        kernel,
        grid=(nodes_n // step,),
        in_specs=in_specs,
        out_specs=pl.BlockSpec((c_n, m_n, step, e_n), lambda b: (first // c_n, 0, b, 0)),
        out_shape=jax.ShapeDtypeStruct(shape, jnp.float32),
        scratch_shapes=[pltpu.VMEM((c_n, step, m_n, e_n), jnp.float32)],
        input_output_aliases=aliases,
        compiler_params=params(),
        cost_estimate=pl.CostEstimate(
            flops=rows_n * LANES * 400, bytes_accessed=rows_n * LANES * 12, transcendentals=0
        ),
        name="spread",
    )(*args)


def fill_up(values, multiple, filler):
    short = -values.shape[-1] % multiple
    pad = [(0, 0)] * (values.ndim - 1) + [(0, short)]
    return jnp.pad(values, pad, constant_values=filler)


def pair_lists(ids, edges):
    rows_n = ids.shape[0]
    place = jnp.arange(rows_n, dtype=jnp.int32)
    ids_sorted, member = lax.sort((ids, place), num_keys=1)
    head = jnp.concatenate([jnp.ones((1,), bool), ids_sorted[1:] != ids_sorted[:-1]])
    last = jnp.concatenate([head[1:], jnp.ones((1,), bool)])
    code = lax.cummax(jnp.where(head, place * rows_n + member, 0))
    rep = code % rows_n
    rank = place - code // rows_n
    group = jnp.where((rank == 1) & last, 0, jnp.minimum(rank, CLASSES))
    group = jnp.where(rank == 0, CLASSES + 1, group).astype(jnp.int32)
    spare = jnp.full((CLASSES * BATCH,), rows_n, jnp.int32)
    spare_group = jnp.arange(CLASSES * BATCH, dtype=jnp.int32) // BATCH
    _, members, reps = lax.sort(
        (
            jnp.concatenate([group, spare_group]),
            jnp.concatenate([member, spare]),
            jnp.concatenate([rep, spare]),
        ),
        num_keys=1,
        is_stable=True,
    )
    pairs_n = rows_n - UNIQUE + CLASSES * BATCH
    numbers = jnp.stack([jnp.sum(group == k, dtype=jnp.int32) for k in range(CLASSES + 1)])
    starts = jnp.cumsum(numbers) - numbers + BATCH * jnp.arange(CLASSES + 1, dtype=jnp.int32)
    bounds = jnp.stack([starts, numbers], axis=1).reshape(-1).astype(jnp.int32)
    more = BATCH + -pairs_n % BATCH
    members = jnp.pad(members[:pairs_n], (0, more), constant_values=rows_n)
    reps = jnp.pad(reps[:pairs_n], (0, more), constant_values=rows_n)
    flat = edges.reshape(-1)
    start = jnp.sum(ids_sorted[None, :] < flat[:, None], axis=1, dtype=jnp.int32)
    edge_reps = fill_up(member[start].reshape(edges.shape), BATCH, rows_n)
    return (members, reps, bounds), edge_reps


def edge_takers(edges, connect_here, edge_reps):
    k_n = edge_reps.shape[1]
    here_n = connect_here.size
    ids = fill_up(edges, BATCH, -1)
    column = jnp.arange(here_n, dtype=jnp.int32)
    same = ids[:, :, None] == connect_here.reshape(-1)
    first = jnp.min(jnp.where(same, column, here_n), axis=2)
    has = (first < here_n).astype(jnp.float32)
    theirs = jnp.stack(swap_edges(has[0], has[1]))
    lost = jnp.max(theirs * (1.0 - has))
    spread_out = lax.pmax(lost, ("mesh", "four")) > 0.5
    at_rep = jnp.where(edge_reps // here_n == lax.axis_index("four"), edge_reps % here_n, -1)
    takers = jnp.where(spread_out, at_rep, jnp.where(first < here_n, first, -1))
    return ids.reshape(2 * k_n, 1), takers.reshape(2 * k_n, 1).astype(jnp.int32), spread_out


def swap_edges(low, up):
    count = lax.axis_size("mesh")
    upward = [(i, (i + 1) % count) for i in range(count)]
    downward = [(j, i) for i, j in upward]
    return lax.ppermute(up, "mesh", upward), lax.ppermute(low, "mesh", downward)


def inverse_mass(mass, ids, edges):
    summed = jnp.zeros((UNIQUE,), jnp.float32).at[ids].add(mass.reshape(-1))
    came = jnp.concatenate(swap_edges(summed[edges[0]], summed[edges[1]]))
    summed = summed.at[edges.reshape(-1)].add(came)
    return (1.0 / summed[ids]).reshape(mass.shape)


def exchange(x):
    return lax.all_to_all(x, "four", split_axis=0, concat_axis=0, tiled=True)


def body(adj_modes, base_flow, geometry, mass, connect, edge_nodes):
    comps, m_n, nodes_n, e_n = adj_modes.shape
    parts = lax.axis_size("four")
    l_n = nodes_n // parts
    mine = lax.axis_index("four") * l_n
    synth, along, analysis = plane_tables(PLANES)
    both_3 = left_form(np.concatenate([synth, along]))
    synth_3, analysis_3 = left_form(synth), left_form(analysis)
    together = lax.optimization_barrier
    spot = lambda n: (n // l_n, n % l_n)
    along_r = [[spot(NP * i + j) for i in range(NP)] for j in range(NP)]
    along_s = [[spot(NP * i + j) for j in range(NP)] for i in range(NP)]
    inside = [[(a, l + j) for j in range(NP)] for a in range(parts) for l in range(0, l_n, NP)]
    whole_rows = l_n % NP == 0

    u_first = adj_modes[0].reshape(m_n, parts, l_n, e_n).transpose(1, 0, 2, 3)
    u_first, adj_modes = together((u_first, adj_modes))
    first_here = exchange(u_first)

    u = node_major(adj_modes, parts)
    ur_a, ur_b = derivative(u, along_r, 0, 2), derivative(u, along_r, 2, 1)
    sent = [u[:, 1:], ur_a] + ([] if whole_rows else [derivative(u, along_s)])
    sent = jnp.concatenate(sent, axis=1)
    sent, u, ur_b, first_here, connect, edge_nodes, mass, base_flow = together(
        (sent, u, ur_b, first_here, connect, edge_nodes, mass, base_flow)
    )

    here = exchange(sent)
    edges = edge_nodes[0]
    ids = connect.reshape(-1)
    pairs, edge_reps = pair_lists(ids, edges)
    inverse = inverse_mass(mass, ids, edges)
    base = base_flow.transpose(0, 2, 1, 3)
    if l_n % 8 == 0:
        u0_here = node_major(first_here, 1).reshape(parts, 1, l_n, m_n, e_n)
    else:
        u0_here = first_here.transpose(0, 2, 1, 3)[:, None]
    us0_here = derivative(u0_here, inside, 0, 1) if whole_rows else None
    mass_here = lax.dynamic_slice_in_dim(mass, mine, l_n, 0)
    connect_here = lax.dynamic_slice_in_dim(connect, mine, l_n, 0)
    edge_ids, takers, spread_out = edge_takers(edges, connect_here, edge_reps)
    held = (here, ur_b, pairs, edge_reps, inverse, base, u0_here, us0_here, edge_ids, takers, spread_out)
    here, ur_b, pairs, edge_reps, inverse, base, u0_here, us0_here, edge_ids, takers, spread_out = together(held)

    ur_b_here = exchange(ur_b)
    us_here = derivative(here, inside, 0, 2) if whole_rows else here[:, 5:7]
    if not whole_rows:
        us0_here = here[:, 4:5]
    geo = lax.dynamic_slice_in_dim(geometry, mine, l_n, 1)
    vr, part = base_products(both_3, synth_3, u0_here, here, us0_here, us_here, base, geo)
    f_a = forcing_modes(synth_3, analysis_3, here, vr, part, mass_here, 2, 0, 2)
    f_a, ur_b_here = together((f_a, ur_b_here))

    modes_a = exchange(f_a)
    f_b, rims = forcing_and_rims(
        synth_3, analysis_3, ur_b_here, here, vr, part, mass_here, connect_here, edge_ids, 2, 1
    )
    half = rims.shape[0] // 2
    rims = jnp.concatenate(swap_edges(rims[:half], rims[half:]))
    rims = lax.cond(spread_out, lambda r: lax.psum(r, "four"), lambda r: r, rims)
    f_b = take_rims(f_b, rims.T, takers)
    f_b, modes_a = together((f_b, modes_a))

    modes_b = exchange(f_b)
    table, *rims = local_sums(modes_a, u, mass, pairs, edge_reps, 0)
    out = spread(table, swap_edges(*rims), pairs, edge_reps, inverse, None, adj_modes.shape, 0, 2)
    modes_b, out = together((modes_b, out))

    return finish(modes_b, u, mass, pairs, inverse, out, adj_modes.shape, 2)


def solution(mesh):
    return jax.shard_map(
        body,
        mesh=mesh,
        in_specs=(
            P(None, "four", None, "mesh"),
            P(None, None, "four", "mesh"),
            P(None, None, "mesh"),
            P(None, "mesh"),
            P(None, "mesh"),
            P("mesh", None, None),
        ),
        out_specs=P(None, "four", None, "mesh"),
        check_vma=False,
    )
```

```python
import math

import jax
import jax.numpy as jnp
import ml_dtypes
import numpy as np
from jax import lax
from jax.experimental import pallas as pl
from jax.experimental.pallas import tpu as pltpu
from jax.sharding import PartitionSpec as P

NP = 8
PLANES = 256
UNIQUE = 12825
STEP_SIZE = 0.1
LANES = 128
BATCH = 16
CLASSES = 4
VMEM_LIMIT = 56 * 1024 * 1024


def legendre_values(degree, point):
    before = 1.0
    current = point
    for order in range(1, degree):
        after = ((2 * order + 1) * point * current - order * before) / (order + 1)
        before = current
        current = after
    return (current, before)


def gll_derivative(points_n):
    degree = points_n - 1
    points = []
    for index in range(points_n):
        point = -math.cos(math.pi * index / degree)
        for sweep in range(100):
            top_val, below_val = legendre_values(degree, point)
            point = point - (point * top_val - below_val) / (points_n * top_val)
        points.append(point)
    values = [legendre_values(degree, point)[0] for point in points]
    deriv_rows = []
    for row_index in range(points_n):
        row_vals = []
        for col_index in range(points_n):
            if row_index != col_index:
                row_vals.append(
                    values[row_index]
                    / (values[col_index] * (points[row_index] - points[col_index]))
                )
            else:
                row_vals.append(0.0)
        deriv_rows.append(row_vals)
    deriv_rows[0][0] = -degree * (degree + 1) / 4.0
    deriv_rows[degree][degree] = degree * (degree + 1) / 4.0
    return deriv_rows


def plane_tables(planes):
    plane = np.arange(planes)
    wave = plane // 2
    phase = ((plane[:, None] * wave[None, :]) % planes) * (2.0 * math.pi / planes)
    synth = np.where((plane % 2 == 1)[None, :], np.sin(phase), np.cos(phase))
    synth[:, 1] = 1 - 2 * (plane % 2)
    scales = np.where(wave == 0, 1.0 / planes, 2.0 / planes)
    analysis = synth.T * scales[:, None]
    number = wave * (2.0 / planes)
    along = np.zeros_like(synth)
    along[:, 1::2] = number[1::2] * synth[:, 0::2]
    along[:, 0::2] = -number[0::2] * synth[:, 1::2]
    along[:, :2] = 0.0
    return tuple(t.astype(np.float32) for t in (synth, along, analysis))


def params(**kw):
    return pltpu.CompilerParams(vmem_limit_bytes=VMEM_LIMIT, **kw)


def slabs(x, parts):
    _, m_n, n_n, e_n = x.shape
    l_n = n_n // parts
    if l_n % 8:
        return x[0].reshape(m_n, parts, l_n, e_n).transpose(1, 0, 2, 3)

    def kernel(x_ref, o_ref, sems):
        copies = [
            pltpu.make_async_copy(x_ref.at[0, :, pl.ds(q * l_n, l_n), :], o_ref.at[q], sems.at[q])
            for q in range(parts)
        ]
        for copy in copies:
            copy.start()
        for copy in copies:
            copy.wait()

    return pl.pallas_call(
        kernel,
        in_specs=[pl.BlockSpec(memory_space=pl.ANY)],
        out_specs=pl.BlockSpec(memory_space=pl.ANY),
        out_shape=jax.ShapeDtypeStruct((parts, m_n, l_n, e_n), jnp.float32),
        scratch_shapes=[pltpu.SemaphoreType.DMA((parts,))],
        compiler_params=params(),
        cost_estimate=pl.CostEstimate(flops=0, bytes_accessed=8 * m_n * n_n * e_n, transcendentals=0),
        name="slabs",
    )(x)


def node_major(x, parts):
    c_n, m_n, n_n, e_n = x.shape
    l_n = n_n // parts
    rows = 16

    def kernel(x_ref, o_ref):
        for n in range(0, n_n, 8):
            turned = jnp.swapaxes(x_ref[0, :, n : n + 8, :], 0, 1)
            for t in range(8):
                o_ref[(n + t) // l_n, 0, (n + t) % l_n] = turned[t]

    return pl.pallas_call(
        kernel,
        grid=(c_n, m_n // rows),
        in_specs=[pl.BlockSpec((1, rows, n_n, e_n), lambda c, m: (c, m, 0, 0))],
        out_specs=pl.BlockSpec((parts, 1, l_n, rows, e_n), lambda c, m: (0, c, 0, m, 0)),
        out_shape=jax.ShapeDtypeStruct((parts, c_n, l_n, m_n, e_n), jnp.float32),
        compiler_params=params(),
        cost_estimate=pl.CostEstimate(flops=x.size, bytes_accessed=8 * x.size, transcendentals=0),
        name="node_major",
    )(x)


def derivative(x, groups, first=0, c_n=3):
    a_n, _, l_n, m_n, e_n = x.shape
    deriv = gll_derivative(NP)
    rows = 8

    def kernel(x_ref, o_ref):
        for line in groups:
            vals = [x_ref[a, 0, l] for a, l in line]
            for i, (a, l) in enumerate(line):
                total = deriv[i][0] * vals[0]
                for k in range(1, NP):
                    if deriv[i][k] != 0.0:
                        total = total + deriv[i][k] * vals[k]
                o_ref[a, 0, l] = total

    block = (a_n, 1, l_n, rows, e_n)
    size = a_n * c_n * l_n * m_n * e_n
    return pl.pallas_call(
        kernel,
        grid=(c_n, m_n // rows),
        in_specs=[pl.BlockSpec(block, lambda c, m: (0, first + c, 0, m, 0))],
        out_specs=pl.BlockSpec(block, lambda c, m: (0, c, 0, m, 0)),
        out_shape=jax.ShapeDtypeStruct((a_n, c_n, l_n, m_n, e_n), jnp.float32),
        compiler_params=params(),
        cost_estimate=pl.CostEstimate(flops=16 * size, bytes_accessed=8 * size, transcendentals=0),
        name="line_derivative",
    )(x)


def split(x):
    high = x.astype(jnp.bfloat16)
    return high, (x - high.astype(jnp.float32)).astype(jnp.bfloat16)


def left_form(table):
    high = table.astype(ml_dtypes.bfloat16)
    low = (table - high.astype(np.float32)).astype(ml_dtypes.bfloat16)
    return jnp.asarray(np.concatenate([high, high, low], axis=1))


def right_form(x):
    high, low = split(x)
    return jnp.concatenate([high, low, high], axis=0)


def product(left, right):
    return jnp.dot(left, right, preferred_element_type=jnp.float32)


def base_products(synth_along, synth, u_a, u_b, us_a, us_b, base, geo):
    s_n, _, l_n, m_n, e_n = u_a.shape
    p_n = base.shape[2]

    def kernel(both_ref, synth_ref, ua_ref, ub_ref, usa_ref, usb_ref, b_ref, g_ref, vr_ref, part_ref):
        l = pl.program_id(0)
        field = lambda i: b_ref[i, 0].astype(jnp.float32)
        g = [g_ref[i, pl.ds(l, 1), :] for i in range(4)]
        ux, uy = field(0), field(1)
        vr_ref[0] = ux * g[0] + uy * g[2]
        vs = ux * g[1] + uy * g[3]
        uz = field(2)
        phys = []
        for c in range(3):
            u_c = ua_ref[:, 0, 0] if c == 0 else ub_ref[:, c - 1, 0]
            us_c = usa_ref[:, 0, 0] if c == 0 else usb_ref[:, c - 1, 0]
            both = product(both_ref[...], right_form(u_c.reshape(s_n * m_n, e_n)))
            phys.append(both[:p_n])
            ds = product(synth_ref[...], right_form(us_c.reshape(s_n * m_n, e_n)))
            part_ref[c, 0] = -(vs * ds) - uz * both[p_n:]
        for c in range(3):
            part_ref[c, 0] += phys[0] * field(3 + 3 * c) + phys[1] * field(4 + 3 * c) + phys[2] * field(5 + 3 * c)

    one = pl.BlockSpec((s_n, 1, 1, m_n, e_n), lambda l: (0, 0, l, 0, 0))
    two = pl.BlockSpec((s_n, 2, 1, m_n, e_n), lambda l: (0, 0, l, 0, 0))
    return pl.pallas_call(
        kernel,
        grid=(l_n,),
        in_specs=[
            pl.BlockSpec((2 * p_n, 3 * p_n), lambda l: (0, 0)),
            pl.BlockSpec((p_n, 3 * p_n), lambda l: (0, 0)),
            one,
            two,
            one,
            two,
            pl.BlockSpec((12, 1, p_n, e_n), lambda l: (0, l, 0, 0)),
            pl.BlockSpec((4, l_n, e_n), lambda l: (0, 0, 0)),
        ],
        out_specs=[
            pl.BlockSpec((1, p_n, e_n), lambda l: (l, 0, 0)),
            pl.BlockSpec((3, 1, p_n, e_n), lambda l: (0, l, 0, 0)),
        ],
        out_shape=[
            jax.ShapeDtypeStruct((l_n, p_n, e_n), jnp.float32),
            jax.ShapeDtypeStruct((3, l_n, p_n, e_n), jnp.float32),
        ],
        compiler_params=params(),
        cost_estimate=pl.CostEstimate(
            flops=9 * 2 * 3 * l_n * p_n * p_n * e_n, bytes_accessed=l_n * p_n * e_n * 64, transcendentals=0
        ),
        name="base_products",
    )(synth_along, synth, u_a, u_b, us_a, us_b, base, geo)


def forcing_modes(synth, analysis, ur, vr, part, mass, held_at, first, c_n):
    s_n, _, l_n, m_n, e_n = ur.shape
    p_n = vr.shape[1]

    def kernel(synth_ref, analysis_ref, ur_ref, vr_ref, part_ref, mass_ref, o_ref):
        l = pl.program_id(1)
        dr = product(synth_ref[...], right_form(ur_ref[:, 0, 0].reshape(s_n * m_n, e_n)))
        forcing = part_ref[0, 0] - vr_ref[0] * dr
        modes = product(analysis_ref[...], right_form(forcing)) * (STEP_SIZE * mass_ref[pl.ds(l, 1), :])
        o_ref[:, 0, 0] = modes.reshape(s_n, m_n, e_n)

    whole = pl.BlockSpec((p_n, 3 * p_n), lambda c, l: (0, 0))
    block = (s_n, 1, 1, m_n, e_n)
    return pl.pallas_call(
        kernel,
        grid=(c_n, l_n),
        in_specs=[
            whole,
            whole,
            pl.BlockSpec(block, lambda c, l: (0, held_at + c, l, 0, 0)),
            pl.BlockSpec((1, p_n, e_n), lambda c, l: (l, 0, 0)),
            pl.BlockSpec((1, 1, p_n, e_n), lambda c, l: (first + c, l, 0, 0)),
            pl.BlockSpec((l_n, e_n), lambda c, l: (0, 0)),
        ],
        out_specs=pl.BlockSpec(block, lambda c, l: (0, c, l, 0, 0)),
        out_shape=jax.ShapeDtypeStruct((s_n, c_n, l_n, m_n, e_n), jnp.float32),
        compiler_params=params(),
        cost_estimate=pl.CostEstimate(
            flops=2 * 2 * 3 * c_n * l_n * p_n * p_n * e_n,
            bytes_accessed=c_n * l_n * p_n * e_n * 16,
            transcendentals=0,
        ),
        name="forcing_modes",
    )(synth, analysis, ur, vr, part, mass)


def forcing_and_rims(synth, analysis, ur, u, vr, part, mass, connect, edge_ids, c, u_at):
    s_n, _, l_n, m_n, e_n = ur.shape
    p_n = vr.shape[1]
    k_n = edge_ids.shape[0]

    def kernel(synth_ref, analysis_ref, ur_ref, u_ref, vr_ref, part_ref, mass_ref, conn_ref, id_ref, o_ref, rim_ref):
        l = pl.program_id(0)
        dr = product(synth_ref[...], right_form(ur_ref[:, 0, 0].reshape(s_n * m_n, e_n)))
        forcing = part_ref[0, 0] - vr_ref[0] * dr
        weight = mass_ref[pl.ds(l, 1), :]
        modes = product(analysis_ref[...], right_form(forcing)) * (STEP_SIZE * weight)
        o_ref[:, 0, 0] = modes.reshape(s_n, m_n, e_n)
        high, low = split(modes + weight * u_ref[:, 0, 0].reshape(s_n * m_n, e_n))
        here = jnp.where(id_ref[...] == conn_ref[pl.ds(l, 1), :], 1.0, 0.0).astype(jnp.bfloat16)
        sums = lax.dot_general(
            jnp.concatenate([here, here], axis=1),
            jnp.concatenate([high, low], axis=1),
            (((1,), (1,)), ((), ())),
            preferred_element_type=jnp.float32,
        )

        @pl.when(l == 0)
        def _():
            rim_ref[...] = sums

        @pl.when(l > 0)
        def _():
            rim_ref[...] += sums

    whole = pl.BlockSpec((p_n, 3 * p_n), lambda l: (0, 0))
    block = (s_n, 1, 1, m_n, e_n)
    nodes = pl.BlockSpec((l_n, e_n), lambda l: (0, 0))
    return pl.pallas_call(
        kernel,
        grid=(l_n,),
        in_specs=[
            whole,
            whole,
            pl.BlockSpec(block, lambda l: (0, 0, l, 0, 0)),
            pl.BlockSpec(block, lambda l: (0, u_at, l, 0, 0)),
            pl.BlockSpec((1, p_n, e_n), lambda l: (l, 0, 0)),
            pl.BlockSpec((1, 1, p_n, e_n), lambda l: (c, l, 0, 0)),
            nodes,
            nodes,
            pl.BlockSpec((k_n, 1), lambda l: (0, 0)),
        ],
        out_specs=[
            pl.BlockSpec(block, lambda l: (0, 0, l, 0, 0)),
            pl.BlockSpec((k_n, s_n * m_n), lambda l: (0, 0)),
        ],
        out_shape=[
            jax.ShapeDtypeStruct((s_n, 1, l_n, m_n, e_n), jnp.float32),
            jax.ShapeDtypeStruct((k_n, s_n * m_n), jnp.float32),
        ],
        compiler_params=params(),
        cost_estimate=pl.CostEstimate(
            flops=4 * 2 * 3 * l_n * p_n * p_n * e_n, bytes_accessed=l_n * p_n * e_n * 20, transcendentals=0
        ),
        name="forcing_and_rims",
    )(synth, analysis, ur, u, vr, part, mass, connect, edge_ids)


def own_sums(modes, u, mass, connect, rims, edge_ids, u_at):
    s_n, _, l_n, m_n, e_n = modes.shape
    k_n = edge_ids.shape[0]
    coefs = s_n * m_n

    def kernel(f_ref, u_ref, mass_ref, conn_ref, turned_ref, rim_ref, id_ref, o_ref, held):
        l = pl.program_id(0)

        @pl.when(l == 0)
        def _():
            for k in range(l_n):
                weighted = f_ref[:, 0, k] + mass_ref[k : k + 1, :] * u_ref[:, 0, k]
                high, low = split(weighted.reshape(coefs, e_n))
                held[k] = jnp.concatenate([high, low], axis=1)

        mine = conn_ref[pl.ds(l, 1), :]

        def same(ids):
            there = jnp.where(ids == mine, 1.0, 0.0).astype(jnp.bfloat16)
            return jnp.concatenate([there, there], axis=0)

        high, low = split(rim_ref[...])
        total = product(jnp.concatenate([high, low], axis=1), same(id_ref[...]))
        for k in range(l_n):
            total = total + product(held[k], same(turned_ref[k]))
        o_ref[:, 0, 0] = total.reshape(s_n, m_n, e_n)

    def whole(*shape):
        return pl.BlockSpec(shape, lambda l: (0,) * len(shape))

    return pl.pallas_call(
        kernel,
        grid=(l_n,),
        in_specs=[
            whole(s_n, 1, l_n, m_n, e_n),
            pl.BlockSpec((s_n, 1, l_n, m_n, e_n), lambda l: (0, u_at, 0, 0, 0)),
            whole(l_n, e_n),
            whole(l_n, e_n),
            whole(l_n, e_n, 1),
            whole(coefs, k_n),
            whole(k_n, 1),
        ],
        out_specs=pl.BlockSpec((s_n, 1, 1, m_n, e_n), lambda l: (0, 0, l, 0, 0)),
        out_shape=jax.ShapeDtypeStruct(modes.shape, jnp.float32),
        scratch_shapes=[pltpu.VMEM((l_n, coefs, 2 * e_n), jnp.bfloat16)],
        compiler_params=params(),
        cost_estimate=pl.CostEstimate(
            flops=4 * l_n * l_n * coefs * e_n * e_n, bytes_accessed=12 * modes.size, transcendentals=0
        ),
        name="own_sums",
    )(modes, u, mass, connect, connect[:, :, None], rims, edge_ids)


def rows_of(ref, places):
    return [ref[pl.ds(r, 1), :] for r in places]


def put_rows(ref, places, rows):
    for r, row in zip(places, rows):
        ref[pl.ds(r, 1), :] = row


def sum_class(ref, mem, rep, start, number, both):
    def batch(i, _):
        at = start + i * BATCH
        heads = [rep[at + t] for t in range(BATCH)]
        others = [mem[at + t] for t in range(BATCH)]
        sums = [a + b for a, b in zip(rows_of(ref, heads), rows_of(ref, others))]
        put_rows(ref, heads, sums)
        if both:
            put_rows(ref, others, sums)
        return 0

    lax.fori_loop(0, pl.cdiv(number, BATCH), batch, 0)


def sum_rest(ref, mem, rep, start, number):
    def one(i, _):
        r = rep[start + i]
        ref[pl.ds(r, 1), :] = ref[pl.ds(r, 1), :] + ref[pl.ds(mem[start + i], 1), :]
        return 0

    lax.fori_loop(0, number, one, 0)


def hand_back(ref, mem, rep, start, end):
    def batch(i, _):
        at = start + i * BATCH
        put_rows(ref, [mem[at + t] for t in range(BATCH)], rows_of(ref, [rep[at + t] for t in range(BATCH)]))
        return 0

    lax.fori_loop(0, pl.cdiv(end - start, BATCH), batch, 0)


def finish(sums, pairs, inverse, held, shape, c):
    s_n, _, l_n, m_n, e_n = sums.shape
    _, _, nodes_n, _ = shape
    rows_n = nodes_n * e_n
    members, reps, bounds = pairs
    step = max(8, l_n)
    outs = nodes_n // step

    def kernel(mem, rep, bnd, f_ref, inv_ref, _, o_ref, table, stage):
        b = pl.program_id(0)

        @pl.when(b < s_n)
        def _():
            for t in range(l_n):
                node = b * l_n + t
                table[pl.ds(pl.multiple_of(node * e_n, e_n), e_n), :] = f_ref[0, 0, t].T

        @pl.when(b == s_n - 1)
        def _():
            table[pl.ds(rows_n, 8), :] = jnp.zeros((8, m_n), jnp.float32)
            for k in range(CLASSES):
                sum_class(table, mem, rep, bnd[2 * k], bnd[2 * k + 1], k == 0)
            sum_rest(table, mem, rep, bnd[2 * CLASSES], bnd[2 * CLASSES + 1])
            hand_back(table, mem, rep, bnd[2], bnd[2 * CLASSES + 2] + bnd[2 * CLASSES + 3])

        @pl.when(b >= s_n)
        def _():
            for t in range(step):
                n = (b - s_n) * step + t
                rows = table[pl.ds(pl.multiple_of(n * e_n, e_n), e_n), :].T
                stage[t] = rows * inv_ref[pl.ds(n, 1), :]
            o_ref[0] = jnp.swapaxes(stage[...], 0, 1)

    smem = pl.BlockSpec(memory_space=pltpu.SMEM)
    return pl.pallas_call(
        kernel,
        grid=(s_n + outs,),
        in_specs=[smem] * 3
        + [
            pl.BlockSpec((1, 1, l_n, m_n, e_n), lambda b: (jnp.minimum(b, s_n - 1), 0, 0, 0, 0)),
            pl.BlockSpec((nodes_n, e_n), lambda b: (0, 0)),
            pl.BlockSpec(memory_space=pl.ANY),
        ],
        out_specs=pl.BlockSpec((1, m_n, step, e_n), lambda b: (c, 0, jnp.maximum(b - s_n, 0), 0)),
        out_shape=jax.ShapeDtypeStruct(shape, jnp.float32),
        scratch_shapes=[pltpu.VMEM((rows_n + 8, m_n), jnp.float32), pltpu.VMEM((step, m_n, e_n), jnp.float32)],
        input_output_aliases={5: 0},
        compiler_params=params(),
        cost_estimate=pl.CostEstimate(
            flops=rows_n * LANES * 400, bytes_accessed=rows_n * m_n * 12, transcendentals=0
        ),
        name="finish",
    )(members, reps, bounds, sums, inverse, held)


def local_sums(modes, u, mass, pairs, edge_reps, first):
    s_n, c_n, l_n, m_n, e_n = modes.shape
    nodes_n = s_n * l_n
    rows_n = nodes_n * e_n
    step = min(8, l_n)
    per = l_n // step
    members, reps, bounds = pairs
    edges_n = edge_reps.shape[1]
    feats = c_n * m_n

    def kernel(mem, rep, bnd, er, f_ref, u_ref, mass_ref, o_ref, low_ref, up_ref):
        b = pl.program_id(0)
        for t in range(step):
            node = b * step + t
            weight = mass_ref[pl.ds(node, 1), :]
            rows = [f_ref[0, c, t] + weight * u_ref[0, c, t] for c in range(c_n)]
            table = jnp.concatenate(rows, axis=0) if c_n > 1 else rows[0]
            o_ref[pl.ds(pl.multiple_of(node * e_n, e_n), e_n), :] = table.T

        @pl.when(b == pl.num_programs(0) - 1)
        def _():
            o_ref[pl.ds(rows_n, 8), :] = jnp.zeros((8, feats), jnp.float32)

            for k in range(CLASSES):
                sum_class(o_ref, mem, rep, bnd[2 * k], bnd[2 * k + 1], False)
            sum_rest(o_ref, mem, rep, bnd[2 * CLASSES], bnd[2 * CLASSES + 1])

            def edge(i, _):
                for side, to in enumerate((low_ref, up_ref)):
                    got = rows_of(o_ref, [er[side, i * BATCH + t] for t in range(BATCH)])
                    put_rows(to, [i * BATCH + t for t in range(BATCH)], got)
                return 0

            lax.fori_loop(0, edges_n // BATCH, edge, 0)

    smem = pl.BlockSpec(memory_space=pltpu.SMEM)
    where = lambda b: (b // per, 0, b % per, 0, 0)
    where_u = lambda b: (b // per, first // c_n, b % per, 0, 0)
    rim = pl.BlockSpec((edges_n, feats), lambda b: (0, 0))
    rim_shape = jax.ShapeDtypeStruct((edges_n, feats), jnp.float32)
    return pl.pallas_call(
        kernel,
        grid=(nodes_n // step,),
        in_specs=[smem] * 4
        + [
            pl.BlockSpec((1, c_n, step, m_n, e_n), where),
            pl.BlockSpec((1, c_n, step, m_n, e_n), where_u),
            pl.BlockSpec((nodes_n, e_n), lambda b: (0, 0)),
        ],
        out_specs=[pl.BlockSpec((rows_n + 8, feats), lambda b: (0, 0)), rim, rim],
        out_shape=[jax.ShapeDtypeStruct((rows_n + 8, feats), jnp.float32), rim_shape, rim_shape],
        compiler_params=params(),
        cost_estimate=pl.CostEstimate(
            flops=rows_n * LANES * 400, bytes_accessed=rows_n * LANES * 12, transcendentals=0
        ),
        name="local_sums",
    )(members, reps, bounds, edge_reps, modes, u, mass)


def spread(table, rims, pairs, edge_reps, inverse, held, shape, first, c_n):
    _, m_n, nodes_n, e_n = shape
    rows_n = nodes_n * e_n
    step = 8
    edges_n = edge_reps.shape[1]
    members, reps, bounds = pairs
    feats = c_n * m_n

    def kernel(mem, rep, bnd, er, t_ref, low_ref, up_ref, inv_ref, *rest):
        o_ref, stage = rest[-2:]
        b = pl.program_id(0)

        @pl.when(b == 0)
        def _():
            def edge(i, _):
                for side, came in enumerate((low_ref, up_ref)):
                    spots = [er[side, i * BATCH + t] for t in range(BATCH)]
                    more = rows_of(came, [i * BATCH + t for t in range(BATCH)])
                    put_rows(t_ref, spots, [a + b for a, b in zip(rows_of(t_ref, spots), more)])
                return 0

            lax.fori_loop(0, edges_n // BATCH, edge, 0)
            hand_back(t_ref, mem, rep, 0, bnd[2 * CLASSES] + bnd[2 * CLASSES + 1])

        for t in range(step):
            n = b * step + t
            rows = t_ref[pl.ds(pl.multiple_of(n * e_n, e_n), e_n), :].T
            scaled = rows * inv_ref[pl.ds(n, 1), :]
            for c in range(c_n):
                stage[c, t] = scaled[c * m_n : (c + 1) * m_n]
        for c in range(c_n):
            o_ref[c] = jnp.swapaxes(stage[c], 0, 1)

    smem = pl.BlockSpec(memory_space=pltpu.SMEM)
    rim = pl.BlockSpec((edges_n, feats), lambda b: (0, 0))
    in_specs = [smem] * 4 + [
        pl.BlockSpec((rows_n + 8, feats), lambda b: (0, 0)),
        rim,
        rim,
        pl.BlockSpec((nodes_n, e_n), lambda b: (0, 0)),
    ]
    args = [members, reps, bounds, edge_reps, table, *rims, inverse]
    aliases = {}
    if held is not None:
        in_specs.append(pl.BlockSpec(memory_space=pl.ANY))
        args.append(held)
        aliases = {len(args) - 1: 0}
    return pl.pallas_call(
        kernel,
        grid=(nodes_n // step,),
        in_specs=in_specs,
        out_specs=pl.BlockSpec((c_n, m_n, step, e_n), lambda b: (first // c_n, 0, b, 0)),
        out_shape=jax.ShapeDtypeStruct(shape, jnp.float32),
        scratch_shapes=[pltpu.VMEM((c_n, step, m_n, e_n), jnp.float32)],
        input_output_aliases=aliases,
        compiler_params=params(),
        cost_estimate=pl.CostEstimate(
            flops=rows_n * LANES * 400, bytes_accessed=rows_n * LANES * 12, transcendentals=0
        ),
        name="spread",
    )(*args)


def fill_up(values, multiple, filler):
    short = -values.shape[-1] % multiple
    pad = [(0, 0)] * (values.ndim - 1) + [(0, short)]
    return jnp.pad(values, pad, constant_values=filler)


def grouped(group, classes, member, rep, pairs_n):
    rows_n = group.shape[0]
    spare = jnp.full((CLASSES * BATCH,), rows_n, jnp.int32)
    spare_group = jnp.arange(CLASSES * BATCH, dtype=jnp.int32) // BATCH
    _, members, reps = lax.sort(
        (
            jnp.concatenate([group.astype(jnp.int32), spare_group]),
            jnp.concatenate([member, spare]),
            jnp.concatenate([rep, spare]),
        ),
        num_keys=1,
        is_stable=True,
    )
    spares = BATCH * jnp.minimum(jnp.arange(classes, dtype=jnp.int32), CLASSES)
    numbers = jnp.stack([jnp.sum(group == k, dtype=jnp.int32) for k in range(classes)])
    starts = jnp.cumsum(numbers) - numbers + spares
    bounds = jnp.stack([starts, numbers], axis=1).reshape(-1).astype(jnp.int32)
    length = pairs_n + CLASSES * BATCH
    more = BATCH + -length % BATCH
    members = jnp.pad(members[:length], (0, more), constant_values=rows_n)
    reps = jnp.pad(reps[:length], (0, more), constant_values=rows_n)
    return members, reps, bounds


def pair_lists(ids, edges, parts):
    rows_n = ids.shape[0]
    place = jnp.arange(rows_n, dtype=jnp.int32)
    ids_sorted, member = lax.sort((ids, place), num_keys=1, is_stable=True)
    yes = jnp.ones((1,), bool)
    head = jnp.concatenate([yes, ids_sorted[1:] != ids_sorted[:-1]])
    last = jnp.concatenate([head[1:], yes])
    code = lax.cummax(jnp.where(head, place * rows_n + member, 0))
    rep = code % rows_n
    rank = place - code // rows_n
    pairs_n = rows_n - UNIQUE
    group = jnp.where((rank == 1) & last, 0, jnp.minimum(rank, CLASSES))
    group = jnp.where(rank == 0, CLASSES + 1, group)
    pairs = grouped(group, CLASSES + 1, member, rep, pairs_n)

    device = member // (rows_n // parts)
    device_first = head | jnp.concatenate([yes, device[1:] != device[:-1]])
    device_no = lax.cumsum(device_first.astype(jnp.int32))
    device_rank = device_no - lax.cummax(jnp.where(head, device_no, 0))
    most = lax.cummax(jnp.where(last, (rows_n - place) * parts + device_rank, 0), reverse=True) % parts
    group = jnp.where(device_first, jnp.minimum(device_rank, CLASSES), CLASSES + 1)
    group = jnp.where((rank == 1) & last & (device_rank == 1), 0, group)
    group = jnp.where((rank == 0) | (most == 0), CLASSES + 2, group)
    across = grouped(group, CLASSES + 2, member, rep, pairs_n)

    flat = edges.reshape(-1)
    start = jnp.sum(ids_sorted[None, :] < flat[:, None], axis=1, dtype=jnp.int32)
    edge_reps = fill_up(member[start].reshape(edges.shape), BATCH, rows_n)
    return pairs, across, edge_reps


def shifted(x, axis, step):
    count = lax.axis_size(axis)
    return lax.ppermute(x, axis, [(i, (i + step) % count) for i in range(count)])


def largest(x):
    for axis in ("mesh", "four"):
        step = 1
        while step < lax.axis_size(axis):
            x = jnp.maximum(x, shifted(x, axis, step))
            step *= 2
    return x


def total_over_four(x):
    total = x
    for step in range(1, lax.axis_size("four")):
        total = total + shifted(x, "four", step)
    return total


def swap_edges(low, up):
    return shifted(up, "mesh", 1), shifted(low, "mesh", -1)


def edge_takers(edges, connect_here, edge_reps):
    here_n = connect_here.size
    ids = fill_up(edges, BATCH, -1)
    has = jnp.any(ids[:, :, None] == connect_here.reshape(-1), axis=2).astype(jnp.float32)
    theirs = jnp.stack(swap_edges(has[0], has[1]))
    spread_out = largest(jnp.max(theirs * (1.0 - has)).reshape(1))[0] > 0.5
    at_rep = jnp.where(edge_reps // here_n == lax.axis_index("four"), ids, -1)
    taken = jnp.where(spread_out, at_rep, ids)
    return ids.reshape(-1, 1), taken.reshape(-1, 1), spread_out


def inverse_mass(mass, ids, edges):
    summed = jnp.zeros((UNIQUE,), jnp.float32).at[ids].add(mass.reshape(-1))
    came = jnp.concatenate(swap_edges(summed[edges[0]], summed[edges[1]]))
    summed = summed.at[edges.reshape(-1)].add(came)
    return (1.0 / summed[ids]).reshape(mass.shape)


def exchange(x):
    return lax.all_to_all(x, "four", split_axis=0, concat_axis=0, tiled=True)


def body(adj_modes, base_flow, geometry, mass, connect, edge_nodes):
    comps, m_n, nodes_n, e_n = adj_modes.shape
    parts = lax.axis_size("four")
    l_n = nodes_n // parts
    mine = lax.axis_index("four") * l_n
    synth, along, analysis = plane_tables(PLANES)
    both_3 = left_form(np.concatenate([synth, along]))
    synth_3, analysis_3 = left_form(synth), left_form(analysis)
    together = lax.optimization_barrier
    spot = lambda n: (n // l_n, n % l_n)
    along_r = [[spot(NP * i + j) for i in range(NP)] for j in range(NP)]
    along_s = [[spot(NP * i + j) for j in range(NP)] for i in range(NP)]
    inside = [[(a, l + j) for j in range(NP)] for a in range(parts) for l in range(0, l_n, NP)]
    whole_rows = l_n % NP == 0

    u_first = slabs(adj_modes, parts)
    u_first, adj_modes = together((u_first, adj_modes))
    first_here = exchange(u_first)

    u = node_major(adj_modes, parts)
    ur_a, ur_b = derivative(u, along_r, 0, 2), derivative(u, along_r, 2, 1)
    sent = [u[:, 1:], ur_a] + ([] if whole_rows else [derivative(u, along_s)])
    sent = jnp.concatenate(sent, axis=1)
    sent, u, ur_b, first_here, connect, edge_nodes, mass, base_flow = together(
        (sent, u, ur_b, first_here, connect, edge_nodes, mass, base_flow)
    )

    here = exchange(sent)
    edges = edge_nodes[0]
    ids = connect.reshape(-1)
    pairs, across, edge_reps = pair_lists(ids, edges, parts)
    inverse = inverse_mass(mass, ids, edges)
    base = base_flow.transpose(0, 2, 1, 3)
    if l_n % 8 == 0:
        u0_here = node_major(first_here, 1).reshape(parts, 1, l_n, m_n, e_n)
    else:
        u0_here = first_here.transpose(0, 2, 1, 3)[:, None]
    us0_here = derivative(u0_here, inside, 0, 1) if whole_rows else None
    mass_here = lax.dynamic_slice_in_dim(mass, mine, l_n, 0)
    connect_here = lax.dynamic_slice_in_dim(connect, mine, l_n, 0)
    edge_ids, taken_ids, spread_out = edge_takers(edges, connect_here, edge_reps)
    held = (here, ur_b, pairs, across, edge_reps, inverse, base, u0_here, us0_here, edge_ids, taken_ids, spread_out)
    here, ur_b, pairs, across, edge_reps, inverse, base, u0_here, us0_here, edge_ids, taken_ids, spread_out = together(held)

    ur_b_here = exchange(ur_b)
    us_here = derivative(here, inside, 0, 2) if whole_rows else here[:, 5:7]
    if not whole_rows:
        us0_here = here[:, 4:5]
    geo = lax.dynamic_slice_in_dim(geometry, mine, l_n, 1)
    vr, part = base_products(both_3, synth_3, u0_here, here, us0_here, us_here, base, geo)
    f_a = forcing_modes(synth_3, analysis_3, here, vr, part, mass_here, 2, 0, 2)
    f_a, ur_b_here = together((f_a, ur_b_here))

    modes_a = exchange(f_a)
    f_b, rims = forcing_and_rims(
        synth_3, analysis_3, ur_b_here, here, vr, part, mass_here, connect_here, edge_ids, 2, 1
    )
    half = rims.shape[0] // 2
    rims = jnp.concatenate(swap_edges(rims[:half], rims[half:]))
    rims = lax.cond(spread_out, total_over_four, lambda r: r, rims)
    f_b = own_sums(f_b, here, mass_here, connect_here, rims.T, taken_ids, 1)
    f_b, modes_a = together((f_b, modes_a))

    modes_b = exchange(f_b)
    table, *rims = local_sums(modes_a, u, mass, pairs, edge_reps, 0)
    out = spread(table, swap_edges(*rims), pairs, edge_reps, inverse, None, adj_modes.shape, 0, 2)
    modes_b, out = together((modes_b, out))

    return finish(modes_b, across, inverse, out, adj_modes.shape, 2)


def solution(mesh):
    return jax.shard_map(
        body,
        mesh=mesh,
        in_specs=(
            P(None, "four", None, "mesh"),
            P(None, None, "four", "mesh"),
            P(None, None, "mesh"),
            P(None, "mesh"),
            P(None, "mesh"),
            P("mesh", None, None),
        ),
        out_specs=P(None, "four", None, "mesh"),
        check_vma=False,
    )
```

```python
import math

import jax
import jax.numpy as jnp
import ml_dtypes
import numpy as np
from jax import lax
from jax.experimental import pallas as pl
from jax.experimental.pallas import tpu as pltpu
from jax.sharding import PartitionSpec as P

NP = 8
PLANES = 256
UNIQUE = 12825
STEP_SIZE = 0.1
LANES = 128
BATCH = 16
CLASSES = 4
PACK = 15
VMEM_LIMIT = 56 * 1024 * 1024


def legendre_values(degree, point):
    before = 1.0
    current = point
    for order in range(1, degree):
        after = ((2 * order + 1) * point * current - order * before) / (order + 1)
        before = current
        current = after
    return (current, before)


def gll_derivative(points_n):
    degree = points_n - 1
    points = []
    for index in range(points_n):
        point = -math.cos(math.pi * index / degree)
        for sweep in range(100):
            top_val, below_val = legendre_values(degree, point)
            point = point - (point * top_val - below_val) / (points_n * top_val)
        points.append(point)
    values = [legendre_values(degree, point)[0] for point in points]
    deriv_rows = []
    for row_index in range(points_n):
        row_vals = []
        for col_index in range(points_n):
            if row_index != col_index:
                row_vals.append(
                    values[row_index]
                    / (values[col_index] * (points[row_index] - points[col_index]))
                )
            else:
                row_vals.append(0.0)
        deriv_rows.append(row_vals)
    deriv_rows[0][0] = -degree * (degree + 1) / 4.0
    deriv_rows[degree][degree] = degree * (degree + 1) / 4.0
    return deriv_rows


def plane_tables(planes):
    plane = np.arange(planes)
    wave = plane // 2
    phase = ((plane[:, None] * wave[None, :]) % planes) * (2.0 * math.pi / planes)
    synth = np.where((plane % 2 == 1)[None, :], np.sin(phase), np.cos(phase))
    synth[:, 1] = 1 - 2 * (plane % 2)
    scales = np.where(wave == 0, 1.0 / planes, 2.0 / planes)
    analysis = synth.T * scales[:, None]
    number = wave * (2.0 / planes)
    along = np.zeros_like(synth)
    along[:, 1::2] = number[1::2] * synth[:, 0::2]
    along[:, 0::2] = -number[0::2] * synth[:, 1::2]
    along[:, :2] = 0.0
    return tuple(t.astype(np.float32) for t in (synth, along, analysis))


def params(**kw):
    return pltpu.CompilerParams(vmem_limit_bytes=VMEM_LIMIT, **kw)


def slabs(x, parts):
    _, m_n, n_n, e_n = x.shape
    l_n = n_n // parts
    if l_n % 8:
        return x[0].reshape(m_n, parts, l_n, e_n).transpose(1, 0, 2, 3)

    rows = m_n // 4 if m_n % 4 == 0 else m_n

    def kernel(x_ref, o_ref):
        o_ref[...] = x_ref[...]

    return pl.pallas_call(
        kernel,
        grid=(parts, m_n // rows),
        in_specs=[pl.BlockSpec((1, rows, l_n, e_n), lambda q, m: (0, m, q, 0))],
        out_specs=pl.BlockSpec((1, rows, l_n, e_n), lambda q, m: (q, m, 0, 0)),
        out_shape=jax.ShapeDtypeStruct((parts, m_n, l_n, e_n), jnp.float32),
        compiler_params=params(),
        cost_estimate=pl.CostEstimate(flops=0, bytes_accessed=8 * m_n * n_n * e_n, transcendentals=0),
        name="slabs",
    )(x)


def node_major(x, parts):
    c_n, m_n, n_n, e_n = x.shape
    l_n = n_n // parts
    rows = 16

    def kernel(x_ref, o_ref):
        for n in range(0, n_n, 8):
            turned = jnp.swapaxes(x_ref[0, :, n : n + 8, :], 0, 1)
            for t in range(8):
                o_ref[(n + t) // l_n, 0, (n + t) % l_n] = turned[t]

    return pl.pallas_call(
        kernel,
        grid=(c_n, m_n // rows),
        in_specs=[pl.BlockSpec((1, rows, n_n, e_n), lambda c, m: (c, m, 0, 0))],
        out_specs=pl.BlockSpec((parts, 1, l_n, rows, e_n), lambda c, m: (0, c, 0, m, 0)),
        out_shape=jax.ShapeDtypeStruct((parts, c_n, l_n, m_n, e_n), jnp.float32),
        compiler_params=params(),
        cost_estimate=pl.CostEstimate(flops=x.size, bytes_accessed=8 * x.size, transcendentals=0),
        name="node_major",
    )(x)


def derivative(x, groups, first=0, c_n=3):
    a_n, _, l_n, m_n, e_n = x.shape
    deriv = gll_derivative(NP)
    rows = 8

    def kernel(x_ref, o_ref):
        for line in groups:
            vals = [x_ref[a, 0, l] for a, l in line]
            for i, (a, l) in enumerate(line):
                total = deriv[i][0] * vals[0]
                for k in range(1, NP):
                    if deriv[i][k] != 0.0:
                        total = total + deriv[i][k] * vals[k]
                o_ref[a, 0, l] = total

    block = (a_n, 1, l_n, rows, e_n)
    size = a_n * c_n * l_n * m_n * e_n
    return pl.pallas_call(
        kernel,
        grid=(c_n, m_n // rows),
        in_specs=[pl.BlockSpec(block, lambda c, m: (0, first + c, 0, m, 0))],
        out_specs=pl.BlockSpec(block, lambda c, m: (0, c, 0, m, 0)),
        out_shape=jax.ShapeDtypeStruct((a_n, c_n, l_n, m_n, e_n), jnp.float32),
        compiler_params=params(),
        cost_estimate=pl.CostEstimate(flops=16 * size, bytes_accessed=8 * size, transcendentals=0),
        name="line_derivative",
    )(x)


def split(x):
    high = x.astype(jnp.bfloat16)
    return high, (x - high.astype(jnp.float32)).astype(jnp.bfloat16)


def left_form(table):
    high = table.astype(ml_dtypes.bfloat16)
    low = (table - high.astype(np.float32)).astype(ml_dtypes.bfloat16)
    return jnp.asarray(np.concatenate([high, high, low], axis=1))


def right_form(x):
    high, low = split(x)
    return jnp.concatenate([high, low, high], axis=0)


def product(left, right):
    return jnp.dot(left, right, preferred_element_type=jnp.float32)


def base_products(synth_along, synth, u_a, u_b, us_a, us_b, base, geo):
    s_n, _, l_n, m_n, e_n = u_a.shape
    p_n = base.shape[2]

    def kernel(both_ref, synth_ref, ua_ref, ub_ref, usa_ref, usb_ref, b_ref, g_ref, vr_ref, part_ref):
        l = pl.program_id(0)
        field = lambda i: b_ref[i, 0].astype(jnp.float32)
        g = [g_ref[i, pl.ds(l, 1), :] for i in range(4)]
        ux, uy = field(0), field(1)
        vr_ref[0] = ux * g[0] + uy * g[2]
        vs = ux * g[1] + uy * g[3]
        uz = field(2)
        phys = []
        for c in range(3):
            u_c = ua_ref[:, 0, 0] if c == 0 else ub_ref[:, c - 1, 0]
            us_c = usa_ref[:, 0, 0] if c == 0 else usb_ref[:, c - 1, 0]
            both = product(both_ref[...], right_form(u_c.reshape(s_n * m_n, e_n)))
            phys.append(both[:p_n])
            ds = product(synth_ref[...], right_form(us_c.reshape(s_n * m_n, e_n)))
            part_ref[c, 0] = -(vs * ds) - uz * both[p_n:]
        for c in range(3):
            part_ref[c, 0] += phys[0] * field(3 + 3 * c) + phys[1] * field(4 + 3 * c) + phys[2] * field(5 + 3 * c)

    one = pl.BlockSpec((s_n, 1, 1, m_n, e_n), lambda l: (0, 0, l, 0, 0))
    two = pl.BlockSpec((s_n, 2, 1, m_n, e_n), lambda l: (0, 0, l, 0, 0))
    return pl.pallas_call(
        kernel,
        grid=(l_n,),
        in_specs=[
            pl.BlockSpec((2 * p_n, 3 * p_n), lambda l: (0, 0)),
            pl.BlockSpec((p_n, 3 * p_n), lambda l: (0, 0)),
            one,
            two,
            one,
            two,
            pl.BlockSpec((12, 1, p_n, e_n), lambda l: (0, l, 0, 0)),
            pl.BlockSpec((4, l_n, e_n), lambda l: (0, 0, 0)),
        ],
        out_specs=[
            pl.BlockSpec((1, p_n, e_n), lambda l: (l, 0, 0)),
            pl.BlockSpec((3, 1, p_n, e_n), lambda l: (0, l, 0, 0)),
        ],
        out_shape=[
            jax.ShapeDtypeStruct((l_n, p_n, e_n), jnp.float32),
            jax.ShapeDtypeStruct((3, l_n, p_n, e_n), jnp.float32),
        ],
        compiler_params=params(),
        cost_estimate=pl.CostEstimate(
            flops=9 * 2 * 3 * l_n * p_n * p_n * e_n, bytes_accessed=l_n * p_n * e_n * 64, transcendentals=0
        ),
        name="base_products",
    )(synth_along, synth, u_a, u_b, us_a, us_b, base, geo)


def forcing_modes(synth, analysis, ur, vr, part, mass, held_at, first, c_n):
    s_n, _, l_n, m_n, e_n = ur.shape
    p_n = vr.shape[1]

    def kernel(synth_ref, analysis_ref, ur_ref, vr_ref, part_ref, mass_ref, o_ref):
        l = pl.program_id(1)
        dr = product(synth_ref[...], right_form(ur_ref[:, 0, 0].reshape(s_n * m_n, e_n)))
        forcing = part_ref[0, 0] - vr_ref[0] * dr
        modes = product(analysis_ref[...], right_form(forcing)) * (STEP_SIZE * mass_ref[pl.ds(l, 1), :])
        o_ref[:, 0, 0] = modes.reshape(s_n, m_n, e_n)

    whole = pl.BlockSpec((p_n, 3 * p_n), lambda c, l: (0, 0))
    block = (s_n, 1, 1, m_n, e_n)
    return pl.pallas_call(
        kernel,
        grid=(c_n, l_n),
        in_specs=[
            whole,
            whole,
            pl.BlockSpec(block, lambda c, l: (0, held_at + c, l, 0, 0)),
            pl.BlockSpec((1, p_n, e_n), lambda c, l: (l, 0, 0)),
            pl.BlockSpec((1, 1, p_n, e_n), lambda c, l: (first + c, l, 0, 0)),
            pl.BlockSpec((l_n, e_n), lambda c, l: (0, 0)),
        ],
        out_specs=pl.BlockSpec(block, lambda c, l: (0, c, l, 0, 0)),
        out_shape=jax.ShapeDtypeStruct((s_n, c_n, l_n, m_n, e_n), jnp.float32),
        compiler_params=params(),
        cost_estimate=pl.CostEstimate(
            flops=2 * 2 * 3 * c_n * l_n * p_n * p_n * e_n,
            bytes_accessed=c_n * l_n * p_n * e_n * 16,
            transcendentals=0,
        ),
        name="forcing_modes",
    )(synth, analysis, ur, vr, part, mass)


def forcing_and_rims(synth, analysis, ur, u, vr, part, mass, connect, edge_ids, c, u_at):
    s_n, _, l_n, m_n, e_n = ur.shape
    p_n = vr.shape[1]
    k_n = edge_ids.shape[0]

    def kernel(synth_ref, analysis_ref, ur_ref, u_ref, vr_ref, part_ref, mass_ref, conn_ref, id_ref, o_ref, rim_ref):
        l = pl.program_id(0)
        dr = product(synth_ref[...], right_form(ur_ref[:, 0, 0].reshape(s_n * m_n, e_n)))
        forcing = part_ref[0, 0] - vr_ref[0] * dr
        weight = mass_ref[pl.ds(l, 1), :]
        modes = product(analysis_ref[...], right_form(forcing)) * (STEP_SIZE * weight)
        o_ref[:, 0, 0] = modes.reshape(s_n, m_n, e_n)
        high, low = split(modes + weight * u_ref[:, 0, 0].reshape(s_n * m_n, e_n))
        here = jnp.where(id_ref[...] == conn_ref[pl.ds(l, 1), :], 1.0, 0.0).astype(jnp.bfloat16)
        sums = lax.dot_general(
            jnp.concatenate([here, here], axis=1),
            jnp.concatenate([high, low], axis=1),
            (((1,), (1,)), ((), ())),
            preferred_element_type=jnp.float32,
        )

        @pl.when(l == 0)
        def _():
            rim_ref[...] = sums

        @pl.when(l > 0)
        def _():
            rim_ref[...] += sums

    whole = pl.BlockSpec((p_n, 3 * p_n), lambda l: (0, 0))
    block = (s_n, 1, 1, m_n, e_n)
    nodes = pl.BlockSpec((l_n, e_n), lambda l: (0, 0))
    return pl.pallas_call(
        kernel,
        grid=(l_n,),
        in_specs=[
            whole,
            whole,
            pl.BlockSpec(block, lambda l: (0, 0, l, 0, 0)),
            pl.BlockSpec(block, lambda l: (0, u_at, l, 0, 0)),
            pl.BlockSpec((1, p_n, e_n), lambda l: (l, 0, 0)),
            pl.BlockSpec((1, 1, p_n, e_n), lambda l: (c, l, 0, 0)),
            nodes,
            nodes,
            pl.BlockSpec((k_n, 1), lambda l: (0, 0)),
        ],
        out_specs=[
            pl.BlockSpec(block, lambda l: (0, 0, l, 0, 0)),
            pl.BlockSpec((k_n, s_n * m_n), lambda l: (0, 0)),
        ],
        out_shape=[
            jax.ShapeDtypeStruct((s_n, 1, l_n, m_n, e_n), jnp.float32),
            jax.ShapeDtypeStruct((k_n, s_n * m_n), jnp.float32),
        ],
        compiler_params=params(),
        cost_estimate=pl.CostEstimate(
            flops=4 * 2 * 3 * l_n * p_n * p_n * e_n, bytes_accessed=l_n * p_n * e_n * 20, transcendentals=0
        ),
        name="forcing_and_rims",
    )(synth, analysis, ur, u, vr, part, mass, connect, edge_ids)


def own_sums(modes, u, mass, connect, rims, edge_ids, u_at):
    s_n, _, l_n, m_n, e_n = modes.shape
    k_n = edge_ids.shape[0]
    coefs = s_n * m_n

    def kernel(f_ref, u_ref, mass_ref, conn_ref, turned_ref, rim_ref, id_ref, o_ref, held):
        l = pl.program_id(0)

        @pl.when(l == 0)
        def _():
            for k in range(l_n):
                weighted = f_ref[:, 0, k] + mass_ref[k : k + 1, :] * u_ref[:, 0, k]
                high, low = split(weighted.reshape(coefs, e_n))
                held[k] = jnp.concatenate([high, low], axis=1)

        mine = conn_ref[pl.ds(l, 1), :]

        def same(ids):
            there = jnp.where(ids == mine, 1.0, 0.0).astype(jnp.bfloat16)
            return jnp.concatenate([there, there], axis=0)

        high, low = split(rim_ref[...])
        total = product(jnp.concatenate([high, low], axis=1), same(id_ref[...]))
        for k in range(l_n):
            total = total + product(held[k], same(turned_ref[k]))
        o_ref[:, 0, 0] = total.reshape(s_n, m_n, e_n)

    def whole(*shape):
        return pl.BlockSpec(shape, lambda l: (0,) * len(shape))

    return pl.pallas_call(
        kernel,
        grid=(l_n,),
        in_specs=[
            whole(s_n, 1, l_n, m_n, e_n),
            pl.BlockSpec((s_n, 1, l_n, m_n, e_n), lambda l: (0, u_at, 0, 0, 0)),
            whole(l_n, e_n),
            whole(l_n, e_n),
            whole(l_n, e_n, 1),
            whole(coefs, k_n),
            whole(k_n, 1),
        ],
        out_specs=pl.BlockSpec((s_n, 1, 1, m_n, e_n), lambda l: (0, 0, l, 0, 0)),
        out_shape=jax.ShapeDtypeStruct(modes.shape, jnp.float32),
        scratch_shapes=[pltpu.VMEM((l_n, coefs, 2 * e_n), jnp.bfloat16)],
        compiler_params=params(),
        cost_estimate=pl.CostEstimate(
            flops=4 * l_n * l_n * coefs * e_n * e_n, bytes_accessed=12 * modes.size, transcendentals=0
        ),
        name="own_sums",
    )(modes, u, mass, connect, connect[:, :, None], rims, edge_ids)


def rows_of(ref, places):
    if len(ref.shape) == 3:
        return [ref[r >> 3, pl.ds(r & 7, 1), :] for r in places]
    return [ref[pl.ds(r, 1), :] for r in places]


def put_rows(ref, places, rows):
    for r, row in zip(places, rows):
        if len(ref.shape) == 3:
            ref[r >> 3, pl.ds(r & 7, 1), :] = row
        else:
            ref[pl.ds(r, 1), :] = row


def some_pairs(codes, at, number):
    found = [codes[at + t] for t in range(number)]
    return [code >> PACK for code in found], [code & (1 << PACK) - 1 for code in found]


def sum_class(ref, codes, start, number, both):
    def batch(i, _):
        others, heads = some_pairs(codes, start + i * BATCH, BATCH)
        sums = [a + b for a, b in zip(rows_of(ref, heads), rows_of(ref, others))]
        put_rows(ref, heads, sums)
        if both:
            put_rows(ref, others, sums)
        return 0

    lax.fori_loop(0, pl.cdiv(number, BATCH), batch, 0)


def sum_rest(ref, codes, start, number):
    def one(i, _):
        others, heads = some_pairs(codes, start + i, 1)
        put_rows(ref, heads, [rows_of(ref, heads)[0] + rows_of(ref, others)[0]])
        return 0

    lax.fori_loop(0, number, one, 0)


def hand_back(ref, codes, start, end):
    def batch(i, _):
        others, heads = some_pairs(codes, start + i * BATCH, BATCH)
        put_rows(ref, others, rows_of(ref, heads))
        return 0

    lax.fori_loop(0, pl.cdiv(end - start, BATCH), batch, 0)


def finish(sums, pairs, inverse, held, shape, c):
    s_n, _, l_n, m_n, e_n = sums.shape
    _, _, nodes_n, _ = shape
    rows_n = nodes_n * e_n
    codes, bounds = pairs
    step = max(8, l_n)
    tiles = e_n // 8
    outs = nodes_n // step

    def kernel(codes, bnd, f_ref, inv_ref, _, o_ref, table, stage):
        b = pl.program_id(0)

        @pl.when(b < s_n)
        def _():
            for t in range(l_n):
                node = b * l_n + t
                table[pl.ds(node * tiles, tiles)] = f_ref[0, 0, t].T.reshape(tiles, 8, m_n)

        @pl.when(b == s_n - 1)
        def _():
            table[nodes_n * tiles] = jnp.zeros((8, m_n), jnp.float32)
            for k in range(CLASSES):
                sum_class(table, codes, bnd[2 * k], bnd[2 * k + 1], k == 0)
            sum_rest(table, codes, bnd[2 * CLASSES], bnd[2 * CLASSES + 1])
            hand_back(table, codes, bnd[2], bnd[2 * CLASSES + 2] + bnd[2 * CLASSES + 3])

        @pl.when(b >= s_n)
        def _():
            for t in range(step):
                n = (b - s_n) * step + t
                rows = table[pl.ds(n * tiles, tiles)].reshape(e_n, m_n).T
                stage[t] = rows * inv_ref[pl.ds(n, 1), :]
            o_ref[0] = jnp.swapaxes(stage[...], 0, 1)

    smem = pl.BlockSpec(memory_space=pltpu.SMEM)
    return pl.pallas_call(
        kernel,
        grid=(s_n + outs,),
        in_specs=[smem] * 2
        + [
            pl.BlockSpec((1, 1, l_n, m_n, e_n), lambda b: (jnp.minimum(b, s_n - 1), 0, 0, 0, 0)),
            pl.BlockSpec((nodes_n, e_n), lambda b: (0, 0)),
            pl.BlockSpec(memory_space=pl.ANY),
        ],
        out_specs=pl.BlockSpec((1, m_n, step, e_n), lambda b: (c, 0, jnp.maximum(b - s_n, 0), 0)),
        out_shape=jax.ShapeDtypeStruct(shape, jnp.float32),
        scratch_shapes=[pltpu.VMEM((nodes_n * tiles + 1, 8, m_n), jnp.float32), pltpu.VMEM((step, m_n, e_n), jnp.float32)],
        input_output_aliases={4: 0},
        compiler_params=params(),
        cost_estimate=pl.CostEstimate(
            flops=rows_n * LANES * 400, bytes_accessed=rows_n * m_n * 12, transcendentals=0
        ),
        name="finish",
    )(codes, bounds, sums, inverse, held)


def local_sums(modes, u, mass, pairs, edge_reps, first):
    s_n, c_n, l_n, m_n, e_n = modes.shape
    nodes_n = s_n * l_n
    rows_n = nodes_n * e_n
    step = min(8, l_n)
    per = l_n // step
    codes, bounds = pairs
    edges_n = edge_reps.shape[1]
    feats = c_n * m_n

    def kernel(codes, bnd, er, f_ref, u_ref, mass_ref, o_ref, low_ref, up_ref):
        b = pl.program_id(0)
        for t in range(step):
            node = b * step + t
            weight = mass_ref[pl.ds(node, 1), :]
            rows = [f_ref[0, c, t] + weight * u_ref[0, c, t] for c in range(c_n)]
            table = jnp.concatenate(rows, axis=0) if c_n > 1 else rows[0]
            o_ref[pl.ds(pl.multiple_of(node * e_n, e_n), e_n), :] = table.T

        @pl.when(b == pl.num_programs(0) - 1)
        def _():
            o_ref[pl.ds(rows_n, 8), :] = jnp.zeros((8, feats), jnp.float32)

            for k in range(CLASSES):
                sum_class(o_ref, codes, bnd[2 * k], bnd[2 * k + 1], False)
            sum_rest(o_ref, codes, bnd[2 * CLASSES], bnd[2 * CLASSES + 1])

            def edge(i, _):
                for side, to in enumerate((low_ref, up_ref)):
                    got = rows_of(o_ref, [er[side, i * BATCH + t] for t in range(BATCH)])
                    put_rows(to, [i * BATCH + t for t in range(BATCH)], got)
                return 0

            lax.fori_loop(0, edges_n // BATCH, edge, 0)

    smem = pl.BlockSpec(memory_space=pltpu.SMEM)
    where = lambda b: (b // per, 0, b % per, 0, 0)
    where_u = lambda b: (b // per, first // c_n, b % per, 0, 0)
    rim = pl.BlockSpec((edges_n, feats), lambda b: (0, 0))
    rim_shape = jax.ShapeDtypeStruct((edges_n, feats), jnp.float32)
    return pl.pallas_call(
        kernel,
        grid=(nodes_n // step,),
        in_specs=[smem] * 3
        + [
            pl.BlockSpec((1, c_n, step, m_n, e_n), where),
            pl.BlockSpec((1, c_n, step, m_n, e_n), where_u),
            pl.BlockSpec((nodes_n, e_n), lambda b: (0, 0)),
        ],
        out_specs=[pl.BlockSpec((rows_n + 8, feats), lambda b: (0, 0)), rim, rim],
        out_shape=[jax.ShapeDtypeStruct((rows_n + 8, feats), jnp.float32), rim_shape, rim_shape],
        compiler_params=params(),
        cost_estimate=pl.CostEstimate(
            flops=rows_n * LANES * 400, bytes_accessed=rows_n * LANES * 12, transcendentals=0
        ),
        name="local_sums",
    )(codes, bounds, edge_reps, modes, u, mass)


def spread(table, rims, pairs, edge_reps, inverse, held, shape, first, c_n):
    _, m_n, nodes_n, e_n = shape
    rows_n = nodes_n * e_n
    step = 8
    edges_n = edge_reps.shape[1]
    codes, bounds = pairs
    feats = c_n * m_n

    def kernel(codes, bnd, er, t_ref, low_ref, up_ref, inv_ref, *rest):
        o_ref, stage = rest[-2:]
        b = pl.program_id(0)

        @pl.when(b == 0)
        def _():
            def edge(i, _):
                for side, came in enumerate((low_ref, up_ref)):
                    spots = [er[side, i * BATCH + t] for t in range(BATCH)]
                    more = rows_of(came, [i * BATCH + t for t in range(BATCH)])
                    put_rows(t_ref, spots, [a + b for a, b in zip(rows_of(t_ref, spots), more)])
                return 0

            lax.fori_loop(0, edges_n // BATCH, edge, 0)
            hand_back(t_ref, codes, 0, bnd[2 * CLASSES] + bnd[2 * CLASSES + 1])

        for t in range(step):
            n = b * step + t
            rows = t_ref[pl.ds(pl.multiple_of(n * e_n, e_n), e_n), :].T
            scaled = rows * inv_ref[pl.ds(n, 1), :]
            for c in range(c_n):
                stage[c, t] = scaled[c * m_n : (c + 1) * m_n]
        for c in range(c_n):
            o_ref[c] = jnp.swapaxes(stage[c], 0, 1)

    smem = pl.BlockSpec(memory_space=pltpu.SMEM)
    rim = pl.BlockSpec((edges_n, feats), lambda b: (0, 0))
    in_specs = [smem] * 3 + [
        pl.BlockSpec((rows_n + 8, feats), lambda b: (0, 0)),
        rim,
        rim,
        pl.BlockSpec((nodes_n, e_n), lambda b: (0, 0)),
    ]
    args = [codes, bounds, edge_reps, table, *rims, inverse]
    aliases = {}
    if held is not None:
        in_specs.append(pl.BlockSpec(memory_space=pl.ANY))
        args.append(held)
        aliases = {len(args) - 1: 0}
    return pl.pallas_call(
        kernel,
        grid=(nodes_n // step,),
        in_specs=in_specs,
        out_specs=pl.BlockSpec((c_n, m_n, step, e_n), lambda b: (first // c_n, 0, b, 0)),
        out_shape=jax.ShapeDtypeStruct(shape, jnp.float32),
        scratch_shapes=[pltpu.VMEM((c_n, step, m_n, e_n), jnp.float32)],
        input_output_aliases=aliases,
        compiler_params=params(),
        cost_estimate=pl.CostEstimate(
            flops=rows_n * LANES * 400, bytes_accessed=rows_n * LANES * 12, transcendentals=0
        ),
        name="spread",
    )(*args)


def fill_up(values, multiple, filler):
    short = -values.shape[-1] % multiple
    pad = [(0, 0)] * (values.ndim - 1) + [(0, short)]
    return jnp.pad(values, pad, constant_values=filler)


def grouped(group, classes, member, rep, pairs_n):
    rows_n = group.shape[0]
    assert rows_n < 1 << PACK
    nobody = rows_n * (1 << PACK) + rows_n
    spare_group = jnp.arange(CLASSES * BATCH, dtype=jnp.int32) // BATCH
    _, codes = lax.sort(
        (
            jnp.concatenate([group.astype(jnp.int32), spare_group]),
            jnp.concatenate([member * (1 << PACK) + rep, jnp.full((CLASSES * BATCH,), nobody, jnp.int32)]),
        ),
        num_keys=1,
        is_stable=True,
    )
    spares = BATCH * jnp.minimum(jnp.arange(classes, dtype=jnp.int32), CLASSES)
    numbers = jnp.stack([jnp.sum(group == k, dtype=jnp.int32) for k in range(classes)])
    starts = jnp.cumsum(numbers) - numbers + spares
    bounds = jnp.stack([starts, numbers], axis=1).reshape(-1).astype(jnp.int32)
    length = pairs_n + CLASSES * BATCH
    return jnp.pad(codes[:length], (0, BATCH + -length % BATCH), constant_values=nobody), bounds


def pair_lists(ids, edges, parts):
    rows_n = ids.shape[0]
    place = jnp.arange(rows_n, dtype=jnp.int32)
    ids_sorted, member = lax.sort((ids, place), num_keys=1, is_stable=True)
    yes = jnp.ones((1,), bool)
    head = jnp.concatenate([yes, ids_sorted[1:] != ids_sorted[:-1]])
    last = jnp.concatenate([head[1:], yes])
    code = lax.cummax(jnp.where(head, place * rows_n + member, 0))
    rep = code % rows_n
    rank = place - code // rows_n
    pairs_n = rows_n - UNIQUE
    group = jnp.where((rank == 1) & last, 0, jnp.minimum(rank, CLASSES))
    group = jnp.where(rank == 0, CLASSES + 1, group)
    pairs = grouped(group, CLASSES + 1, member, rep, pairs_n)

    device = member // (rows_n // parts)
    device_first = head | jnp.concatenate([yes, device[1:] != device[:-1]])
    device_no = lax.cumsum(device_first.astype(jnp.int32))
    device_rank = device_no - lax.cummax(jnp.where(head, device_no, 0))
    most = lax.cummax(jnp.where(last, (rows_n - place) * parts + device_rank, 0), reverse=True) % parts
    group = jnp.where(device_first, jnp.minimum(device_rank, CLASSES), CLASSES + 1)
    group = jnp.where((rank == 1) & last & (device_rank == 1), 0, group)
    group = jnp.where((rank == 0) | (most == 0), CLASSES + 2, group)
    across = grouped(group, CLASSES + 2, member, rep, pairs_n)

    flat = edges.reshape(-1)
    start = jnp.sum(ids_sorted[None, :] < flat[:, None], axis=1, dtype=jnp.int32)
    edge_reps = fill_up(member[start].reshape(edges.shape), BATCH, rows_n)
    return pairs, across, edge_reps


def shifted(x, axis, step):
    count = lax.axis_size(axis)
    return lax.ppermute(x, axis, [(i, (i + step) % count) for i in range(count)])


def largest_of_partitions(x):
    step = 1
    while step < lax.axis_size("mesh"):
        x = jnp.maximum(x, shifted(x, "mesh", step))
        step *= 2
    return x


def total_over_four(x):
    total = x
    for step in range(1, lax.axis_size("four")):
        total = total + shifted(x, "four", step)
    return total


def swap_edges(low, up):
    return shifted(up, "mesh", 1), shifted(low, "mesh", -1)


def edge_takers(edges, connect, edge_reps, parts):
    here_n = connect.size // parts
    ids = fill_up(edges, BATCH, -1)
    has = jnp.any(ids[:, None, :, None] == connect.reshape(1, parts, 1, here_n), axis=3).astype(jnp.float32)
    theirs = jnp.stack(swap_edges(has[0], has[1]))
    spread_out = largest_of_partitions(jnp.max(theirs * (1.0 - has)).reshape(1))[0] > 0.5
    at_rep = jnp.where(edge_reps // here_n == lax.axis_index("four"), ids, -1)
    taken = jnp.where(spread_out, at_rep, ids)
    return ids.reshape(-1, 1), taken.reshape(-1, 1), spread_out


def inverse_mass(mass, ids, edges):
    summed = jnp.zeros((UNIQUE,), jnp.float32).at[ids].add(mass.reshape(-1))
    came = jnp.concatenate(swap_edges(summed[edges[0]], summed[edges[1]]))
    summed = summed.at[edges.reshape(-1)].add(came)
    return (1.0 / summed[ids]).reshape(mass.shape)


def exchange(x):
    return lax.all_to_all(x, "four", split_axis=0, concat_axis=0, tiled=True)


def body(adj_modes, base_flow, geometry, mass, connect, edge_nodes):
    comps, m_n, nodes_n, e_n = adj_modes.shape
    parts = lax.axis_size("four")
    l_n = nodes_n // parts
    mine = lax.axis_index("four") * l_n
    synth, along, analysis = plane_tables(PLANES)
    both_3 = left_form(np.concatenate([synth, along]))
    synth_3, analysis_3 = left_form(synth), left_form(analysis)
    together = lax.optimization_barrier
    spot = lambda n: (n // l_n, n % l_n)
    along_r = [[spot(NP * i + j) for i in range(NP)] for j in range(NP)]
    along_s = [[spot(NP * i + j) for j in range(NP)] for i in range(NP)]
    inside = [[(a, l + j) for j in range(NP)] for a in range(parts) for l in range(0, l_n, NP)]
    whole_rows = l_n % NP == 0

    u_first = slabs(adj_modes, parts)
    u_first, adj_modes = together((u_first, adj_modes))
    first_here = exchange(u_first)

    u = node_major(adj_modes, parts)
    ur_a, ur_b = derivative(u, along_r, 0, 2), derivative(u, along_r, 2, 1)
    sent = [u[:, 1:], ur_a] + ([] if whole_rows else [derivative(u, along_s)])
    sent = jnp.concatenate(sent, axis=1)
    sent, u, ur_b, first_here, connect, edge_nodes, mass, base_flow = together(
        (sent, u, ur_b, first_here, connect, edge_nodes, mass, base_flow)
    )

    here = exchange(sent)
    edges = edge_nodes[0]
    ids = connect.reshape(-1)
    pairs, across, edge_reps = pair_lists(ids, edges, parts)
    inverse = inverse_mass(mass, ids, edges)
    base = base_flow.transpose(0, 2, 1, 3)
    if l_n % 8 == 0:
        u0_here = node_major(first_here, 1).reshape(parts, 1, l_n, m_n, e_n)
    else:
        u0_here = first_here.transpose(0, 2, 1, 3)[:, None]
    us0_here = derivative(u0_here, inside, 0, 1) if whole_rows else None
    mass_here = lax.dynamic_slice_in_dim(mass, mine, l_n, 0)
    connect_here = lax.dynamic_slice_in_dim(connect, mine, l_n, 0)
    edge_ids, taken_ids, spread_out = edge_takers(edges, connect, edge_reps, parts)
    held = (here, ur_b, pairs, across, edge_reps, inverse, base, u0_here, us0_here, edge_ids, taken_ids, spread_out)
    here, ur_b, pairs, across, edge_reps, inverse, base, u0_here, us0_here, edge_ids, taken_ids, spread_out = together(held)

    ur_b_here = exchange(ur_b)
    us_here = derivative(here, inside, 0, 2) if whole_rows else here[:, 5:7]
    if not whole_rows:
        us0_here = here[:, 4:5]
    geo = lax.dynamic_slice_in_dim(geometry, mine, l_n, 1)
    vr, part = base_products(both_3, synth_3, u0_here, here, us0_here, us_here, base, geo)
    f_a = forcing_modes(synth_3, analysis_3, here, vr, part, mass_here, 2, 0, 2)
    f_a, ur_b_here = together((f_a, ur_b_here))

    modes_a = exchange(f_a)
    f_b, rims = forcing_and_rims(
        synth_3, analysis_3, ur_b_here, here, vr, part, mass_here, connect_here, edge_ids, 2, 1
    )
    half = rims.shape[0] // 2
    rims = jnp.concatenate(swap_edges(rims[:half], rims[half:]))
    rims = lax.cond(spread_out, total_over_four, lambda r: r, rims)
    f_b = own_sums(f_b, here, mass_here, connect_here, rims.T, taken_ids, 1)
    f_b, modes_a = together((f_b, modes_a))

    modes_b = exchange(f_b)
    table, *rims = local_sums(modes_a, u, mass, pairs, edge_reps, 0)
    out = spread(table, swap_edges(*rims), pairs, edge_reps, inverse, None, adj_modes.shape, 0, 2)
    modes_b, out = together((modes_b, out))

    return finish(modes_b, across, inverse, out, adj_modes.shape, 2)


def solution(mesh):
    return jax.shard_map(
        body,
        mesh=mesh,
        in_specs=(
            P(None, "four", None, "mesh"),
            P(None, None, "four", "mesh"),
            P(None, None, "mesh"),
            P(None, "mesh"),
            P(None, "mesh"),
            P("mesh", None, None),
        ),
        out_specs=P(None, "four", None, "mesh"),
        check_vma=False,
    )
```

```python
import math

import jax
import jax.numpy as jnp
import ml_dtypes
import numpy as np
from jax import lax
from jax.experimental import pallas as pl
from jax.experimental.pallas import tpu as pltpu
from jax.sharding import PartitionSpec as P

NP = 8
PLANES = 256
UNIQUE = 12825
STEP_SIZE = 0.1
LANES = 128
BATCH = 16
CLASSES = 4
PACK = 15
VMEM_LIMIT = 56 * 1024 * 1024


def legendre_values(degree, point):
    before = 1.0
    current = point
    for order in range(1, degree):
        after = ((2 * order + 1) * point * current - order * before) / (order + 1)
        before = current
        current = after
    return (current, before)


def gll_derivative(points_n):
    degree = points_n - 1
    points = []
    for index in range(points_n):
        point = -math.cos(math.pi * index / degree)
        for sweep in range(100):
            top_val, below_val = legendre_values(degree, point)
            point = point - (point * top_val - below_val) / (points_n * top_val)
        points.append(point)
    values = [legendre_values(degree, point)[0] for point in points]
    deriv_rows = []
    for row_index in range(points_n):
        row_vals = []
        for col_index in range(points_n):
            if row_index != col_index:
                row_vals.append(
                    values[row_index]
                    / (values[col_index] * (points[row_index] - points[col_index]))
                )
            else:
                row_vals.append(0.0)
        deriv_rows.append(row_vals)
    deriv_rows[0][0] = -degree * (degree + 1) / 4.0
    deriv_rows[degree][degree] = degree * (degree + 1) / 4.0
    return deriv_rows


def plane_tables(planes):
    plane = np.arange(planes)
    wave = plane // 2
    phase = ((plane[:, None] * wave[None, :]) % planes) * (2.0 * math.pi / planes)
    synth = np.where((plane % 2 == 1)[None, :], np.sin(phase), np.cos(phase))
    synth[:, 1] = 1 - 2 * (plane % 2)
    scales = np.where(wave == 0, 1.0 / planes, 2.0 / planes)
    analysis = synth.T * scales[:, None]
    number = wave * (2.0 / planes)
    along = np.zeros_like(synth)
    along[:, 1::2] = number[1::2] * synth[:, 0::2]
    along[:, 0::2] = -number[0::2] * synth[:, 1::2]
    along[:, :2] = 0.0
    return tuple(t.astype(np.float32) for t in (synth, along, analysis))


def params(**kw):
    return pltpu.CompilerParams(vmem_limit_bytes=VMEM_LIMIT, **kw)


def node_major(x, parts):
    c_n, m_n, n_n, e_n = x.shape
    l_n = n_n // parts
    rows = 16

    def kernel(x_ref, o_ref):
        for n in range(0, n_n, 8):
            turned = jnp.swapaxes(x_ref[0, :, n : n + 8, :], 0, 1)
            for t in range(8):
                o_ref[(n + t) // l_n, 0, (n + t) % l_n] = turned[t]

    return pl.pallas_call(
        kernel,
        grid=(c_n, m_n // rows),
        in_specs=[pl.BlockSpec((1, rows, n_n, e_n), lambda c, m: (c, m, 0, 0))],
        out_specs=pl.BlockSpec((parts, 1, l_n, rows, e_n), lambda c, m: (0, c, 0, m, 0)),
        out_shape=jax.ShapeDtypeStruct((parts, c_n, l_n, m_n, e_n), jnp.float32),
        compiler_params=params(),
        cost_estimate=pl.CostEstimate(flops=x.size, bytes_accessed=8 * x.size, transcendentals=0),
        name="node_major",
    )(x)


def derivative(x, groups, first=0, c_n=3):
    a_n, _, l_n, m_n, e_n = x.shape
    deriv = gll_derivative(NP)
    rows = 8

    def kernel(x_ref, o_ref):
        for line in groups:
            vals = [x_ref[a, 0, l] for a, l in line]
            for i, (a, l) in enumerate(line):
                total = deriv[i][0] * vals[0]
                for k in range(1, NP):
                    if deriv[i][k] != 0.0:
                        total = total + deriv[i][k] * vals[k]
                o_ref[a, 0, l] = total

    block = (a_n, 1, l_n, rows, e_n)
    size = a_n * c_n * l_n * m_n * e_n
    return pl.pallas_call(
        kernel,
        grid=(c_n, m_n // rows),
        in_specs=[pl.BlockSpec(block, lambda c, m: (0, first + c, 0, m, 0))],
        out_specs=pl.BlockSpec(block, lambda c, m: (0, c, 0, m, 0)),
        out_shape=jax.ShapeDtypeStruct((a_n, c_n, l_n, m_n, e_n), jnp.float32),
        compiler_params=params(),
        cost_estimate=pl.CostEstimate(flops=16 * size, bytes_accessed=8 * size, transcendentals=0),
        name="line_derivative",
    )(x)


def split(x):
    high = x.astype(jnp.bfloat16)
    return high, (x - high.astype(jnp.float32)).astype(jnp.bfloat16)


def left_form(table):
    high = table.astype(ml_dtypes.bfloat16)
    low = (table - high.astype(np.float32)).astype(ml_dtypes.bfloat16)
    return jnp.asarray(np.concatenate([high, high, low], axis=1))


def right_form(x):
    high, low = split(x)
    return jnp.concatenate([high, low, high], axis=0)


def product(left, right):
    return jnp.dot(left, right, preferred_element_type=jnp.float32)


def base_products(synth_along, synth, u_a, u_b, us_a, us_b, base, geo):
    s_n, _, l_n, m_n, e_n = u_a.shape
    p_n = base.shape[2]

    def kernel(both_ref, synth_ref, ua_ref, ub_ref, usa_ref, usb_ref, b_ref, g_ref, vr_ref, part_ref):
        l = pl.program_id(0)
        field = lambda i: b_ref[i, 0].astype(jnp.float32)
        g = [g_ref[i, pl.ds(l, 1), :] for i in range(4)]
        ux, uy = field(0), field(1)
        vr_ref[0] = ux * g[0] + uy * g[2]
        vs = ux * g[1] + uy * g[3]
        uz = field(2)
        phys = []
        for c in range(3):
            u_c = ua_ref[:, 0, 0] if c == 0 else ub_ref[:, c - 1, 0]
            us_c = usa_ref[:, 0, 0] if c == 0 else usb_ref[:, c - 1, 0]
            both = product(both_ref[...], right_form(u_c.reshape(s_n * m_n, e_n)))
            phys.append(both[:p_n])
            ds = product(synth_ref[...], right_form(us_c.reshape(s_n * m_n, e_n)))
            part_ref[c, 0] = -(vs * ds) - uz * both[p_n:]
        for c in range(3):
            part_ref[c, 0] += phys[0] * field(3 + 3 * c) + phys[1] * field(4 + 3 * c) + phys[2] * field(5 + 3 * c)

    one = pl.BlockSpec((s_n, 1, 1, m_n, e_n), lambda l: (0, 0, l, 0, 0))
    two = pl.BlockSpec((s_n, 2, 1, m_n, e_n), lambda l: (0, 0, l, 0, 0))
    return pl.pallas_call(
        kernel,
        grid=(l_n,),
        in_specs=[
            pl.BlockSpec((2 * p_n, 3 * p_n), lambda l: (0, 0)),
            pl.BlockSpec((p_n, 3 * p_n), lambda l: (0, 0)),
            one,
            two,
            one,
            two,
            pl.BlockSpec((12, 1, p_n, e_n), lambda l: (0, l, 0, 0)),
            pl.BlockSpec((4, l_n, e_n), lambda l: (0, 0, 0)),
        ],
        out_specs=[
            pl.BlockSpec((1, p_n, e_n), lambda l: (l, 0, 0)),
            pl.BlockSpec((3, 1, p_n, e_n), lambda l: (0, l, 0, 0)),
        ],
        out_shape=[
            jax.ShapeDtypeStruct((l_n, p_n, e_n), jnp.float32),
            jax.ShapeDtypeStruct((3, l_n, p_n, e_n), jnp.float32),
        ],
        compiler_params=params(),
        cost_estimate=pl.CostEstimate(
            flops=9 * 2 * 3 * l_n * p_n * p_n * e_n, bytes_accessed=l_n * p_n * e_n * 64, transcendentals=0
        ),
        name="base_products",
    )(synth_along, synth, u_a, u_b, us_a, us_b, base, geo)


def forcing_modes(synth, analysis, ur, vr, part, mass, held_at, first, c_n):
    s_n, _, l_n, m_n, e_n = ur.shape
    p_n = vr.shape[1]

    def kernel(synth_ref, analysis_ref, ur_ref, vr_ref, part_ref, mass_ref, o_ref):
        l = pl.program_id(1)
        dr = product(synth_ref[...], right_form(ur_ref[:, 0, 0].reshape(s_n * m_n, e_n)))
        forcing = part_ref[0, 0] - vr_ref[0] * dr
        modes = product(analysis_ref[...], right_form(forcing)) * (STEP_SIZE * mass_ref[pl.ds(l, 1), :])
        o_ref[:, 0, 0] = modes.reshape(s_n, m_n, e_n)

    whole = pl.BlockSpec((p_n, 3 * p_n), lambda c, l: (0, 0))
    block = (s_n, 1, 1, m_n, e_n)
    return pl.pallas_call(
        kernel,
        grid=(c_n, l_n),
        in_specs=[
            whole,
            whole,
            pl.BlockSpec(block, lambda c, l: (0, held_at + c, l, 0, 0)),
            pl.BlockSpec((1, p_n, e_n), lambda c, l: (l, 0, 0)),
            pl.BlockSpec((1, 1, p_n, e_n), lambda c, l: (first + c, l, 0, 0)),
            pl.BlockSpec((l_n, e_n), lambda c, l: (0, 0)),
        ],
        out_specs=pl.BlockSpec(block, lambda c, l: (0, c, l, 0, 0)),
        out_shape=jax.ShapeDtypeStruct((s_n, c_n, l_n, m_n, e_n), jnp.float32),
        compiler_params=params(),
        cost_estimate=pl.CostEstimate(
            flops=2 * 2 * 3 * c_n * l_n * p_n * p_n * e_n,
            bytes_accessed=c_n * l_n * p_n * e_n * 16,
            transcendentals=0,
        ),
        name="forcing_modes",
    )(synth, analysis, ur, vr, part, mass)


def forcing_and_rims(synth, analysis, ur, u, vr, part, mass, connect, edge_ids, c, u_at):
    s_n, _, l_n, m_n, e_n = ur.shape
    p_n = vr.shape[1]
    k_n = edge_ids.shape[0]

    def kernel(synth_ref, analysis_ref, ur_ref, u_ref, vr_ref, part_ref, mass_ref, conn_ref, id_ref, o_ref, rim_ref):
        l = pl.program_id(0)
        dr = product(synth_ref[...], right_form(ur_ref[:, 0, 0].reshape(s_n * m_n, e_n)))
        forcing = part_ref[0, 0] - vr_ref[0] * dr
        weight = mass_ref[pl.ds(l, 1), :]
        modes = product(analysis_ref[...], right_form(forcing)) * (STEP_SIZE * weight)
        o_ref[:, 0, 0] = modes.reshape(s_n, m_n, e_n)
        high, low = split(modes + weight * u_ref[:, 0, 0].reshape(s_n * m_n, e_n))
        here = jnp.where(id_ref[...] == conn_ref[pl.ds(l, 1), :], 1.0, 0.0).astype(jnp.bfloat16)
        sums = lax.dot_general(
            jnp.concatenate([here, here], axis=1),
            jnp.concatenate([high, low], axis=1),
            (((1,), (1,)), ((), ())),
            preferred_element_type=jnp.float32,
        )

        @pl.when(l == 0)
        def _():
            rim_ref[...] = sums

        @pl.when(l > 0)
        def _():
            rim_ref[...] += sums

    whole = pl.BlockSpec((p_n, 3 * p_n), lambda l: (0, 0))
    block = (s_n, 1, 1, m_n, e_n)
    nodes = pl.BlockSpec((l_n, e_n), lambda l: (0, 0))
    return pl.pallas_call(
        kernel,
        grid=(l_n,),
        in_specs=[
            whole,
            whole,
            pl.BlockSpec(block, lambda l: (0, 0, l, 0, 0)),
            pl.BlockSpec(block, lambda l: (0, u_at, l, 0, 0)),
            pl.BlockSpec((1, p_n, e_n), lambda l: (l, 0, 0)),
            pl.BlockSpec((1, 1, p_n, e_n), lambda l: (c, l, 0, 0)),
            nodes,
            nodes,
            pl.BlockSpec((k_n, 1), lambda l: (0, 0)),
        ],
        out_specs=[
            pl.BlockSpec(block, lambda l: (0, 0, l, 0, 0)),
            pl.BlockSpec((k_n, s_n * m_n), lambda l: (0, 0)),
        ],
        out_shape=[
            jax.ShapeDtypeStruct((s_n, 1, l_n, m_n, e_n), jnp.float32),
            jax.ShapeDtypeStruct((k_n, s_n * m_n), jnp.float32),
        ],
        compiler_params=params(),
        cost_estimate=pl.CostEstimate(
            flops=4 * 2 * 3 * l_n * p_n * p_n * e_n, bytes_accessed=l_n * p_n * e_n * 20, transcendentals=0
        ),
        name="forcing_and_rims",
    )(synth, analysis, ur, u, vr, part, mass, connect, edge_ids)


def own_sums(modes, u, mass, connect, rims, edge_ids, u_at):
    s_n, _, l_n, m_n, e_n = modes.shape
    k_n = edge_ids.shape[0]
    coefs = s_n * m_n

    def kernel(f_ref, u_ref, mass_ref, conn_ref, turned_ref, rim_ref, id_ref, o_ref, held):
        l = pl.program_id(0)

        @pl.when(l == 0)
        def _():
            for k in range(l_n):
                weighted = f_ref[:, 0, k] + mass_ref[k : k + 1, :] * u_ref[:, 0, k]
                high, low = split(weighted.reshape(coefs, e_n))
                held[k] = jnp.concatenate([high, low], axis=1)

        mine = conn_ref[pl.ds(l, 1), :]

        def same(ids):
            there = jnp.where(ids == mine, 1.0, 0.0).astype(jnp.bfloat16)
            return jnp.concatenate([there, there], axis=0)

        high, low = split(rim_ref[...])
        total = product(jnp.concatenate([high, low], axis=1), same(id_ref[...]))
        for k in range(l_n):
            total = total + product(held[k], same(turned_ref[k]))
        o_ref[:, 0, 0] = total.reshape(s_n, m_n, e_n)

    def whole(*shape):
        return pl.BlockSpec(shape, lambda l: (0,) * len(shape))

    return pl.pallas_call(
        kernel,
        grid=(l_n,),
        in_specs=[
            whole(s_n, 1, l_n, m_n, e_n),
            pl.BlockSpec((s_n, 1, l_n, m_n, e_n), lambda l: (0, u_at, 0, 0, 0)),
            whole(l_n, e_n),
            whole(l_n, e_n),
            whole(l_n, e_n, 1),
            whole(coefs, k_n),
            whole(k_n, 1),
        ],
        out_specs=pl.BlockSpec((s_n, 1, 1, m_n, e_n), lambda l: (0, 0, l, 0, 0)),
        out_shape=jax.ShapeDtypeStruct(modes.shape, jnp.float32),
        scratch_shapes=[pltpu.VMEM((l_n, coefs, 2 * e_n), jnp.bfloat16)],
        compiler_params=params(),
        cost_estimate=pl.CostEstimate(
            flops=4 * l_n * l_n * coefs * e_n * e_n, bytes_accessed=12 * modes.size, transcendentals=0
        ),
        name="own_sums",
    )(modes, u, mass, connect, connect[:, :, None], rims, edge_ids)


def rows_of(ref, places):
    return [ref[pl.ds(r, 1), :] for r in places]


def put_rows(ref, places, rows):
    for r, row in zip(places, rows):
        ref[pl.ds(r, 1), :] = row


def some_pairs(codes, at, number):
    found = [codes[at + t] for t in range(number)]
    return [code >> PACK for code in found], [code & (1 << PACK) - 1 for code in found]


def sum_class(ref, codes, start, number, both):
    def batch(i, _):
        others, heads = some_pairs(codes, start + i * BATCH, BATCH)
        sums = [a + b for a, b in zip(rows_of(ref, heads), rows_of(ref, others))]
        put_rows(ref, heads, sums)
        if both:
            put_rows(ref, others, sums)
        return 0

    lax.fori_loop(0, pl.cdiv(number, BATCH), batch, 0)


def sum_rest(ref, codes, start, number):
    def one(i, _):
        others, heads = some_pairs(codes, start + i, 1)
        put_rows(ref, heads, [rows_of(ref, heads)[0] + rows_of(ref, others)[0]])
        return 0

    lax.fori_loop(0, number, one, 0)


def hand_back(ref, codes, start, end):
    def batch(i, _):
        others, heads = some_pairs(codes, start + i * BATCH, BATCH)
        put_rows(ref, others, rows_of(ref, heads))
        return 0

    lax.fori_loop(0, pl.cdiv(end - start, BATCH), batch, 0)


def finish(sums, pairs, shared, inverse, held, shape, c):
    s_n, _, l_n, m_n, e_n = sums.shape
    _, _, nodes_n, _ = shape
    rows_n = nodes_n * e_n
    codes, bounds = pairs
    batch = nodes_n // shared.shape[0]
    step = max(8, l_n)
    outs = nodes_n // step

    def kernel(codes, bnd, mark, f_ref, again_ref, inv_ref, _, o_ref, table, stage):
        b = pl.program_id(0)

        def place(node):
            return pl.ds(pl.multiple_of(node * e_n, e_n), e_n)

        @pl.when(b < s_n)
        def _():
            for at in range(0, l_n, batch):

                @pl.when(mark[(b * l_n + at) // batch] != 0)
                def _():
                    for t in range(at, at + batch):
                        table[place(b * l_n + t), :] = f_ref[0, 0, t].T

        @pl.when(b == s_n - 1)
        def _():
            table[pl.ds(rows_n, 8), :] = jnp.zeros((8, m_n), jnp.float32)
            for k in range(CLASSES):
                sum_class(table, codes, bnd[2 * k], bnd[2 * k + 1], k == 0)
            sum_rest(table, codes, bnd[2 * CLASSES], bnd[2 * CLASSES + 1])
            hand_back(table, codes, bnd[2], bnd[2 * CLASSES + 2] + bnd[2 * CLASSES + 3])

        @pl.when(b >= s_n)
        def _():
            first = (b - s_n) * step
            for at in range(0, step, batch):
                marked = mark[(first + at) // batch] != 0

                @pl.when(marked)
                def _():
                    for t in range(at, at + batch):
                        n = first + t
                        stage[t] = table[place(n), :].T * inv_ref[pl.ds(n, 1), :]

                @pl.when(jnp.logical_not(marked))
                def _():
                    for t in range(at, at + batch):
                        stage[t] = again_ref[t // l_n, 0, t % l_n] * inv_ref[pl.ds(first + t, 1), :]

            o_ref[0] = jnp.swapaxes(stage[...], 0, 1)

    smem = pl.BlockSpec(memory_space=pltpu.SMEM)
    return pl.pallas_call(
        kernel,
        grid=(s_n + outs,),
        in_specs=[smem] * 3
        + [
            pl.BlockSpec((1, 1, l_n, m_n, e_n), lambda b: (jnp.minimum(b, s_n - 1), 0, 0, 0, 0)),
            pl.BlockSpec((step // l_n, 1, l_n, m_n, e_n), lambda b: (jnp.maximum(b - s_n, 0), 0, 0, 0, 0)),
            pl.BlockSpec((nodes_n, e_n), lambda b: (0, 0)),
            pl.BlockSpec(memory_space=pl.ANY),
        ],
        out_specs=pl.BlockSpec((1, m_n, step, e_n), lambda b: (c, 0, jnp.maximum(b - s_n, 0), 0)),
        out_shape=jax.ShapeDtypeStruct(shape, jnp.float32),
        scratch_shapes=[pltpu.VMEM((rows_n + 8, m_n), jnp.float32), pltpu.VMEM((step, m_n, e_n), jnp.float32)],
        input_output_aliases={6: 0},
        compiler_params=params(),
        cost_estimate=pl.CostEstimate(
            flops=rows_n * LANES * 400, bytes_accessed=rows_n * m_n * 12, transcendentals=0
        ),
        name="finish",
    )(codes, bounds, shared, sums, sums, inverse, held)


def local_sums(modes, u, mass, pairs, edge_reps, first):
    s_n, c_n, l_n, m_n, e_n = modes.shape
    nodes_n = s_n * l_n
    rows_n = nodes_n * e_n
    step = min(8, l_n)
    per = l_n // step
    codes, bounds = pairs
    edges_n = edge_reps.shape[1]
    feats = c_n * m_n

    def kernel(codes, bnd, er, f_ref, u_ref, mass_ref, o_ref, low_ref, up_ref):
        b = pl.program_id(0)
        for t in range(step):
            node = b * step + t
            weight = mass_ref[pl.ds(node, 1), :]
            rows = [f_ref[0, c, t] + weight * u_ref[0, c, t] for c in range(c_n)]
            table = jnp.concatenate(rows, axis=0) if c_n > 1 else rows[0]
            o_ref[pl.ds(pl.multiple_of(node * e_n, e_n), e_n), :] = table.T

        @pl.when(b == pl.num_programs(0) - 1)
        def _():
            o_ref[pl.ds(rows_n, 8), :] = jnp.zeros((8, feats), jnp.float32)

            for k in range(CLASSES):
                sum_class(o_ref, codes, bnd[2 * k], bnd[2 * k + 1], False)
            sum_rest(o_ref, codes, bnd[2 * CLASSES], bnd[2 * CLASSES + 1])

            def edge(i, _):
                for side, to in enumerate((low_ref, up_ref)):
                    got = rows_of(o_ref, [er[side, i * BATCH + t] for t in range(BATCH)])
                    put_rows(to, [i * BATCH + t for t in range(BATCH)], got)
                return 0

            lax.fori_loop(0, edges_n // BATCH, edge, 0)

    smem = pl.BlockSpec(memory_space=pltpu.SMEM)
    where = lambda b: (b // per, 0, b % per, 0, 0)
    where_u = lambda b: (b // per, first // c_n, b % per, 0, 0)
    rim = pl.BlockSpec((edges_n, feats), lambda b: (0, 0))
    rim_shape = jax.ShapeDtypeStruct((edges_n, feats), jnp.float32)
    return pl.pallas_call(
        kernel,
        grid=(nodes_n // step,),
        in_specs=[smem] * 3
        + [
            pl.BlockSpec((1, c_n, step, m_n, e_n), where),
            pl.BlockSpec((1, c_n, step, m_n, e_n), where_u),
            pl.BlockSpec((nodes_n, e_n), lambda b: (0, 0)),
        ],
        out_specs=[pl.BlockSpec((rows_n + 8, feats), lambda b: (0, 0)), rim, rim],
        out_shape=[jax.ShapeDtypeStruct((rows_n + 8, feats), jnp.float32), rim_shape, rim_shape],
        compiler_params=params(),
        cost_estimate=pl.CostEstimate(
            flops=rows_n * LANES * 400, bytes_accessed=rows_n * LANES * 12, transcendentals=0
        ),
        name="local_sums",
    )(codes, bounds, edge_reps, modes, u, mass)


def spread(table, rims, pairs, edge_reps, inverse, held, shape, first, c_n):
    _, m_n, nodes_n, e_n = shape
    rows_n = nodes_n * e_n
    step = 8
    edges_n = edge_reps.shape[1]
    codes, bounds = pairs
    feats = c_n * m_n

    def kernel(codes, bnd, er, t_ref, low_ref, up_ref, inv_ref, *rest):
        o_ref, stage = rest[-2:]
        b = pl.program_id(0)

        @pl.when(b == 0)
        def _():
            def edge(i, _):
                for side, came in enumerate((low_ref, up_ref)):
                    spots = [er[side, i * BATCH + t] for t in range(BATCH)]
                    more = rows_of(came, [i * BATCH + t for t in range(BATCH)])
                    put_rows(t_ref, spots, [a + b for a, b in zip(rows_of(t_ref, spots), more)])
                return 0

            lax.fori_loop(0, edges_n // BATCH, edge, 0)
            hand_back(t_ref, codes, 0, bnd[2 * CLASSES] + bnd[2 * CLASSES + 1])

        for t in range(step):
            n = b * step + t
            rows = t_ref[pl.ds(pl.multiple_of(n * e_n, e_n), e_n), :].T
            scaled = rows * inv_ref[pl.ds(n, 1), :]
            for c in range(c_n):
                stage[c, t] = scaled[c * m_n : (c + 1) * m_n]
        for c in range(c_n):
            o_ref[c] = jnp.swapaxes(stage[c], 0, 1)

    smem = pl.BlockSpec(memory_space=pltpu.SMEM)
    rim = pl.BlockSpec((edges_n, feats), lambda b: (0, 0))
    in_specs = [smem] * 3 + [
        pl.BlockSpec((rows_n + 8, feats), lambda b: (0, 0)),
        rim,
        rim,
        pl.BlockSpec((nodes_n, e_n), lambda b: (0, 0)),
    ]
    args = [codes, bounds, edge_reps, table, *rims, inverse]
    aliases = {}
    if held is not None:
        in_specs.append(pl.BlockSpec(memory_space=pl.ANY))
        args.append(held)
        aliases = {len(args) - 1: 0}
    return pl.pallas_call(
        kernel,
        grid=(nodes_n // step,),
        in_specs=in_specs,
        out_specs=pl.BlockSpec((c_n, m_n, step, e_n), lambda b: (first // c_n, 0, b, 0)),
        out_shape=jax.ShapeDtypeStruct(shape, jnp.float32),
        scratch_shapes=[pltpu.VMEM((c_n, step, m_n, e_n), jnp.float32)],
        input_output_aliases=aliases,
        compiler_params=params(),
        cost_estimate=pl.CostEstimate(
            flops=rows_n * LANES * 400, bytes_accessed=rows_n * LANES * 12, transcendentals=0
        ),
        name="spread",
    )(*args)


def fill_up(values, multiple, filler):
    short = -values.shape[-1] % multiple
    pad = [(0, 0)] * (values.ndim - 1) + [(0, short)]
    return jnp.pad(values, pad, constant_values=filler)


def grouped(group, classes, member, rep, pairs_n):
    rows_n = group.shape[0]
    assert rows_n < 1 << PACK
    nobody = rows_n * (1 << PACK) + rows_n
    spare_group = jnp.arange(CLASSES * BATCH, dtype=jnp.int32) // BATCH
    _, codes = lax.sort(
        (
            jnp.concatenate([group.astype(jnp.int32), spare_group]),
            jnp.concatenate([member * (1 << PACK) + rep, jnp.full((CLASSES * BATCH,), nobody, jnp.int32)]),
        ),
        num_keys=1,
        is_stable=True,
    )
    spares = BATCH * jnp.minimum(jnp.arange(classes, dtype=jnp.int32), CLASSES)
    numbers = jnp.stack([jnp.sum(group == k, dtype=jnp.int32) for k in range(classes)])
    starts = jnp.cumsum(numbers) - numbers + spares
    bounds = jnp.stack([starts, numbers], axis=1).reshape(-1).astype(jnp.int32)
    length = pairs_n + CLASSES * BATCH
    return jnp.pad(codes[:length], (0, BATCH + -length % BATCH), constant_values=nobody), bounds


def pair_lists(ids, edges, parts, nodes_n):
    rows_n = ids.shape[0]
    place = jnp.arange(rows_n, dtype=jnp.int32)
    ids_sorted, member = lax.sort((ids, place), num_keys=1, is_stable=True)
    yes = jnp.ones((1,), bool)
    head = jnp.concatenate([yes, ids_sorted[1:] != ids_sorted[:-1]])
    last = jnp.concatenate([head[1:], yes])
    code = lax.cummax(jnp.where(head, place * rows_n + member, 0))
    rep = code % rows_n
    rank = place - code // rows_n
    pairs_n = rows_n - UNIQUE
    group = jnp.where((rank == 1) & last, 0, jnp.minimum(rank, CLASSES))
    group = jnp.where(rank == 0, CLASSES + 1, group)
    pairs = grouped(group, CLASSES + 1, member, rep, pairs_n)

    device = member // (rows_n // parts)
    device_first = head | jnp.concatenate([yes, device[1:] != device[:-1]])
    device_no = lax.cumsum(device_first.astype(jnp.int32))
    device_rank = device_no - lax.cummax(jnp.where(head, device_no, 0))
    most = lax.cummax(jnp.where(last, (rows_n - place) * parts + device_rank, 0), reverse=True) % parts
    group = jnp.where(device_first, jnp.minimum(device_rank, CLASSES), CLASSES + 1)
    group = jnp.where((rank == 1) & last & (device_rank == 1), 0, group)
    group = jnp.where((rank == 0) | (most == 0), CLASSES + 2, group)
    across = grouped(group, CLASSES + 2, member, rep, pairs_n)
    points = rows_n // nodes_n * min(8, nodes_n // parts)
    point_group = jnp.arange(rows_n // points, dtype=jnp.int32)
    shared = jnp.any((member // points == point_group[:, None]) & (most > 0), axis=1).astype(jnp.int32)

    flat = edges.reshape(-1)
    start = jnp.sum(ids_sorted[None, :] < flat[:, None], axis=1, dtype=jnp.int32)
    edge_reps = fill_up(member[start].reshape(edges.shape), BATCH, rows_n)
    return pairs, across, shared, edge_reps


def shifted(x, axis, step):
    count = lax.axis_size(axis)
    return lax.ppermute(x, axis, [(i, (i + step) % count) for i in range(count)])


def largest_of_partitions(x):
    step = 1
    while step < lax.axis_size("mesh"):
        x = jnp.maximum(x, shifted(x, "mesh", step))
        step *= 2
    return x


def total_over_four(x):
    total = x
    for step in range(1, lax.axis_size("four")):
        total = total + shifted(x, "four", step)
    return total


def swap_edges(low, up):
    return shifted(up, "mesh", 1), shifted(low, "mesh", -1)


def edge_takers(edges, connect, edge_reps, parts):
    here_n = connect.size // parts
    ids = fill_up(edges, BATCH, -1)
    has = jnp.any(ids[:, None, :, None] == connect.reshape(1, parts, 1, here_n), axis=3).astype(jnp.float32)
    theirs = jnp.stack(swap_edges(has[0], has[1]))
    spread_out = largest_of_partitions(jnp.max(theirs * (1.0 - has)).reshape(1))[0] > 0.5
    at_rep = jnp.where(edge_reps // here_n == lax.axis_index("four"), ids, -1)
    taken = jnp.where(spread_out, at_rep, ids)
    return ids.reshape(-1, 1), taken.reshape(-1, 1), spread_out


def inverse_mass(mass, ids, edges):
    summed = jnp.zeros((UNIQUE,), jnp.float32).at[ids].add(mass.reshape(-1))
    came = jnp.concatenate(swap_edges(summed[edges[0]], summed[edges[1]]))
    summed = summed.at[edges.reshape(-1)].add(came)
    return (1.0 / summed[ids]).reshape(mass.shape)


def exchange(x):
    return lax.all_to_all(x, "four", split_axis=0, concat_axis=0, tiled=True)


def body(adj_modes, base_flow, geometry, mass, connect, edge_nodes):
    comps, m_n, nodes_n, e_n = adj_modes.shape
    parts = lax.axis_size("four")
    l_n = nodes_n // parts
    mine = lax.axis_index("four") * l_n
    synth, along, analysis = plane_tables(PLANES)
    both_3 = left_form(np.concatenate([synth, along]))
    synth_3, analysis_3 = left_form(synth), left_form(analysis)
    together = lax.optimization_barrier
    spot = lambda n: (n // l_n, n % l_n)
    along_r = [[spot(NP * i + j) for i in range(NP)] for j in range(NP)]
    along_s = [[spot(NP * i + j) for j in range(NP)] for i in range(NP)]
    inside = [[(a, l + j) for j in range(NP)] for a in range(parts) for l in range(0, l_n, NP)]
    whole_rows = l_n % NP == 0

    u_first = adj_modes[0].reshape(m_n, parts, l_n, e_n).transpose(1, 0, 2, 3)
    u_first, adj_modes = together((u_first, adj_modes))
    first_here = exchange(u_first)

    u = node_major(adj_modes, parts)
    ur_a, ur_b = derivative(u, along_r, 0, 2), derivative(u, along_r, 2, 1)
    sent = [u[:, 1:], ur_a] + ([] if whole_rows else [derivative(u, along_s)])
    sent = jnp.concatenate(sent, axis=1)
    sent, u, ur_b, first_here, connect, edge_nodes, mass, base_flow = together(
        (sent, u, ur_b, first_here, connect, edge_nodes, mass, base_flow)
    )

    here = exchange(sent)
    edges = edge_nodes[0]
    ids = connect.reshape(-1)
    pairs, across, shared, edge_reps = pair_lists(ids, edges, parts, nodes_n)
    inverse = inverse_mass(mass, ids, edges)
    base = base_flow.transpose(0, 2, 1, 3)
    if l_n % 8 == 0:
        u0_here = node_major(first_here, 1).reshape(parts, 1, l_n, m_n, e_n)
    else:
        u0_here = first_here.transpose(0, 2, 1, 3)[:, None]
    us0_here = derivative(u0_here, inside, 0, 1) if whole_rows else None
    mass_here = lax.dynamic_slice_in_dim(mass, mine, l_n, 0)
    connect_here = lax.dynamic_slice_in_dim(connect, mine, l_n, 0)
    edge_ids, taken_ids, spread_out = edge_takers(edges, connect, edge_reps, parts)
    held = (here, ur_b, pairs, across, shared, edge_reps, inverse, base, u0_here, us0_here, edge_ids, taken_ids, spread_out)
    here, ur_b, pairs, across, shared, edge_reps, inverse, base, u0_here, us0_here, edge_ids, taken_ids, spread_out = together(held)

    ur_b_here = exchange(ur_b)
    us_here = derivative(here, inside, 0, 2) if whole_rows else here[:, 5:7]
    if not whole_rows:
        us0_here = here[:, 4:5]
    geo = lax.dynamic_slice_in_dim(geometry, mine, l_n, 1)
    vr, part = base_products(both_3, synth_3, u0_here, here, us0_here, us_here, base, geo)
    f_a = forcing_modes(synth_3, analysis_3, here, vr, part, mass_here, 2, 0, 2)
    f_a, ur_b_here = together((f_a, ur_b_here))

    modes_a = exchange(f_a)
    f_b, rims = forcing_and_rims(
        synth_3, analysis_3, ur_b_here, here, vr, part, mass_here, connect_here, edge_ids, 2, 1
    )
    half = rims.shape[0] // 2
    rims = jnp.concatenate(swap_edges(rims[:half], rims[half:]))
    rims = lax.cond(spread_out, total_over_four, lambda r: r, rims)
    f_b = own_sums(f_b, here, mass_here, connect_here, rims.T, taken_ids, 1)
    f_b, modes_a = together((f_b, modes_a))

    modes_b = exchange(f_b)
    table, *rims = local_sums(modes_a, u, mass, pairs, edge_reps, 0)
    out = spread(table, swap_edges(*rims), pairs, edge_reps, inverse, None, adj_modes.shape, 0, 2)
    modes_b, out = together((modes_b, out))

    return finish(modes_b, across, shared, inverse, out, adj_modes.shape, 2)


def solution(mesh):
    return jax.shard_map(
        body,
        mesh=mesh,
        in_specs=(
            P(None, "four", None, "mesh"),
            P(None, None, "four", "mesh"),
            P(None, None, "mesh"),
            P(None, "mesh"),
            P(None, "mesh"),
            P("mesh", None, None),
        ),
        out_specs=P(None, "four", None, "mesh"),
        check_vma=False,
    )
```

```python
import math

import jax
import jax.numpy as jnp
import ml_dtypes
import numpy as np
from jax import lax
from jax.experimental import pallas as pl
from jax.experimental.pallas import tpu as pltpu
from jax.sharding import PartitionSpec as P

NP = 8
PLANES = 256
UNIQUE = 12825
STEP_SIZE = 0.1
LANES = 128
BATCH = 32
CLASSES = 4
PACK = 15
BITS = 14
VMEM_LIMIT = 56 * 1024 * 1024


def legendre_values(degree, point):
    before = 1.0
    current = point
    for order in range(1, degree):
        after = ((2 * order + 1) * point * current - order * before) / (order + 1)
        before = current
        current = after
    return (current, before)


def gll_derivative(points_n):
    degree = points_n - 1
    points = []
    for index in range(points_n):
        point = -math.cos(math.pi * index / degree)
        for sweep in range(100):
            top_val, below_val = legendre_values(degree, point)
            point = point - (point * top_val - below_val) / (points_n * top_val)
        points.append(point)
    values = [legendre_values(degree, point)[0] for point in points]
    deriv_rows = []
    for row_index in range(points_n):
        row_vals = []
        for col_index in range(points_n):
            if row_index != col_index:
                row_vals.append(
                    values[row_index]
                    / (values[col_index] * (points[row_index] - points[col_index]))
                )
            else:
                row_vals.append(0.0)
        deriv_rows.append(row_vals)
    deriv_rows[0][0] = -degree * (degree + 1) / 4.0
    deriv_rows[degree][degree] = degree * (degree + 1) / 4.0
    return deriv_rows


def plane_tables(planes):
    plane = np.arange(planes)
    wave = plane // 2
    phase = ((plane[:, None] * wave[None, :]) % planes) * (2.0 * math.pi / planes)
    synth = np.where((plane % 2 == 1)[None, :], np.sin(phase), np.cos(phase))
    synth[:, 1] = 1 - 2 * (plane % 2)
    scales = np.where(wave == 0, 1.0 / planes, 2.0 / planes)
    analysis = synth.T * scales[:, None]
    number = wave * (2.0 / planes)
    along = np.zeros_like(synth)
    along[:, 1::2] = number[1::2] * synth[:, 0::2]
    along[:, 0::2] = -number[0::2] * synth[:, 1::2]
    along[:, :2] = 0.0
    return tuple(t.astype(np.float32) for t in (synth, along, analysis))


def params(**kw):
    return pltpu.CompilerParams(vmem_limit_bytes=VMEM_LIMIT, **kw)


def node_major(x, parts):
    c_n, m_n, n_n, e_n = x.shape
    l_n = n_n // parts
    rows = 16

    def kernel(x_ref, o_ref):
        for n in range(0, n_n, 8):
            turned = jnp.swapaxes(x_ref[0, :, n : n + 8, :], 0, 1)
            for t in range(8):
                o_ref[(n + t) // l_n, 0, (n + t) % l_n] = turned[t]

    return pl.pallas_call(
        kernel,
        grid=(c_n, m_n // rows),
        in_specs=[pl.BlockSpec((1, rows, n_n, e_n), lambda c, m: (c, m, 0, 0))],
        out_specs=pl.BlockSpec((parts, 1, l_n, rows, e_n), lambda c, m: (0, c, 0, m, 0)),
        out_shape=jax.ShapeDtypeStruct((parts, c_n, l_n, m_n, e_n), jnp.float32),
        compiler_params=params(),
        cost_estimate=pl.CostEstimate(flops=x.size, bytes_accessed=8 * x.size, transcendentals=0),
        name="node_major",
    )(x)


def derivative(x, groups, first=0, c_n=3):
    a_n, _, l_n, m_n, e_n = x.shape
    deriv = gll_derivative(NP)
    rows = 8

    def kernel(x_ref, o_ref):
        for line in groups:
            vals = [x_ref[a, 0, l] for a, l in line]
            for i, (a, l) in enumerate(line):
                total = deriv[i][0] * vals[0]
                for k in range(1, NP):
                    if deriv[i][k] != 0.0:
                        total = total + deriv[i][k] * vals[k]
                o_ref[a, 0, l] = total

    block = (a_n, 1, l_n, rows, e_n)
    size = a_n * c_n * l_n * m_n * e_n
    return pl.pallas_call(
        kernel,
        grid=(c_n, m_n // rows),
        in_specs=[pl.BlockSpec(block, lambda c, m: (0, first + c, 0, m, 0))],
        out_specs=pl.BlockSpec(block, lambda c, m: (0, c, 0, m, 0)),
        out_shape=jax.ShapeDtypeStruct((a_n, c_n, l_n, m_n, e_n), jnp.float32),
        compiler_params=params(),
        cost_estimate=pl.CostEstimate(flops=16 * size, bytes_accessed=8 * size, transcendentals=0),
        name="line_derivative",
    )(x)


def split(x):
    high = x.astype(jnp.bfloat16)
    return high, (x - high.astype(jnp.float32)).astype(jnp.bfloat16)


def left_form(table):
    high = table.astype(ml_dtypes.bfloat16)
    low = (table - high.astype(np.float32)).astype(ml_dtypes.bfloat16)
    return jnp.asarray(np.concatenate([high, high, low], axis=1))


def right_form(x):
    high, low = split(x)
    return jnp.concatenate([high, low, high], axis=0)


def product(left, right):
    return jnp.dot(left, right, preferred_element_type=jnp.float32)


def base_products(synth_along, synth, u_a, u_b, us_a, us_b, base, geo):
    s_n, _, l_n, m_n, e_n = u_a.shape
    p_n = base.shape[2]

    def kernel(both_ref, synth_ref, ua_ref, ub_ref, usa_ref, usb_ref, b_ref, g_ref, vr_ref, part_ref):
        l = pl.program_id(0)
        field = lambda i: b_ref[i, 0].astype(jnp.float32)
        g = [g_ref[i, pl.ds(l, 1), :] for i in range(4)]
        ux, uy = field(0), field(1)
        vr_ref[0] = ux * g[0] + uy * g[2]
        vs = ux * g[1] + uy * g[3]
        uz = field(2)
        phys = []
        for c in range(3):
            u_c = ua_ref[:, 0, 0] if c == 0 else ub_ref[:, c - 1, 0]
            us_c = usa_ref[:, 0, 0] if c == 0 else usb_ref[:, c - 1, 0]
            both = product(both_ref[...], right_form(u_c.reshape(s_n * m_n, e_n)))
            phys.append(both[:p_n])
            ds = product(synth_ref[...], right_form(us_c.reshape(s_n * m_n, e_n)))
            part_ref[c, 0] = -(vs * ds) - uz * both[p_n:]
        for c in range(3):
            part_ref[c, 0] += phys[0] * field(3 + 3 * c) + phys[1] * field(4 + 3 * c) + phys[2] * field(5 + 3 * c)

    one = pl.BlockSpec((s_n, 1, 1, m_n, e_n), lambda l: (0, 0, l, 0, 0))
    two = pl.BlockSpec((s_n, 2, 1, m_n, e_n), lambda l: (0, 0, l, 0, 0))
    return pl.pallas_call(
        kernel,
        grid=(l_n,),
        in_specs=[
            pl.BlockSpec((2 * p_n, 3 * p_n), lambda l: (0, 0)),
            pl.BlockSpec((p_n, 3 * p_n), lambda l: (0, 0)),
            one,
            two,
            one,
            two,
            pl.BlockSpec((12, 1, p_n, e_n), lambda l: (0, l, 0, 0)),
            pl.BlockSpec((4, l_n, e_n), lambda l: (0, 0, 0)),
        ],
        out_specs=[
            pl.BlockSpec((1, p_n, e_n), lambda l: (l, 0, 0)),
            pl.BlockSpec((3, 1, p_n, e_n), lambda l: (0, l, 0, 0)),
        ],
        out_shape=[
            jax.ShapeDtypeStruct((l_n, p_n, e_n), jnp.float32),
            jax.ShapeDtypeStruct((3, l_n, p_n, e_n), jnp.float32),
        ],
        compiler_params=params(),
        cost_estimate=pl.CostEstimate(
            flops=9 * 2 * 3 * l_n * p_n * p_n * e_n, bytes_accessed=l_n * p_n * e_n * 64, transcendentals=0
        ),
        name="base_products",
    )(synth_along, synth, u_a, u_b, us_a, us_b, base, geo)


def forcing_modes(synth, analysis, ur, vr, part, mass, held_at, first, c_n):
    s_n, _, l_n, m_n, e_n = ur.shape
    p_n = vr.shape[1]

    def kernel(synth_ref, analysis_ref, ur_ref, vr_ref, part_ref, mass_ref, o_ref):
        l = pl.program_id(1)
        dr = product(synth_ref[...], right_form(ur_ref[:, 0, 0].reshape(s_n * m_n, e_n)))
        forcing = part_ref[0, 0] - vr_ref[0] * dr
        modes = product(analysis_ref[...], right_form(forcing)) * (STEP_SIZE * mass_ref[pl.ds(l, 1), :])
        o_ref[:, 0, 0] = modes.reshape(s_n, m_n, e_n)

    whole = pl.BlockSpec((p_n, 3 * p_n), lambda c, l: (0, 0))
    block = (s_n, 1, 1, m_n, e_n)
    return pl.pallas_call(
        kernel,
        grid=(c_n, l_n),
        in_specs=[
            whole,
            whole,
            pl.BlockSpec(block, lambda c, l: (0, held_at + c, l, 0, 0)),
            pl.BlockSpec((1, p_n, e_n), lambda c, l: (l, 0, 0)),
            pl.BlockSpec((1, 1, p_n, e_n), lambda c, l: (first + c, l, 0, 0)),
            pl.BlockSpec((l_n, e_n), lambda c, l: (0, 0)),
        ],
        out_specs=pl.BlockSpec(block, lambda c, l: (0, c, l, 0, 0)),
        out_shape=jax.ShapeDtypeStruct((s_n, c_n, l_n, m_n, e_n), jnp.float32),
        compiler_params=params(),
        cost_estimate=pl.CostEstimate(
            flops=2 * 2 * 3 * c_n * l_n * p_n * p_n * e_n,
            bytes_accessed=c_n * l_n * p_n * e_n * 16,
            transcendentals=0,
        ),
        name="forcing_modes",
    )(synth, analysis, ur, vr, part, mass)


def forcing_and_rims(synth, analysis, ur, u, vr, part, mass, connect, edge_ids, c, u_at):
    s_n, _, l_n, m_n, e_n = ur.shape
    p_n = vr.shape[1]
    k_n = edge_ids.shape[0]

    def kernel(synth_ref, analysis_ref, ur_ref, u_ref, vr_ref, part_ref, mass_ref, conn_ref, id_ref, o_ref, rim_ref):
        l = pl.program_id(0)
        dr = product(synth_ref[...], right_form(ur_ref[:, 0, 0].reshape(s_n * m_n, e_n)))
        forcing = part_ref[0, 0] - vr_ref[0] * dr
        weight = mass_ref[pl.ds(l, 1), :]
        modes = product(analysis_ref[...], right_form(forcing)) * (STEP_SIZE * weight)
        o_ref[:, 0, 0] = modes.reshape(s_n, m_n, e_n)
        high, low = split(modes + weight * u_ref[:, 0, 0].reshape(s_n * m_n, e_n))
        here = jnp.where(id_ref[...] == conn_ref[pl.ds(l, 1), :], 1.0, 0.0).astype(jnp.bfloat16)
        sums = lax.dot_general(
            jnp.concatenate([here, here], axis=1),
            jnp.concatenate([high, low], axis=1),
            (((1,), (1,)), ((), ())),
            preferred_element_type=jnp.float32,
        )

        @pl.when(l == 0)
        def _():
            rim_ref[...] = sums

        @pl.when(l > 0)
        def _():
            rim_ref[...] += sums

    whole = pl.BlockSpec((p_n, 3 * p_n), lambda l: (0, 0))
    block = (s_n, 1, 1, m_n, e_n)
    nodes = pl.BlockSpec((l_n, e_n), lambda l: (0, 0))
    return pl.pallas_call(
        kernel,
        grid=(l_n,),
        in_specs=[
            whole,
            whole,
            pl.BlockSpec(block, lambda l: (0, 0, l, 0, 0)),
            pl.BlockSpec(block, lambda l: (0, u_at, l, 0, 0)),
            pl.BlockSpec((1, p_n, e_n), lambda l: (l, 0, 0)),
            pl.BlockSpec((1, 1, p_n, e_n), lambda l: (c, l, 0, 0)),
            nodes,
            nodes,
            pl.BlockSpec((k_n, 1), lambda l: (0, 0)),
        ],
        out_specs=[
            pl.BlockSpec(block, lambda l: (0, 0, l, 0, 0)),
            pl.BlockSpec((k_n, s_n * m_n), lambda l: (0, 0)),
        ],
        out_shape=[
            jax.ShapeDtypeStruct((s_n, 1, l_n, m_n, e_n), jnp.float32),
            jax.ShapeDtypeStruct((k_n, s_n * m_n), jnp.float32),
        ],
        compiler_params=params(),
        cost_estimate=pl.CostEstimate(
            flops=4 * 2 * 3 * l_n * p_n * p_n * e_n, bytes_accessed=l_n * p_n * e_n * 20, transcendentals=0
        ),
        name="forcing_and_rims",
    )(synth, analysis, ur, u, vr, part, mass, connect, edge_ids)


def own_sums(modes, u, mass, connect, rims, edge_ids, u_at):
    s_n, _, l_n, m_n, e_n = modes.shape
    k_n = edge_ids.shape[0]
    coefs = s_n * m_n

    def kernel(f_ref, u_ref, mass_ref, conn_ref, turned_ref, rim_ref, id_ref, o_ref, held):
        l = pl.program_id(0)

        @pl.when(l == 0)
        def _():
            def hold(k, _):
                weighted = f_ref[:, 0, k] + mass_ref[pl.ds(k, 1), :] * u_ref[:, 0, k]
                high, low = split(weighted.reshape(coefs, e_n))
                held[k] = jnp.concatenate([high, low], axis=1)
                return 0

            lax.fori_loop(0, l_n, hold, 0)

        mine = conn_ref[pl.ds(l, 1), :]

        def same(ids):
            there = jnp.where(ids == mine, 1.0, 0.0).astype(jnp.bfloat16)
            return jnp.concatenate([there, there], axis=0)

        high, low = split(rim_ref[...])
        total = product(jnp.concatenate([high, low], axis=1), same(id_ref[...]))
        total = lax.fori_loop(0, l_n, lambda k, t: t + product(held[k], same(turned_ref[k])), total)
        o_ref[:, 0, 0] = total.reshape(s_n, m_n, e_n)

    def whole(*shape):
        return pl.BlockSpec(shape, lambda l: (0,) * len(shape))

    return pl.pallas_call(
        kernel,
        grid=(l_n,),
        in_specs=[
            whole(s_n, 1, l_n, m_n, e_n),
            pl.BlockSpec((s_n, 1, l_n, m_n, e_n), lambda l: (0, u_at, 0, 0, 0)),
            whole(l_n, e_n),
            whole(l_n, e_n),
            whole(l_n, e_n, 1),
            whole(coefs, k_n),
            whole(k_n, 1),
        ],
        out_specs=pl.BlockSpec((s_n, 1, 1, m_n, e_n), lambda l: (0, 0, l, 0, 0)),
        out_shape=jax.ShapeDtypeStruct(modes.shape, jnp.float32),
        scratch_shapes=[pltpu.VMEM((l_n, coefs, 2 * e_n), jnp.bfloat16)],
        compiler_params=params(),
        cost_estimate=pl.CostEstimate(
            flops=4 * l_n * l_n * coefs * e_n * e_n, bytes_accessed=12 * modes.size, transcendentals=0
        ),
        name="own_sums",
    )(modes, u, mass, connect, connect[:, :, None], rims, edge_ids)


def rows_of(ref, places):
    return [ref[pl.ds(r, 1), :] for r in places]


def put_rows(ref, places, rows):
    for r, row in zip(places, rows):
        ref[pl.ds(r, 1), :] = row


def some_pairs(codes, at, number):
    found = [codes[at + t] for t in range(number)]
    return [code >> PACK for code in found], [code & (1 << PACK) - 1 for code in found]


def sum_class(ref, codes, start, number, both):
    def batch(i, _):
        others, heads = some_pairs(codes, start + i * BATCH, BATCH)
        sums = [a + b for a, b in zip(rows_of(ref, heads), rows_of(ref, others))]
        put_rows(ref, heads, sums)
        if both:
            put_rows(ref, others, sums)
        return 0

    lax.fori_loop(0, pl.cdiv(number, BATCH), batch, 0)


def sum_rest(ref, codes, start, number):
    def one(i, _):
        others, heads = some_pairs(codes, start + i, 1)
        put_rows(ref, heads, [rows_of(ref, heads)[0] + rows_of(ref, others)[0]])
        return 0

    lax.fori_loop(0, number, one, 0)


def hand_back(ref, codes, start, end):
    def batch(i, _):
        others, heads = some_pairs(codes, start + i * BATCH, BATCH)
        put_rows(ref, others, rows_of(ref, heads))
        return 0

    lax.fori_loop(0, pl.cdiv(end - start, BATCH), batch, 0)


def finish(sums, pairs, shared, inverse, held, shape, c):
    s_n, _, l_n, m_n, e_n = sums.shape
    _, _, nodes_n, _ = shape
    rows_n = nodes_n * e_n
    codes, bounds = pairs
    batch = nodes_n // shared.shape[0]
    step = max(8, l_n)
    outs = nodes_n // step

    def kernel(codes, bnd, mark, f_ref, again_ref, inv_ref, _, o_ref, table, stage):
        b = pl.program_id(0)

        def place(node):
            return pl.ds(pl.multiple_of(node * e_n, e_n), e_n)

        @pl.when(b < s_n)
        def _():
            for at in range(0, l_n, batch):

                @pl.when(mark[(b * l_n + at) // batch] != 0)
                def _():
                    for t in range(at, at + batch):
                        table[place(b * l_n + t), :] = f_ref[0, 0, t].T

        @pl.when(b == s_n - 1)
        def _():
            table[pl.ds(rows_n, 8), :] = jnp.zeros((8, m_n), jnp.float32)
            for k in range(CLASSES):
                sum_class(table, codes, bnd[2 * k], bnd[2 * k + 1], k == 0)
            sum_rest(table, codes, bnd[2 * CLASSES], bnd[2 * CLASSES + 1])
            hand_back(table, codes, bnd[2], bnd[2 * CLASSES + 2] + bnd[2 * CLASSES + 3])

        @pl.when(b >= s_n)
        def _():
            first = (b - s_n) * step
            for at in range(0, step, batch):
                marked = mark[(first + at) // batch] != 0

                @pl.when(marked)
                def _():
                    for t in range(at, at + batch):
                        n = first + t
                        stage[t] = table[place(n), :].T * inv_ref[pl.ds(n, 1), :]

                @pl.when(jnp.logical_not(marked))
                def _():
                    for t in range(at, at + batch):
                        stage[t] = again_ref[t // l_n, 0, t % l_n] * inv_ref[pl.ds(first + t, 1), :]

            o_ref[0] = jnp.swapaxes(stage[...], 0, 1)

    smem = pl.BlockSpec(memory_space=pltpu.SMEM)
    return pl.pallas_call(
        kernel,
        grid=(s_n + outs,),
        in_specs=[smem] * 3
        + [
            pl.BlockSpec((1, 1, l_n, m_n, e_n), lambda b: (jnp.minimum(b, s_n - 1), 0, 0, 0, 0)),
            pl.BlockSpec((step // l_n, 1, l_n, m_n, e_n), lambda b: (jnp.maximum(b - s_n, 0), 0, 0, 0, 0)),
            pl.BlockSpec((nodes_n, e_n), lambda b: (0, 0)),
            pl.BlockSpec(memory_space=pl.ANY),
        ],
        out_specs=pl.BlockSpec((1, m_n, step, e_n), lambda b: (c, 0, jnp.maximum(b - s_n, 0), 0)),
        out_shape=jax.ShapeDtypeStruct(shape, jnp.float32),
        scratch_shapes=[pltpu.VMEM((rows_n + 8, m_n), jnp.float32), pltpu.VMEM((step, m_n, e_n), jnp.float32)],
        input_output_aliases={6: 0},
        compiler_params=params(),
        cost_estimate=pl.CostEstimate(
            flops=rows_n * LANES * 400, bytes_accessed=rows_n * m_n * 12, transcendentals=0
        ),
        name="finish",
    )(codes, bounds, shared, sums, sums, inverse, held)


def local_sums(modes, u, mass, pairs, edge_reps, first):
    s_n, c_n, l_n, m_n, e_n = modes.shape
    nodes_n = s_n * l_n
    rows_n = nodes_n * e_n
    step = min(8, l_n)
    per = l_n // step
    codes, bounds = pairs
    edges_n = edge_reps.shape[1]
    feats = c_n * m_n

    def kernel(codes, bnd, er, f_ref, u_ref, mass_ref, o_ref, low_ref, up_ref):
        b = pl.program_id(0)
        for t in range(step):
            node = b * step + t
            weight = mass_ref[pl.ds(node, 1), :]
            rows = [f_ref[0, c, t] + weight * u_ref[0, c, t] for c in range(c_n)]
            table = jnp.concatenate(rows, axis=0) if c_n > 1 else rows[0]
            o_ref[pl.ds(pl.multiple_of(node * e_n, e_n), e_n), :] = table.T

        @pl.when(b == pl.num_programs(0) - 1)
        def _():
            o_ref[pl.ds(rows_n, 8), :] = jnp.zeros((8, feats), jnp.float32)

            for k in range(CLASSES):
                sum_class(o_ref, codes, bnd[2 * k], bnd[2 * k + 1], False)
            sum_rest(o_ref, codes, bnd[2 * CLASSES], bnd[2 * CLASSES + 1])

            def edge(i, _):
                for side, to in enumerate((low_ref, up_ref)):
                    got = rows_of(o_ref, [er[side, i * BATCH + t] for t in range(BATCH)])
                    put_rows(to, [i * BATCH + t for t in range(BATCH)], got)
                return 0

            lax.fori_loop(0, edges_n // BATCH, edge, 0)

    smem = pl.BlockSpec(memory_space=pltpu.SMEM)
    where = lambda b: (b // per, 0, b % per, 0, 0)
    where_u = lambda b: (b // per, first // c_n, b % per, 0, 0)
    rim = pl.BlockSpec((edges_n, feats), lambda b: (0, 0))
    rim_shape = jax.ShapeDtypeStruct((edges_n, feats), jnp.float32)
    return pl.pallas_call(
        kernel,
        grid=(nodes_n // step,),
        in_specs=[smem] * 3
        + [
            pl.BlockSpec((1, c_n, step, m_n, e_n), where),
            pl.BlockSpec((1, c_n, step, m_n, e_n), where_u),
            pl.BlockSpec((nodes_n, e_n), lambda b: (0, 0)),
        ],
        out_specs=[pl.BlockSpec((rows_n + 8, feats), lambda b: (0, 0)), rim, rim],
        out_shape=[jax.ShapeDtypeStruct((rows_n + 8, feats), jnp.float32), rim_shape, rim_shape],
        compiler_params=params(),
        cost_estimate=pl.CostEstimate(
            flops=rows_n * LANES * 400, bytes_accessed=rows_n * LANES * 12, transcendentals=0
        ),
        name="local_sums",
    )(codes, bounds, edge_reps, modes, u, mass)


def spread(table, rims, pairs, edge_reps, inverse, held, shape, first, c_n):
    _, m_n, nodes_n, e_n = shape
    rows_n = nodes_n * e_n
    step = 8
    edges_n = edge_reps.shape[1]
    codes, bounds = pairs
    feats = c_n * m_n

    def kernel(codes, bnd, er, t_ref, low_ref, up_ref, inv_ref, *rest):
        o_ref, stage = rest[-2:]
        b = pl.program_id(0)

        @pl.when(b == 0)
        def _():
            def edge(i, _):
                for side, came in enumerate((low_ref, up_ref)):
                    spots = [er[side, i * BATCH + t] for t in range(BATCH)]
                    more = rows_of(came, [i * BATCH + t for t in range(BATCH)])
                    put_rows(t_ref, spots, [a + b for a, b in zip(rows_of(t_ref, spots), more)])
                return 0

            lax.fori_loop(0, edges_n // BATCH, edge, 0)
            hand_back(t_ref, codes, 0, bnd[2 * CLASSES] + bnd[2 * CLASSES + 1])

        for t in range(step):
            n = b * step + t
            rows = t_ref[pl.ds(pl.multiple_of(n * e_n, e_n), e_n), :].T
            scaled = rows * inv_ref[pl.ds(n, 1), :]
            for c in range(c_n):
                stage[c, t] = scaled[c * m_n : (c + 1) * m_n]
        for c in range(c_n):
            o_ref[c] = jnp.swapaxes(stage[c], 0, 1)

    smem = pl.BlockSpec(memory_space=pltpu.SMEM)
    rim = pl.BlockSpec((edges_n, feats), lambda b: (0, 0))
    in_specs = [smem] * 3 + [
        pl.BlockSpec((rows_n + 8, feats), lambda b: (0, 0)),
        rim,
        rim,
        pl.BlockSpec((nodes_n, e_n), lambda b: (0, 0)),
    ]
    args = [codes, bounds, edge_reps, table, *rims, inverse]
    aliases = {}
    if held is not None:
        in_specs.append(pl.BlockSpec(memory_space=pl.ANY))
        args.append(held)
        aliases = {len(args) - 1: 0}
    return pl.pallas_call(
        kernel,
        grid=(nodes_n // step,),
        in_specs=in_specs,
        out_specs=pl.BlockSpec((c_n, m_n, step, e_n), lambda b: (first // c_n, 0, b, 0)),
        out_shape=jax.ShapeDtypeStruct(shape, jnp.float32),
        scratch_shapes=[pltpu.VMEM((c_n, step, m_n, e_n), jnp.float32)],
        input_output_aliases=aliases,
        compiler_params=params(),
        cost_estimate=pl.CostEstimate(
            flops=rows_n * LANES * 400, bytes_accessed=rows_n * LANES * 12, transcendentals=0
        ),
        name="spread",
    )(*args)


def fill_up(values, multiple, filler):
    short = -values.shape[-1] % multiple
    pad = [(0, 0)] * (values.ndim - 1) + [(0, short)]
    return jnp.pad(values, pad, constant_values=filler)


def grouped(group, classes, member, rep, pairs_n):
    rows_n = group.shape[0]
    assert rows_n <= 1 << BITS and classes < 8
    ones = (1 << 2 * BITS) - 1
    nobody = rows_n * (1 << PACK) + rows_n
    spare = (jnp.arange(CLASSES * BATCH, dtype=jnp.int32) // BATCH) * (ones + 1) + ones
    keys = group.astype(jnp.int32) * (ones + 1) + member * (1 << BITS) + rep
    length = pairs_n + CLASSES * BATCH
    keys = lax.sort(jnp.concatenate([keys, spare]), is_stable=False)[:length] & ones
    codes = jnp.where(keys == ones, nobody, (keys >> BITS) * (1 << PACK) + (keys & (1 << BITS) - 1))
    spares = BATCH * jnp.minimum(jnp.arange(classes, dtype=jnp.int32), CLASSES)
    numbers = jnp.sum(group[None, :] == jnp.arange(classes, dtype=jnp.int32)[:, None], axis=1, dtype=jnp.int32)
    lower = jnp.tri(classes, k=-1, dtype=jnp.int32)
    starts = jnp.sum(lower * numbers[None, :], axis=1) + spares
    bounds = jnp.stack([starts, numbers], axis=1).reshape(-1).astype(jnp.int32)
    return jnp.pad(codes, (0, BATCH + -length % BATCH), constant_values=nobody), bounds


def pair_lists(ids, edges, parts, nodes_n):
    rows_n = ids.shape[0]
    place = jnp.arange(rows_n, dtype=jnp.int32)
    assert rows_n <= 1 << BITS and UNIQUE <= 1 << BITS
    keys = lax.sort(ids * (1 << BITS) + place, is_stable=False)
    ids_sorted, member = keys >> BITS, keys & (1 << BITS) - 1
    yes = jnp.ones((1,), bool)
    head = jnp.concatenate([yes, ids_sorted[1:] != ids_sorted[:-1]])
    last = jnp.concatenate([head[1:], yes])
    code = lax.cummax(jnp.where(head, place * rows_n + member, 0))
    rep = code % rows_n
    rank = place - code // rows_n
    pairs_n = rows_n - UNIQUE
    group = jnp.where((rank == 1) & last, 0, jnp.minimum(rank, CLASSES))
    group = jnp.where(rank == 0, CLASSES + 1, group)
    pairs = grouped(group, CLASSES + 1, member, rep, pairs_n)

    device = member // (rows_n // parts)
    device_first = head | jnp.concatenate([yes, device[1:] != device[:-1]])
    device_no = lax.cumsum(device_first.astype(jnp.int32))
    device_rank = device_no - lax.cummax(jnp.where(head, device_no, 0))
    most = lax.cummax(jnp.where(last, (rows_n - place) * parts + device_rank, 0), reverse=True) % parts
    group = jnp.where(device_first, jnp.minimum(device_rank, CLASSES), CLASSES + 1)
    group = jnp.where((rank == 1) & last & (device_rank == 1), 0, group)
    group = jnp.where((rank == 0) | (most == 0), CLASSES + 2, group)
    across = grouped(group, CLASSES + 2, member, rep, pairs_n)
    points = rows_n // nodes_n * min(8, nodes_n // parts)
    point_group = jnp.arange(rows_n // points, dtype=jnp.int32)
    shared = jnp.any((member // points == point_group[:, None]) & (most > 0), axis=1).astype(jnp.int32)

    flat = edges.reshape(-1)
    start = jnp.sum(ids_sorted[None, :] < flat[:, None], axis=1, dtype=jnp.int32)
    edge_reps = fill_up(member[start].reshape(edges.shape), BATCH, rows_n)
    return pairs, across, shared, edge_reps


def shifted(x, axis, step):
    count = lax.axis_size(axis)
    return lax.ppermute(x, axis, [(i, (i + step) % count) for i in range(count)])


def largest_of_partitions(x):
    step = 1
    while step < lax.axis_size("mesh"):
        x = jnp.maximum(x, shifted(x, "mesh", step))
        step *= 2
    return x


def total_over_four(x):
    total = x
    for step in range(1, lax.axis_size("four")):
        total = total + shifted(x, "four", step)
    return total


def swap_edges(low, up):
    return shifted(up, "mesh", 1), shifted(low, "mesh", -1)


def edge_takers(edges, connect, edge_reps, parts):
    here_n = connect.size // parts
    ids = fill_up(edges, BATCH, -1)
    has = jnp.any(ids[:, None, :, None] == connect.reshape(1, parts, 1, here_n), axis=3).astype(jnp.float32)
    theirs = jnp.stack(swap_edges(has[0], has[1]))
    spread_out = largest_of_partitions(jnp.max(theirs * (1.0 - has)).reshape(1))[0] > 0.5
    at_rep = jnp.where(edge_reps // here_n == lax.axis_index("four"), ids, -1)
    taken = jnp.where(spread_out, at_rep, ids)
    return ids.reshape(-1, 1), taken.reshape(-1, 1), spread_out


def inverse_mass(mass, ids, edges):
    summed = jnp.zeros((UNIQUE,), jnp.float32).at[ids].add(mass.reshape(-1))
    came = jnp.concatenate(swap_edges(summed[edges[0]], summed[edges[1]]))
    summed = summed.at[edges.reshape(-1)].add(came)
    return (1.0 / summed[ids]).reshape(mass.shape)


def exchange(x):
    return lax.all_to_all(x, "four", split_axis=0, concat_axis=0, tiled=True)


def body(adj_modes, base_flow, geometry, mass, connect, edge_nodes):
    comps, m_n, nodes_n, e_n = adj_modes.shape
    parts = lax.axis_size("four")
    l_n = nodes_n // parts
    mine = lax.axis_index("four") * l_n
    synth, along, analysis = plane_tables(PLANES)
    both_3 = left_form(np.concatenate([synth, along]))
    synth_3, analysis_3 = left_form(synth), left_form(analysis)
    together = lax.optimization_barrier
    spot = lambda n: (n // l_n, n % l_n)
    along_r = [[spot(NP * i + j) for i in range(NP)] for j in range(NP)]
    along_s = [[spot(NP * i + j) for j in range(NP)] for i in range(NP)]
    inside = [[(a, l + j) for j in range(NP)] for a in range(parts) for l in range(0, l_n, NP)]
    whole_rows = l_n % NP == 0

    u_first = adj_modes[0].reshape(m_n, parts, l_n, e_n).transpose(1, 0, 2, 3)
    u_first, adj_modes = together((u_first, adj_modes))
    first_here = exchange(u_first)

    u = node_major(adj_modes, parts)
    ur_a, ur_b = derivative(u, along_r, 0, 2), derivative(u, along_r, 2, 1)
    sent = [u[:, 1:], ur_a] + ([] if whole_rows else [derivative(u, along_s)])
    sent = jnp.concatenate(sent, axis=1)
    sent, u, ur_b, first_here, connect, edge_nodes, mass, base_flow = together(
        (sent, u, ur_b, first_here, connect, edge_nodes, mass, base_flow)
    )

    here = exchange(sent)
    edges = edge_nodes[0]
    ids = connect.reshape(-1)
    pairs, across, shared, edge_reps = pair_lists(ids, edges, parts, nodes_n)
    inverse = inverse_mass(mass, ids, edges)
    base = base_flow.transpose(0, 2, 1, 3)
    if l_n % 8 == 0:
        u0_here = node_major(first_here, 1).reshape(parts, 1, l_n, m_n, e_n)
    else:
        u0_here = first_here.transpose(0, 2, 1, 3)[:, None]
    us0_here = derivative(u0_here, inside, 0, 1) if whole_rows else None
    mass_here = lax.dynamic_slice_in_dim(mass, mine, l_n, 0)
    connect_here = lax.dynamic_slice_in_dim(connect, mine, l_n, 0)
    edge_ids, taken_ids, spread_out = edge_takers(edges, connect, edge_reps, parts)
    held = (here, ur_b, pairs, across, shared, edge_reps, inverse, base, u0_here, us0_here, edge_ids, taken_ids, spread_out)
    here, ur_b, pairs, across, shared, edge_reps, inverse, base, u0_here, us0_here, edge_ids, taken_ids, spread_out = together(held)

    ur_b_here = exchange(ur_b)
    us_here = derivative(here, inside, 0, 2) if whole_rows else here[:, 5:7]
    if not whole_rows:
        us0_here = here[:, 4:5]
    geo = lax.dynamic_slice_in_dim(geometry, mine, l_n, 1)
    vr, part = base_products(both_3, synth_3, u0_here, here, us0_here, us_here, base, geo)
    f_a = forcing_modes(synth_3, analysis_3, here, vr, part, mass_here, 2, 0, 2)
    f_a, ur_b_here = together((f_a, ur_b_here))

    modes_a = exchange(f_a)
    f_b, rims = forcing_and_rims(
        synth_3, analysis_3, ur_b_here, here, vr, part, mass_here, connect_here, edge_ids, 2, 1
    )
    half = rims.shape[0] // 2
    rims = jnp.concatenate(swap_edges(rims[:half], rims[half:]))
    rims = lax.cond(spread_out, total_over_four, lambda r: r, rims)
    f_b = own_sums(f_b, here, mass_here, connect_here, rims.T, taken_ids, 1)
    f_b, modes_a = together((f_b, modes_a))

    modes_b = exchange(f_b)
    table, *rims = local_sums(modes_a, u, mass, pairs, edge_reps, 0)
    out = spread(table, swap_edges(*rims), pairs, edge_reps, inverse, None, adj_modes.shape, 0, 2)
    modes_b, out = together((modes_b, out))

    return finish(modes_b, across, shared, inverse, out, adj_modes.shape, 2)


def solution(mesh):
    return jax.shard_map(
        body,
        mesh=mesh,
        in_specs=(
            P(None, "four", None, "mesh"),
            P(None, None, "four", "mesh"),
            P(None, None, "mesh"),
            P(None, "mesh"),
            P(None, "mesh"),
            P("mesh", None, None),
        ),
        out_specs=P(None, "four", None, "mesh"),
        check_vma=False,
    )
```

```python
import math

import jax
import jax.numpy as jnp
import ml_dtypes
import numpy as np
from jax import lax
from jax.experimental import pallas as pl
from jax.experimental.pallas import tpu as pltpu
from jax.sharding import PartitionSpec as P

NP = 8
PLANES = 256
UNIQUE = 12825
STEP_SIZE = 0.1
LANES = 128
BATCH = 8
CLASSES = 4
PACK = 15
BITS = 14
VMEM_LIMIT = 56 * 1024 * 1024


def legendre_values(degree, point):
    before = 1.0
    current = point
    for order in range(1, degree):
        after = ((2 * order + 1) * point * current - order * before) / (order + 1)
        before = current
        current = after
    return (current, before)


def gll_derivative(points_n):
    degree = points_n - 1
    points = []
    for index in range(points_n):
        point = -math.cos(math.pi * index / degree)
        for sweep in range(100):
            top_val, below_val = legendre_values(degree, point)
            point = point - (point * top_val - below_val) / (points_n * top_val)
        points.append(point)
    values = [legendre_values(degree, point)[0] for point in points]
    deriv_rows = []
    for row_index in range(points_n):
        row_vals = []
        for col_index in range(points_n):
            if row_index != col_index:
                row_vals.append(
                    values[row_index]
                    / (values[col_index] * (points[row_index] - points[col_index]))
                )
            else:
                row_vals.append(0.0)
        deriv_rows.append(row_vals)
    deriv_rows[0][0] = -degree * (degree + 1) / 4.0
    deriv_rows[degree][degree] = degree * (degree + 1) / 4.0
    return deriv_rows


def plane_tables(planes):
    plane = np.arange(planes)
    wave = plane // 2
    phase = ((plane[:, None] * wave[None, :]) % planes) * (2.0 * math.pi / planes)
    synth = np.where((plane % 2 == 1)[None, :], np.sin(phase), np.cos(phase))
    synth[:, 1] = 1 - 2 * (plane % 2)
    scales = np.where(wave == 0, 1.0 / planes, 2.0 / planes)
    analysis = synth.T * scales[:, None]
    number = wave * (2.0 / planes)
    along = np.zeros_like(synth)
    along[:, 1::2] = number[1::2] * synth[:, 0::2]
    along[:, 0::2] = -number[0::2] * synth[:, 1::2]
    along[:, :2] = 0.0
    return tuple(t.astype(np.float32) for t in (synth, along, analysis))


def params(**kw):
    return pltpu.CompilerParams(vmem_limit_bytes=VMEM_LIMIT, **kw)


def node_major(x, parts):
    c_n, m_n, n_n, e_n = x.shape
    l_n = n_n // parts
    rows = 16

    def kernel(x_ref, o_ref):
        for n in range(0, n_n, 8):
            turned = jnp.swapaxes(x_ref[0, :, n : n + 8, :], 0, 1)
            for t in range(8):
                o_ref[(n + t) // l_n, 0, (n + t) % l_n] = turned[t]

    return pl.pallas_call(
        kernel,
        grid=(c_n, m_n // rows),
        in_specs=[pl.BlockSpec((1, rows, n_n, e_n), lambda c, m: (c, m, 0, 0))],
        out_specs=pl.BlockSpec((parts, 1, l_n, rows, e_n), lambda c, m: (0, c, 0, m, 0)),
        out_shape=jax.ShapeDtypeStruct((parts, c_n, l_n, m_n, e_n), jnp.float32),
        compiler_params=params(),
        cost_estimate=pl.CostEstimate(flops=x.size, bytes_accessed=8 * x.size, transcendentals=0),
        name="node_major",
    )(x)


def derivative(x, groups, first=0, c_n=3):
    a_n, _, l_n, m_n, e_n = x.shape
    deriv = gll_derivative(NP)
    rows = 8

    def kernel(x_ref, o_ref):
        for line in groups:
            vals = [x_ref[a, 0, l] for a, l in line]
            for i, (a, l) in enumerate(line):
                total = deriv[i][0] * vals[0]
                for k in range(1, NP):
                    if deriv[i][k] != 0.0:
                        total = total + deriv[i][k] * vals[k]
                o_ref[a, 0, l] = total

    block = (a_n, 1, l_n, rows, e_n)
    size = a_n * c_n * l_n * m_n * e_n
    return pl.pallas_call(
        kernel,
        grid=(c_n, m_n // rows),
        in_specs=[pl.BlockSpec(block, lambda c, m: (0, first + c, 0, m, 0))],
        out_specs=pl.BlockSpec(block, lambda c, m: (0, c, 0, m, 0)),
        out_shape=jax.ShapeDtypeStruct((a_n, c_n, l_n, m_n, e_n), jnp.float32),
        compiler_params=params(),
        cost_estimate=pl.CostEstimate(flops=16 * size, bytes_accessed=8 * size, transcendentals=0),
        name="line_derivative",
    )(x)


def split(x):
    high = x.astype(jnp.bfloat16)
    return high, (x - high.astype(jnp.float32)).astype(jnp.bfloat16)


def left_form(table):
    high = table.astype(ml_dtypes.bfloat16)
    low = (table - high.astype(np.float32)).astype(ml_dtypes.bfloat16)
    return jnp.asarray(np.concatenate([high, high, low], axis=1))


def right_form(x):
    high, low = split(x)
    return jnp.concatenate([high, low, high], axis=0)


def product(left, right):
    return jnp.dot(left, right, preferred_element_type=jnp.float32)


def base_products(synth_along, synth, u_a, u_b, us_a, us_b, base, geo):
    s_n, _, l_n, m_n, e_n = u_a.shape
    p_n = base.shape[2]

    def kernel(both_ref, synth_ref, ua_ref, ub_ref, usa_ref, usb_ref, b_ref, g_ref, vr_ref, part_ref):
        l = pl.program_id(0)
        field = lambda i: b_ref[i, 0].astype(jnp.float32)
        g = [g_ref[i, pl.ds(l, 1), :] for i in range(4)]
        ux, uy = field(0), field(1)
        vr_ref[0] = ux * g[0] + uy * g[2]
        vs = ux * g[1] + uy * g[3]
        uz = field(2)
        phys = []
        for c in range(3):
            u_c = ua_ref[:, 0, 0] if c == 0 else ub_ref[:, c - 1, 0]
            us_c = usa_ref[:, 0, 0] if c == 0 else usb_ref[:, c - 1, 0]
            both = product(both_ref[...], right_form(u_c.reshape(s_n * m_n, e_n)))
            phys.append(both[:p_n])
            ds = product(synth_ref[...], right_form(us_c.reshape(s_n * m_n, e_n)))
            part_ref[c, 0] = -(vs * ds) - uz * both[p_n:]
        for c in range(3):
            part_ref[c, 0] += phys[0] * field(3 + 3 * c) + phys[1] * field(4 + 3 * c) + phys[2] * field(5 + 3 * c)

    one = pl.BlockSpec((s_n, 1, 1, m_n, e_n), lambda l: (0, 0, l, 0, 0))
    two = pl.BlockSpec((s_n, 2, 1, m_n, e_n), lambda l: (0, 0, l, 0, 0))
    return pl.pallas_call(
        kernel,
        grid=(l_n,),
        in_specs=[
            pl.BlockSpec((2 * p_n, 3 * p_n), lambda l: (0, 0)),
            pl.BlockSpec((p_n, 3 * p_n), lambda l: (0, 0)),
            one,
            two,
            one,
            two,
            pl.BlockSpec((12, 1, p_n, e_n), lambda l: (0, l, 0, 0)),
            pl.BlockSpec((4, l_n, e_n), lambda l: (0, 0, 0)),
        ],
        out_specs=[
            pl.BlockSpec((1, p_n, e_n), lambda l: (l, 0, 0)),
            pl.BlockSpec((3, 1, p_n, e_n), lambda l: (0, l, 0, 0)),
        ],
        out_shape=[
            jax.ShapeDtypeStruct((l_n, p_n, e_n), jnp.float32),
            jax.ShapeDtypeStruct((3, l_n, p_n, e_n), jnp.float32),
        ],
        compiler_params=params(),
        cost_estimate=pl.CostEstimate(
            flops=9 * 2 * 3 * l_n * p_n * p_n * e_n, bytes_accessed=l_n * p_n * e_n * 64, transcendentals=0
        ),
        name="base_products",
    )(synth_along, synth, u_a, u_b, us_a, us_b, base, geo)


def forcing_modes(synth, analysis, ur, vr, part, mass, held_at, first, c_n):
    s_n, _, l_n, m_n, e_n = ur.shape
    p_n = vr.shape[1]

    def kernel(synth_ref, analysis_ref, ur_ref, vr_ref, part_ref, mass_ref, o_ref):
        l = pl.program_id(1)
        dr = product(synth_ref[...], right_form(ur_ref[:, 0, 0].reshape(s_n * m_n, e_n)))
        forcing = part_ref[0, 0] - vr_ref[0] * dr
        modes = product(analysis_ref[...], right_form(forcing)) * (STEP_SIZE * mass_ref[pl.ds(l, 1), :])
        o_ref[:, 0, 0] = modes.reshape(s_n, m_n, e_n)

    whole = pl.BlockSpec((p_n, 3 * p_n), lambda c, l: (0, 0))
    block = (s_n, 1, 1, m_n, e_n)
    return pl.pallas_call(
        kernel,
        grid=(c_n, l_n),
        in_specs=[
            whole,
            whole,
            pl.BlockSpec(block, lambda c, l: (0, held_at + c, l, 0, 0)),
            pl.BlockSpec((1, p_n, e_n), lambda c, l: (l, 0, 0)),
            pl.BlockSpec((1, 1, p_n, e_n), lambda c, l: (first + c, l, 0, 0)),
            pl.BlockSpec((l_n, e_n), lambda c, l: (0, 0)),
        ],
        out_specs=pl.BlockSpec(block, lambda c, l: (0, c, l, 0, 0)),
        out_shape=jax.ShapeDtypeStruct((s_n, c_n, l_n, m_n, e_n), jnp.float32),
        compiler_params=params(),
        cost_estimate=pl.CostEstimate(
            flops=2 * 2 * 3 * c_n * l_n * p_n * p_n * e_n,
            bytes_accessed=c_n * l_n * p_n * e_n * 16,
            transcendentals=0,
        ),
        name="forcing_modes",
    )(synth, analysis, ur, vr, part, mass)


def forcing_and_rims(synth, analysis, ur, u, vr, part, mass, connect, edge_ids, c, u_at):
    s_n, _, l_n, m_n, e_n = ur.shape
    p_n = vr.shape[1]
    k_n = edge_ids.shape[0]

    def kernel(synth_ref, analysis_ref, ur_ref, u_ref, vr_ref, part_ref, mass_ref, conn_ref, id_ref, o_ref, rim_ref):
        l = pl.program_id(0)
        dr = product(synth_ref[...], right_form(ur_ref[:, 0, 0].reshape(s_n * m_n, e_n)))
        forcing = part_ref[0, 0] - vr_ref[0] * dr
        weight = mass_ref[pl.ds(l, 1), :]
        modes = product(analysis_ref[...], right_form(forcing)) * (STEP_SIZE * weight)
        o_ref[:, 0, 0] = modes.reshape(s_n, m_n, e_n)
        high, low = split(modes + weight * u_ref[:, 0, 0].reshape(s_n * m_n, e_n))
        here = jnp.where(id_ref[...] == conn_ref[pl.ds(l, 1), :], 1.0, 0.0).astype(jnp.bfloat16)
        sums = lax.dot_general(
            jnp.concatenate([here, here], axis=1),
            jnp.concatenate([high, low], axis=1),
            (((1,), (1,)), ((), ())),
            preferred_element_type=jnp.float32,
        )

        @pl.when(l == 0)
        def _():
            rim_ref[...] = sums

        @pl.when(l > 0)
        def _():
            rim_ref[...] += sums

    whole = pl.BlockSpec((p_n, 3 * p_n), lambda l: (0, 0))
    block = (s_n, 1, 1, m_n, e_n)
    nodes = pl.BlockSpec((l_n, e_n), lambda l: (0, 0))
    return pl.pallas_call(
        kernel,
        grid=(l_n,),
        in_specs=[
            whole,
            whole,
            pl.BlockSpec(block, lambda l: (0, 0, l, 0, 0)),
            pl.BlockSpec(block, lambda l: (0, u_at, l, 0, 0)),
            pl.BlockSpec((1, p_n, e_n), lambda l: (l, 0, 0)),
            pl.BlockSpec((1, 1, p_n, e_n), lambda l: (c, l, 0, 0)),
            nodes,
            nodes,
            pl.BlockSpec((k_n, 1), lambda l: (0, 0)),
        ],
        out_specs=[
            pl.BlockSpec(block, lambda l: (0, 0, l, 0, 0)),
            pl.BlockSpec((k_n, s_n * m_n), lambda l: (0, 0)),
        ],
        out_shape=[
            jax.ShapeDtypeStruct((s_n, 1, l_n, m_n, e_n), jnp.float32),
            jax.ShapeDtypeStruct((k_n, s_n * m_n), jnp.float32),
        ],
        compiler_params=params(),
        cost_estimate=pl.CostEstimate(
            flops=4 * 2 * 3 * l_n * p_n * p_n * e_n, bytes_accessed=l_n * p_n * e_n * 20, transcendentals=0
        ),
        name="forcing_and_rims",
    )(synth, analysis, ur, u, vr, part, mass, connect, edge_ids)


def own_sums(modes, u, mass, connect, rims, edge_ids, u_at):
    s_n, _, l_n, m_n, e_n = modes.shape
    k_n = edge_ids.shape[0]
    coefs = s_n * m_n

    def kernel(f_ref, u_ref, mass_ref, conn_ref, turned_ref, rim_ref, id_ref, o_ref, held):
        l = pl.program_id(0)

        @pl.when(l == 0)
        def _():
            def hold(k, _):
                weighted = f_ref[:, 0, k] + mass_ref[pl.ds(k, 1), :] * u_ref[:, 0, k]
                high, low = split(weighted.reshape(coefs, e_n))
                held[k] = jnp.concatenate([high, low], axis=1)
                return 0

            lax.fori_loop(0, l_n, hold, 0)

        mine = conn_ref[pl.ds(l, 1), :]

        def same(ids):
            there = jnp.where(ids == mine, 1.0, 0.0).astype(jnp.bfloat16)
            return jnp.concatenate([there, there], axis=0)

        high, low = split(rim_ref[...])
        total = product(jnp.concatenate([high, low], axis=1), same(id_ref[...]))
        for k in range(l_n):
            total = total + product(held[k], same(turned_ref[k]))
        o_ref[:, 0, 0] = total.reshape(s_n, m_n, e_n)

    def whole(*shape):
        return pl.BlockSpec(shape, lambda l: (0,) * len(shape))

    return pl.pallas_call(
        kernel,
        grid=(l_n,),
        in_specs=[
            whole(s_n, 1, l_n, m_n, e_n),
            pl.BlockSpec((s_n, 1, l_n, m_n, e_n), lambda l: (0, u_at, 0, 0, 0)),
            whole(l_n, e_n),
            whole(l_n, e_n),
            whole(l_n, e_n, 1),
            whole(coefs, k_n),
            whole(k_n, 1),
        ],
        out_specs=pl.BlockSpec((s_n, 1, 1, m_n, e_n), lambda l: (0, 0, l, 0, 0)),
        out_shape=jax.ShapeDtypeStruct(modes.shape, jnp.float32),
        scratch_shapes=[pltpu.VMEM((l_n, coefs, 2 * e_n), jnp.bfloat16)],
        compiler_params=params(),
        cost_estimate=pl.CostEstimate(
            flops=4 * l_n * l_n * coefs * e_n * e_n, bytes_accessed=12 * modes.size, transcendentals=0
        ),
        name="own_sums",
    )(modes, u, mass, connect, connect[:, :, None], rims, edge_ids)


def rows_of(ref, places):
    return [ref[pl.ds(r, 1), :] for r in places]


def put_rows(ref, places, rows):
    for r, row in zip(places, rows):
        ref[pl.ds(r, 1), :] = row


def some_pairs(codes, at, number):
    found = [codes[at + t] for t in range(number)]
    return [code >> PACK for code in found], [code & (1 << PACK) - 1 for code in found]


def sum_class(ref, codes, start, number, both):
    def batch(i, _):
        others, heads = some_pairs(codes, start + i * BATCH, BATCH)
        sums = [a + b for a, b in zip(rows_of(ref, heads), rows_of(ref, others))]
        put_rows(ref, heads, sums)
        if both:
            put_rows(ref, others, sums)
        return 0

    lax.fori_loop(0, pl.cdiv(number, BATCH), batch, 0)


def sum_rest(ref, codes, start, number):
    def one(i, _):
        others, heads = some_pairs(codes, start + i, 1)
        put_rows(ref, heads, [rows_of(ref, heads)[0] + rows_of(ref, others)[0]])
        return 0

    lax.fori_loop(0, number, one, 0)


def hand_back(ref, codes, start, end):
    def batch(i, _):
        others, heads = some_pairs(codes, start + i * BATCH, BATCH)
        put_rows(ref, others, rows_of(ref, heads))
        return 0

    lax.fori_loop(0, pl.cdiv(end - start, BATCH), batch, 0)


def finish(sums, pairs, shared, inverse, held, shape, c):
    s_n, _, l_n, m_n, e_n = sums.shape
    _, _, nodes_n, _ = shape
    rows_n = nodes_n * e_n
    codes, bounds = pairs
    batch = nodes_n // shared.shape[0]
    step = max(8, l_n)
    outs = nodes_n // step

    def kernel(codes, bnd, mark, f_ref, again_ref, inv_ref, _, o_ref, table, stage):
        b = pl.program_id(0)

        def place(node):
            return pl.ds(pl.multiple_of(node * e_n, e_n), e_n)

        @pl.when(b < s_n)
        def _():
            for at in range(0, l_n, batch):

                @pl.when(mark[(b * l_n + at) // batch] != 0)
                def _():
                    for t in range(at, at + batch):
                        table[place(b * l_n + t), :] = f_ref[0, 0, t].T

        @pl.when(b == s_n - 1)
        def _():
            table[pl.ds(rows_n, 8), :] = jnp.zeros((8, m_n), jnp.float32)
            for k in range(CLASSES):
                sum_class(table, codes, bnd[2 * k], bnd[2 * k + 1], k == 0)
            sum_rest(table, codes, bnd[2 * CLASSES], bnd[2 * CLASSES + 1])
            hand_back(table, codes, bnd[2], bnd[2 * CLASSES + 2] + bnd[2 * CLASSES + 3])

        @pl.when(b >= s_n)
        def _():
            first = (b - s_n) * step
            for at in range(0, step, batch):
                marked = mark[(first + at) // batch] != 0

                @pl.when(marked)
                def _():
                    for t in range(at, at + batch):
                        n = first + t
                        stage[t] = table[place(n), :].T * inv_ref[pl.ds(n, 1), :]

                @pl.when(jnp.logical_not(marked))
                def _():
                    for t in range(at, at + batch):
                        stage[t] = again_ref[t // l_n, 0, t % l_n] * inv_ref[pl.ds(first + t, 1), :]

            o_ref[0] = jnp.swapaxes(stage[...], 0, 1)

    smem = pl.BlockSpec(memory_space=pltpu.SMEM)
    return pl.pallas_call(
        kernel,
        grid=(s_n + outs,),
        in_specs=[smem] * 3
        + [
            pl.BlockSpec((1, 1, l_n, m_n, e_n), lambda b: (jnp.minimum(b, s_n - 1), 0, 0, 0, 0)),
            pl.BlockSpec((step // l_n, 1, l_n, m_n, e_n), lambda b: (jnp.maximum(b - s_n, 0), 0, 0, 0, 0)),
            pl.BlockSpec((nodes_n, e_n), lambda b: (0, 0)),
            pl.BlockSpec(memory_space=pl.ANY),
        ],
        out_specs=pl.BlockSpec((1, m_n, step, e_n), lambda b: (c, 0, jnp.maximum(b - s_n, 0), 0)),
        out_shape=jax.ShapeDtypeStruct(shape, jnp.float32),
        scratch_shapes=[pltpu.VMEM((rows_n + 8, m_n), jnp.float32), pltpu.VMEM((step, m_n, e_n), jnp.float32)],
        input_output_aliases={6: 0},
        compiler_params=params(),
        cost_estimate=pl.CostEstimate(
            flops=rows_n * LANES * 400, bytes_accessed=rows_n * m_n * 12, transcendentals=0
        ),
        name="finish",
    )(codes, bounds, shared, sums, sums, inverse, held)


def local_sums(modes, u, mass, pairs, edge_reps, first):
    s_n, c_n, l_n, m_n, e_n = modes.shape
    nodes_n = s_n * l_n
    rows_n = nodes_n * e_n
    step = min(8, l_n)
    per = l_n // step
    codes, bounds = pairs
    edges_n = edge_reps.shape[1]
    feats = c_n * m_n

    def kernel(codes, bnd, er, f_ref, u_ref, mass_ref, o_ref, low_ref, up_ref):
        b = pl.program_id(0)
        for t in range(step):
            node = b * step + t
            weight = mass_ref[pl.ds(node, 1), :]
            rows = [f_ref[0, c, t] + weight * u_ref[0, c, t] for c in range(c_n)]
            table = jnp.concatenate(rows, axis=0) if c_n > 1 else rows[0]
            o_ref[pl.ds(pl.multiple_of(node * e_n, e_n), e_n), :] = table.T

        @pl.when(b == pl.num_programs(0) - 1)
        def _():
            o_ref[pl.ds(rows_n, 8), :] = jnp.zeros((8, feats), jnp.float32)

            for k in range(CLASSES):
                sum_class(o_ref, codes, bnd[2 * k], bnd[2 * k + 1], False)
            sum_rest(o_ref, codes, bnd[2 * CLASSES], bnd[2 * CLASSES + 1])

            def edge(i, _):
                for side, to in enumerate((low_ref, up_ref)):
                    got = rows_of(o_ref, [er[side, i * BATCH + t] for t in range(BATCH)])
                    put_rows(to, [i * BATCH + t for t in range(BATCH)], got)
                return 0

            lax.fori_loop(0, edges_n // BATCH, edge, 0)

    smem = pl.BlockSpec(memory_space=pltpu.SMEM)
    where = lambda b: (b // per, 0, b % per, 0, 0)
    where_u = lambda b: (b // per, first // c_n, b % per, 0, 0)
    rim = pl.BlockSpec((edges_n, feats), lambda b: (0, 0))
    rim_shape = jax.ShapeDtypeStruct((edges_n, feats), jnp.float32)
    return pl.pallas_call(
        kernel,
        grid=(nodes_n // step,),
        in_specs=[smem] * 3
        + [
            pl.BlockSpec((1, c_n, step, m_n, e_n), where),
            pl.BlockSpec((1, c_n, step, m_n, e_n), where_u),
            pl.BlockSpec((nodes_n, e_n), lambda b: (0, 0)),
        ],
        out_specs=[pl.BlockSpec((rows_n + 8, feats), lambda b: (0, 0)), rim, rim],
        out_shape=[jax.ShapeDtypeStruct((rows_n + 8, feats), jnp.float32), rim_shape, rim_shape],
        compiler_params=params(),
        cost_estimate=pl.CostEstimate(
            flops=rows_n * LANES * 400, bytes_accessed=rows_n * LANES * 12, transcendentals=0
        ),
        name="local_sums",
    )(codes, bounds, edge_reps, modes, u, mass)


def spread(table, rims, pairs, edge_reps, inverse, held, shape, first, c_n):
    _, m_n, nodes_n, e_n = shape
    rows_n = nodes_n * e_n
    step = 8
    edges_n = edge_reps.shape[1]
    codes, bounds = pairs
    feats = c_n * m_n

    def kernel(codes, bnd, er, t_ref, low_ref, up_ref, inv_ref, *rest):
        o_ref, stage = rest[-2:]
        b = pl.program_id(0)

        @pl.when(b == 0)
        def _():
            def edge(i, _):
                for side, came in enumerate((low_ref, up_ref)):
                    spots = [er[side, i * BATCH + t] for t in range(BATCH)]
                    more = rows_of(came, [i * BATCH + t for t in range(BATCH)])
                    put_rows(t_ref, spots, [a + b for a, b in zip(rows_of(t_ref, spots), more)])
                return 0

            lax.fori_loop(0, edges_n // BATCH, edge, 0)
            hand_back(t_ref, codes, 0, bnd[2 * CLASSES] + bnd[2 * CLASSES + 1])

        for t in range(step):
            n = b * step + t
            rows = t_ref[pl.ds(pl.multiple_of(n * e_n, e_n), e_n), :].T
            scaled = rows * inv_ref[pl.ds(n, 1), :]
            for c in range(c_n):
                stage[c, t] = scaled[c * m_n : (c + 1) * m_n]
        for c in range(c_n):
            o_ref[c] = jnp.swapaxes(stage[c], 0, 1)

    smem = pl.BlockSpec(memory_space=pltpu.SMEM)
    rim = pl.BlockSpec((edges_n, feats), lambda b: (0, 0))
    in_specs = [smem] * 3 + [
        pl.BlockSpec((rows_n + 8, feats), lambda b: (0, 0)),
        rim,
        rim,
        pl.BlockSpec((nodes_n, e_n), lambda b: (0, 0)),
    ]
    args = [codes, bounds, edge_reps, table, *rims, inverse]
    aliases = {}
    if held is not None:
        in_specs.append(pl.BlockSpec(memory_space=pl.ANY))
        args.append(held)
        aliases = {len(args) - 1: 0}
    return pl.pallas_call(
        kernel,
        grid=(nodes_n // step,),
        in_specs=in_specs,
        out_specs=pl.BlockSpec((c_n, m_n, step, e_n), lambda b: (first // c_n, 0, b, 0)),
        out_shape=jax.ShapeDtypeStruct(shape, jnp.float32),
        scratch_shapes=[pltpu.VMEM((c_n, step, m_n, e_n), jnp.float32)],
        input_output_aliases=aliases,
        compiler_params=params(),
        cost_estimate=pl.CostEstimate(
            flops=rows_n * LANES * 400, bytes_accessed=rows_n * LANES * 12, transcendentals=0
        ),
        name="spread",
    )(*args)


def fill_up(values, multiple, filler):
    short = -values.shape[-1] % multiple
    pad = [(0, 0)] * (values.ndim - 1) + [(0, short)]
    return jnp.pad(values, pad, constant_values=filler)


def grouped(group, classes, member, rep, pairs_n):
    rows_n = group.shape[0]
    assert rows_n <= 1 << BITS and classes < 8
    ones = (1 << 2 * BITS) - 1
    nobody = rows_n * (1 << PACK) + rows_n
    spare = (jnp.arange(CLASSES * BATCH, dtype=jnp.int32) // BATCH) * (ones + 1) + ones
    keys = group.astype(jnp.int32) * (ones + 1) + member * (1 << BITS) + rep
    length = pairs_n + CLASSES * BATCH
    keys = lax.sort(jnp.concatenate([keys, spare]), is_stable=False)[:length] & ones
    codes = jnp.where(keys == ones, nobody, (keys >> BITS) * (1 << PACK) + (keys & (1 << BITS) - 1))
    spares = BATCH * jnp.minimum(jnp.arange(classes, dtype=jnp.int32), CLASSES)
    numbers = jnp.sum(group[None, :] == jnp.arange(classes, dtype=jnp.int32)[:, None], axis=1, dtype=jnp.int32)
    lower = jnp.tri(classes, k=-1, dtype=jnp.int32)
    starts = jnp.sum(lower * numbers[None, :], axis=1) + spares
    bounds = jnp.stack([starts, numbers], axis=1).reshape(-1).astype(jnp.int32)
    return jnp.pad(codes, (0, BATCH + -length % BATCH), constant_values=nobody), bounds


def pair_lists(ids, edges, parts, nodes_n):
    rows_n = ids.shape[0]
    place = jnp.arange(rows_n, dtype=jnp.int32)
    assert rows_n <= 1 << BITS and UNIQUE <= 1 << BITS
    keys = lax.sort(ids * (1 << BITS) + place, is_stable=False)
    ids_sorted, member = keys >> BITS, keys & (1 << BITS) - 1
    yes = jnp.ones((1,), bool)
    head = jnp.concatenate([yes, ids_sorted[1:] != ids_sorted[:-1]])
    last = jnp.concatenate([head[1:], yes])
    code = lax.cummax(jnp.where(head, place * rows_n + member, 0))
    rep = code % rows_n
    rank = place - code // rows_n
    pairs_n = rows_n - UNIQUE
    group = jnp.where((rank == 1) & last, 0, jnp.minimum(rank, CLASSES))
    group = jnp.where(rank == 0, CLASSES + 1, group)
    pairs = grouped(group, CLASSES + 1, member, rep, pairs_n)

    device = member // (rows_n // parts)
    device_first = head | jnp.concatenate([yes, device[1:] != device[:-1]])
    device_no = lax.cumsum(device_first.astype(jnp.int32))
    device_rank = device_no - lax.cummax(jnp.where(head, device_no, 0))
    most = lax.cummax(jnp.where(last, (rows_n - place) * parts + device_rank, 0), reverse=True) % parts
    group = jnp.where(device_first, jnp.minimum(device_rank, CLASSES), CLASSES + 1)
    group = jnp.where((rank == 1) & last & (device_rank == 1), 0, group)
    group = jnp.where((rank == 0) | (most == 0), CLASSES + 2, group)
    across = grouped(group, CLASSES + 2, member, rep, pairs_n)
    points = rows_n // nodes_n * min(8, nodes_n // parts)
    point_group = jnp.arange(rows_n // points, dtype=jnp.int32)
    shared = jnp.any((member // points == point_group[:, None]) & (most > 0), axis=1).astype(jnp.int32)

    flat = edges.reshape(-1)
    start = jnp.sum(ids_sorted[None, :] < flat[:, None], axis=1, dtype=jnp.int32)
    edge_reps = fill_up(member[start].reshape(edges.shape), BATCH, rows_n)
    return pairs, across, shared, edge_reps


def shifted(x, axis, step):
    count = lax.axis_size(axis)
    return lax.ppermute(x, axis, [(i, (i + step) % count) for i in range(count)])


def largest_of_partitions(x):
    step = 1
    while step < lax.axis_size("mesh"):
        x = jnp.maximum(x, shifted(x, "mesh", step))
        step *= 2
    return x


def total_over_four(x):
    total = x
    for step in range(1, lax.axis_size("four")):
        total = total + shifted(x, "four", step)
    return total


def swap_edges(low, up):
    return shifted(up, "mesh", 1), shifted(low, "mesh", -1)


def edge_takers(edges, connect, edge_reps, parts):
    here_n = connect.size // parts
    ids = fill_up(edges, BATCH, -1)
    has = jnp.any(ids[:, None, :, None] == connect.reshape(1, parts, 1, here_n), axis=3).astype(jnp.float32)
    theirs = jnp.stack(swap_edges(has[0], has[1]))
    spread_out = largest_of_partitions(jnp.max(theirs * (1.0 - has)).reshape(1))[0] > 0.5
    at_rep = jnp.where(edge_reps // here_n == lax.axis_index("four"), ids, -1)
    taken = jnp.where(spread_out, at_rep, ids)
    return ids.reshape(-1, 1), taken.reshape(-1, 1), spread_out


def inverse_mass(mass, ids, edges):
    summed = jnp.zeros((UNIQUE,), jnp.float32).at[ids].add(mass.reshape(-1))
    came = jnp.concatenate(swap_edges(summed[edges[0]], summed[edges[1]]))
    summed = summed.at[edges.reshape(-1)].add(came)
    return (1.0 / summed[ids]).reshape(mass.shape)


def exchange(x):
    return lax.all_to_all(x, "four", split_axis=0, concat_axis=0, tiled=True)


def body(adj_modes, base_flow, geometry, mass, connect, edge_nodes):
    comps, m_n, nodes_n, e_n = adj_modes.shape
    parts = lax.axis_size("four")
    l_n = nodes_n // parts
    mine = lax.axis_index("four") * l_n
    synth, along, analysis = plane_tables(PLANES)
    both_3 = left_form(np.concatenate([synth, along]))
    synth_3, analysis_3 = left_form(synth), left_form(analysis)
    together = lax.optimization_barrier
    spot = lambda n: (n // l_n, n % l_n)
    along_r = [[spot(NP * i + j) for i in range(NP)] for j in range(NP)]
    along_s = [[spot(NP * i + j) for j in range(NP)] for i in range(NP)]
    inside = [[(a, l + j) for j in range(NP)] for a in range(parts) for l in range(0, l_n, NP)]
    whole_rows = l_n % NP == 0

    u_first = adj_modes[0].reshape(m_n, parts, l_n, e_n).transpose(1, 0, 2, 3)
    u_first, adj_modes = together((u_first, adj_modes))
    first_here = exchange(u_first)

    u = node_major(adj_modes, parts)
    ur_a, ur_b = derivative(u, along_r, 0, 2), derivative(u, along_r, 2, 1)
    sent = [u[:, 1:], ur_a] + ([] if whole_rows else [derivative(u, along_s)])
    sent = jnp.concatenate(sent, axis=1)
    sent, u, ur_b, first_here, connect, edge_nodes, mass, base_flow = together(
        (sent, u, ur_b, first_here, connect, edge_nodes, mass, base_flow)
    )

    here = exchange(sent)
    edges = edge_nodes[0]
    ids = connect.reshape(-1)
    pairs, across, shared, edge_reps = pair_lists(ids, edges, parts, nodes_n)
    inverse = inverse_mass(mass, ids, edges)
    base = base_flow.transpose(0, 2, 1, 3)
    if l_n % 8 == 0:
        u0_here = node_major(first_here, 1).reshape(parts, 1, l_n, m_n, e_n)
    else:
        u0_here = first_here.transpose(0, 2, 1, 3)[:, None]
    us0_here = derivative(u0_here, inside, 0, 1) if whole_rows else None
    mass_here = lax.dynamic_slice_in_dim(mass, mine, l_n, 0)
    connect_here = lax.dynamic_slice_in_dim(connect, mine, l_n, 0)
    edge_ids, taken_ids, spread_out = edge_takers(edges, connect, edge_reps, parts)
    held = (here, ur_b, pairs, across, shared, edge_reps, inverse, base, u0_here, us0_here, edge_ids, taken_ids, spread_out)
    here, ur_b, pairs, across, shared, edge_reps, inverse, base, u0_here, us0_here, edge_ids, taken_ids, spread_out = together(held)

    ur_b_here = exchange(ur_b)
    us_here = derivative(here, inside, 0, 2) if whole_rows else here[:, 5:7]
    if not whole_rows:
        us0_here = here[:, 4:5]
    geo = lax.dynamic_slice_in_dim(geometry, mine, l_n, 1)
    vr, part = base_products(both_3, synth_3, u0_here, here, us0_here, us_here, base, geo)
    f_a = forcing_modes(synth_3, analysis_3, here, vr, part, mass_here, 2, 0, 2)
    f_a, ur_b_here = together((f_a, ur_b_here))

    modes_a = exchange(f_a)
    f_b, rims = forcing_and_rims(
        synth_3, analysis_3, ur_b_here, here, vr, part, mass_here, connect_here, edge_ids, 2, 1
    )
    half = rims.shape[0] // 2
    rims = jnp.concatenate(swap_edges(rims[:half], rims[half:]))
    rims = lax.cond(spread_out, total_over_four, lambda r: r, rims)
    f_b = own_sums(f_b, here, mass_here, connect_here, rims.T, taken_ids, 1)
    f_b, modes_a = together((f_b, modes_a))

    modes_b = exchange(f_b)
    table, *rims = local_sums(modes_a, u, mass, pairs, edge_reps, 0)
    out = spread(table, swap_edges(*rims), pairs, edge_reps, inverse, None, adj_modes.shape, 0, 2)
    modes_b, out = together((modes_b, out))

    return finish(modes_b, across, shared, inverse, out, adj_modes.shape, 2)


def solution(mesh):
    return jax.shard_map(
        body,
        mesh=mesh,
        in_specs=(
            P(None, "four", None, "mesh"),
            P(None, None, "four", "mesh"),
            P(None, None, "mesh"),
            P(None, "mesh"),
            P(None, "mesh"),
            P("mesh", None, None),
        ),
        out_specs=P(None, "four", None, "mesh"),
        check_vma=False,
    )
```
